32 devices in a mesh: dp: 16 (over z, y, core), seq: 2 (over x).
Axes of the slice: x: 2, y: 2, z: 4, core: 2. Of those that a mesh axis runs over, the one named last changes fastest.
Arguments:
- x_in: bfloat16 [2, 16, 1024, 768], P(None, 'dp', 'seq'), may hold values from -6 to 6
- grad_out: bfloat16 [2, 16, 1024, 768], P(None, 'dp', 'seq'), may hold values from -6 to 6
- norm_gain: bfloat16 [768], P(('dp', 'seq')), may hold values from 0.099609375 to 1.8984375
- in_weight: bfloat16 [768, 3352], P(('dp', 'seq')), may hold values from -0.21875 to 0.21875
- conv_weight: bfloat16 [4, 1792], P(None, ('dp', 'seq')), may hold values from -3 to 3
- conv_bias: bfloat16 [1792], P(('dp', 'seq')), may hold values from -3 to 3
- gate_gain: bfloat16 [1536], P(('dp', 'seq')), may hold values from 0.099609375 to 1.8984375
- out_weight: bfloat16 [1536, 768], P(('dp', 'seq')), may hold values from -0.15625 to 0.15625
- dt_bias: float32 [24], replicated, may hold values from -4.5 to -2
- a_log: float32 [24], replicated, may hold values from -7.5 to 0
- skip: float32 [24], replicated, may hold values from 0.5 to 2
Outputs:
- y_out: bfloat16 [2, 16, 1024, 768], P(None, 'dp', 'seq')
- dx_in: bfloat16 [2, 16, 1024, 768], P(None, 'dp', 'seq')
- grad_norm_gain: float32 [768], P(('dp', 'seq'))
- grad_in_weight: float32 [768, 3352], P(('dp', 'seq'))
- grad_conv_weight: float32 [4, 1792], P(None, ('dp', 'seq'))
- grad_conv_bias: float32 [1792], P(('dp', 'seq'))
- grad_gate_gain: float32 [1536], P(('dp', 'seq'))
- grad_out_weight: float32 [1536, 768], P(('dp', 'seq'))
- grad_dt_bias: float32 [24], replicated
- grad_a_log: float32 [24], replicated
- grad_skip: float32 [24], replicated
The draws below stay inside these ranges and needn't reach their ends.
All inputs are finite; a program needn't handle non-finite values.
Results may differ from the reference program's by a relative error of at most 0.012.
The reference program's roundings to bfloat16 on the way count: a program that leaves them out, or rounds other values in their place, can miss the bound.
Values may be sent and summed in bfloat16 or wider, within the bound.
No kernel may reach another device: no remote copies, remote signals or barrier semaphores. Data moves between devices by JAX's collectives and lax.ppermute only.
A program may use at most 192 MiB of HBM per device.

```python
import jax
import jax.numpy as jnp
from jax import lax

D = 768
HEADS = 24
HEADDIM = 64
STATE = 128
KCONV = 4
GROUP = 256
MICRO = 2
INNER = 1536
CONVW = 1792
PROJ = 3352
SEQ_LEN = 1024
BATCH = 16


def draw_a_log(key, part):
    key = jax.random.fold_in(key, 11)
    return jax.random.uniform(key, (HEADS,), jnp.float32, -6.0, 0.0)


def level_of(key, dims, shards, smallest, top_value):
    gain = 1.0
    for dim, parts in shards:
        heights = jax.random.uniform(jax.random.fold_in(jax.random.fold_in(key, 6), dim), (parts,), jnp.float32, smallest / len(shards), top_value / len(shards))
        gain = gain * jnp.repeat(jnp.exp(heights), dims[dim] // parts).reshape((-1,) + (1,) * (len(dims) - 1 - dim))
    return gain


def bell_draw(key, shape, scale, limit, split=(), dtype=jnp.bfloat16):
    entries = jax.random.normal(key, shape, jnp.float32) * scale
    if len(split) > 0:
        entries = level_of(key, shape, split, -0.22, 0.18) * entries
    return jnp.clip(entries, min=-limit, max=limit).astype(dtype)


def setup_inputs(seed: int = 0) -> dict:
    key_list = jax.random.split(jax.random.key(seed), 12)
    x_in = bell_draw(key_list[0], (MICRO, BATCH, SEQ_LEN, D), 1.0, 6.0, ((1, 16), (2, 2)))
    grad_out = bell_draw(key_list[1], (MICRO, BATCH, SEQ_LEN, D), 1.0, 6.0, ((1, 16), (2, 2)))
    norm_gain = jnp.clip(1.0 + 0.18 * jax.random.normal(key_list[2], (D,), jnp.float32), 0.099609375, 1.8984375).astype(jnp.bfloat16)
    in_weight = bell_draw(key_list[3], (D, PROJ), D ** -0.5, 0.21875, ((0, 32),))
    conv_weight = bell_draw(key_list[4], (KCONV, CONVW), KCONV ** -0.5, 3.0, ((1, 32),))
    conv_bias = bell_draw(key_list[5], (CONVW,), 0.5, 3.0, ((0, 32),))
    gate_gain = jnp.clip(1.0 + 0.18 * jax.random.normal(key_list[6], (INNER,), jnp.float32), 0.099609375, 1.8984375).astype(jnp.bfloat16)
    out_weight = bell_draw(key_list[7], (INNER, D), INNER ** -0.5, 0.15625, ((0, 32),))
    dt_bias = jnp.clip(jax.random.uniform(key_list[8], (HEADS,), jnp.float32, -4.5, -2.0), -4.5, -2.0)
    a_log = draw_a_log(jax.random.fold_in(key_list[11], 71), 0)
    skip = jnp.clip(jax.random.uniform(key_list[10], (HEADS,), jnp.float32, 0.5, 2.0), 0.5, 2.0)
    return dict(x_in=x_in, grad_out=grad_out, norm_gain=norm_gain, in_weight=in_weight, conv_weight=conv_weight, conv_bias=conv_bias, gate_gain=gate_gain, out_weight=out_weight, dt_bias=dt_bias, a_log=a_log, skip=skip)


EPS = 1e-05
HIGH = lax.Precision.HIGHEST

@jax.custom_vjp
def low(v):
    return lax.optimization_barrier(v.astype(jnp.bfloat16)).astype(jnp.float32)

@jax.custom_vjp
def low_back(v):
    return v

def low_keep(v):
    return (low(v), None)

def low_pass(kept, grad):
    return (grad,)

def back_keep(v):
    return (v, None)

def back_low(kept, grad):
    return (low(grad),)
low.defvjp(low_keep, low_pass)
low_back.defvjp(back_keep, back_low)

def group_step(rate, state_in, item):
    xq, bq, cq, step = item
    cum = jnp.cumsum(step * rate[None, :], 0)
    cbq = low_back(jnp.dot(cq, bq.T, precision=HIGH))
    rows = lax.broadcasted_iota(jnp.int32, (GROUP, GROUP), 0)
    cols = lax.broadcasted_iota(jnp.int32, (GROUP, GROUP), 1)
    lower = rows >= cols
    cum_t = cum.T
    diff = cum_t[:, :, None] - cum_t[:, None, :]
    decay = jnp.exp(jnp.where(lower[None], diff, 0.0)) * lower[None].astype(jnp.float32)
    weights = low(cbq[None] * decay * step.T[:, None, :])
    inside = jnp.einsum('hts,shp->thp', weights, xq, precision=HIGH)
    state_low = low(state_in)
    carried = jnp.exp(cum)[:, :, None] * low_back(jnp.einsum('tn,hpn->thp', cq, state_low, precision=HIGH))
    last = cum[-1]
    scale = jnp.exp(last[None, :] - cum) * step
    x_scaled = low(xq * scale[:, :, None])
    local = low_back(jnp.einsum('shp,sn->hpn', x_scaled, bq, precision=HIGH))
    state_out = jnp.exp(last)[:, None, None] * state_in + local
    return (state_out, inside + carried)

def block(params, xf):
    gain_in, w_in, w_conv, b_conv, gain_gate, w_out, dtb, alog, skip = params
    length = xf.shape[0]
    r_in = lax.rsqrt(lax.optimization_barrier(jnp.mean(xf * xf, -1, keepdims=True)) + EPS)
    normed = low(xf * r_in * gain_in)
    proj = low_back(low(jnp.dot(normed, w_in, precision=HIGH)))
    zpart = proj[:, :INNER]
    conv_in = proj[:, INNER:INNER + CONVW]
    dt_raw = proj[:, INNER + CONVW:]
    padded = jnp.concatenate([jnp.zeros((KCONV - 1, CONVW), jnp.float32), conv_in], 0)
    conv_out = b_conv + jnp.zeros((length, CONVW), jnp.float32)
    for tap in range(KCONV):
        conv_out = conv_out + w_conv[tap] * padded[tap:tap + length]
    mixed = low_back(low(jax.nn.silu(conv_out)))
    count = length // GROUP
    xh = mixed[:, :INNER].reshape(count, GROUP, HEADS, HEADDIM)
    bm = mixed[:, INNER:INNER + STATE].reshape(count, GROUP, STATE)
    cm = mixed[:, INNER + STATE:].reshape(count, GROUP, STATE)
    step = jax.nn.softplus(dt_raw + dtb).reshape(count, GROUP, HEADS)
    rate = -jnp.exp(alog)
    start = jnp.zeros((HEADS, HEADDIM, STATE), jnp.float32)
    stepper = jax.checkpoint(lambda carry, item: group_step(rate, carry, item))
    _, outs = lax.scan(stepper, start, (xh, bm, cm, step))
    ssd = outs + skip[None, None, :, None] * xh
    ssd = low_back(ssd.reshape(length, INNER))
    gated = ssd * jax.nn.silu(zpart)
    r_gate = lax.rsqrt(lax.optimization_barrier(jnp.mean(gated * gated, -1, keepdims=True)) + EPS)
    gnorm = low(gated * r_gate * gain_gate)
    return xf + jnp.dot(gnorm, w_out, precision=HIGH)

def reference(x_in, grad_out, norm_gain, in_weight, conv_weight, conv_bias, gate_gain, out_weight, dt_bias, a_log, skip):
    params = tuple((p.astype(jnp.float32) for p in (norm_gain, in_weight, conv_weight, conv_bias, gate_gain, out_weight, dt_bias, a_log, skip)))
    inputs = x_in.reshape(MICRO * BATCH, SEQ_LEN, D).astype(jnp.float32)
    cotans = grad_out.reshape(MICRO * BATCH, SEQ_LEN, D).astype(jnp.float32)

    def one(total, item):
        xf, cot = item
        result, pull = jax.vjp(block, params, xf)
        grad_params, grad_x = pull(cot)
        total = jax.tree.map(lambda a, b: a + b, total, grad_params)
        return (total, (result.astype(jnp.bfloat16), grad_x.astype(jnp.bfloat16)))
    zeros = jax.tree.map(jnp.zeros_like, params)
    total, (outputs, grads) = lax.scan(one, zeros, (inputs, cotans))
    return (outputs.reshape(x_in.shape), grads.reshape(x_in.shape), total[0], total[1], total[2], total[3], total[4], total[5], total[6], total[7], total[8])
```

```python
import jax
import jax.numpy as jnp
from jax import lax
from jax.experimental import pallas as pl
from jax.experimental.pallas import tpu as pltpu
from jax.sharding import PartitionSpec as P

HEADS = 24
HEADDIM = 64
STATE = 128
KCONV = 4
GROUP = 256
INNER = 1536
CONVW = 1792


EPS = 1e-05


def shifted(array, axis, by):
    devices = lax.axis_size(axis)
    pairs = [(i, i + by) for i in range(devices) if 0 <= i + by < devices]
    return lax.ppermute(array, axis, pairs)


def prefix(array, axis, join, neutral, backward):
    count = lax.axis_size(axis)
    place = lax.axis_index(axis)
    ahead = count - 1 - place if backward else place
    gathered = jax.tree.map(
        lambda a, kind: lax.all_gather(a.astype(kind), axis), array, (jnp.bfloat16, jnp.bfloat16)
    )
    state = jax.tree.map(lambda a, e: jnp.zeros_like(a) + jnp.asarray(e, a.dtype), array, neutral)

    def one(hop, state):
        source = count - 1 - hop if backward else hop
        return join(
            state,
            jax.tree.map(
                lambda a, own: lax.dynamic_index_in_dim(a, source, 0, False).astype(own.dtype),
                gathered,
                array,
            ),
        )

    return lax.fori_loop(0, ahead, one, state)


def tdot(left, right):
    return lax.dot_general(
        left, right, (((0,), (0,)), ((), ())), preferred_element_type=jnp.float32
    )


def ndot(left, right):
    return lax.dot_general(
        left, right, (((1,), (1,)), ((), ())), preferred_element_type=jnp.float32
    )


def dsilu(value):
    sig = jax.nn.sigmoid(value)
    return sig * (1.0 + value * (1.0 - sig))


def merge_states(earlier, later):
    return (earlier[0] * later[0], earlier[1] * later[0][:, None, None] + later[1])


def decay_table(cum_t):
    size = cum_t.shape[-1]
    rows = lax.broadcasted_iota(jnp.int32, (size, size), 0)
    cols = lax.broadcasted_iota(jnp.int32, (size, size), 1)
    lower = rows >= cols
    diff = cum_t[:, :, :, None] - cum_t[:, :, None, :]
    return jnp.exp(jnp.where(lower, diff, 0.0)) * lower.astype(jnp.float32)


def forward(xb, wts, dt_bias, rate, skip):
    gain_in, w_in, w_conv, b_conv, gain_gate, w_out = wts
    length = xb.shape[0]
    count = length // GROUP
    xf = xb.astype(jnp.float32)
    r_in = lax.rsqrt(jnp.mean(xf * xf, -1, keepdims=True) + EPS)
    normed = (xf * r_in * gain_in.astype(jnp.float32)).astype(jnp.bfloat16)
    proj = jnp.dot(normed, w_in, preferred_element_type=jnp.float32).astype(jnp.bfloat16)
    conv_in = proj[:, INNER : INNER + CONVW]
    rim = shifted(conv_in[length - KCONV + 1 :], "seq", 1)
    padded = jnp.concatenate([rim, conv_in], 0).astype(jnp.float32)
    taps = w_conv.astype(jnp.float32)
    conv_out = b_conv.astype(jnp.float32) + jnp.zeros((length, CONVW), jnp.float32)
    for tap in range(KCONV):
        conv_out = conv_out + taps[tap] * padded[tap : tap + length]
    mixed = jax.nn.silu(conv_out).astype(jnp.bfloat16)
    xh = mixed[:, :INNER].reshape(count, GROUP, HEADS, HEADDIM)
    bm = mixed[:, INNER : INNER + STATE].reshape(count, GROUP, STATE)
    cm = mixed[:, INNER + STATE :].reshape(count, GROUP, STATE)
    dt_raw = proj[:, INNER + CONVW :].astype(jnp.float32)
    step = jax.nn.softplus(dt_raw + dt_bias)
    step_t = step.reshape(count, GROUP, HEADS).transpose(0, 2, 1)
    cum_t = jnp.cumsum(step_t * rate[None, :, None], -1)
    decay = decay_table(cum_t)
    cbm = jnp.einsum("ctn,csn->cts", cm, bm, preferred_element_type=jnp.float32)
    weights = (cbm[:, None] * decay * step_t[:, :, None, :]).astype(jnp.bfloat16)
    inside = jnp.einsum("chts,cshp->cthp", weights, xh, preferred_element_type=jnp.float32)
    last = cum_t[:, :, -1]
    block_decay = jnp.exp(last)
    scale = (jnp.exp(last[:, :, None] - cum_t) * step_t).transpose(0, 2, 1)
    x_scaled = (xh.astype(jnp.float32) * scale[..., None]).astype(jnp.bfloat16)
    local = jnp.einsum("cshp,csn->chpn", x_scaled, bm, preferred_element_type=jnp.float32)
    total_decay = jnp.ones((HEADS,), jnp.float32)
    total_state = jnp.zeros((HEADS, HEADDIM, STATE), jnp.float32)
    for block in range(count):
        total_state = total_state * block_decay[block][:, None, None] + local[block]
        total_decay = total_decay * block_decay[block]
    identity = (jnp.ones((HEADS,), jnp.float32), jnp.zeros((HEADS, HEADDIM, STATE), jnp.float32))
    _, incoming = prefix((total_decay, total_state), "seq", merge_states, identity, False)
    entering = []
    running = incoming
    for block in range(count):
        entering.append(running)
        running = running * block_decay[block][:, None, None] + local[block]
    state_in = jnp.stack(entering)
    state_low = state_in.astype(jnp.bfloat16)
    exp_cum = jnp.exp(cum_t).transpose(0, 2, 1)
    carried = exp_cum[..., None] * jnp.einsum(
        "ctn,chpn->cthp", cm, state_low, preferred_element_type=jnp.float32
    )
    ssd = (inside + carried + skip[None, None, :, None] * xh.astype(jnp.float32)).reshape(
        length, INNER
    )
    zsig = jax.nn.silu(proj[:, :INNER].astype(jnp.float32))
    gated = ssd * zsig
    r_gate = lax.rsqrt(jnp.mean(gated * gated, -1, keepdims=True) + EPS)
    gnorm = (gated * r_gate * gain_gate.astype(jnp.float32)).astype(jnp.bfloat16)
    result = (xf + jnp.dot(gnorm, w_out, preferred_element_type=jnp.float32)).astype(jnp.bfloat16)
    saved = (
        xf,
        r_in,
        normed,
        proj,
        padded,
        conv_out,
        mixed,
        step_t,
        cum_t,
        state_in,
        state_low,
        carried,
        ssd,
        zsig,
        gated,
        r_gate,
        gnorm,
    )
    return (result, saved)


def backward(saved, cot, wts, dt_bias, rate, skip):
    gain_in, w_in, w_conv, b_conv, gain_gate, w_out = wts
    (
        xf,
        r_in,
        normed,
        proj,
        padded,
        conv_out,
        mixed,
        step_t,
        cum_t,
        state_in,
        state_low,
        carried,
        ssd,
        zsig,
        gated,
        r_gate,
        gnorm,
    ) = saved
    length = xf.shape[0]
    count = length // GROUP
    grad_wout = tdot(gnorm, cot)
    dgnorm = ndot(cot, w_out)
    scaled_g = gain_gate.astype(jnp.float32) * dgnorm
    grad_ggain = jnp.sum(dgnorm * gated * r_gate, 0)
    dgated = r_gate * scaled_g - gated * r_gate**3 * jnp.mean(scaled_g * gated, -1, keepdims=True)
    dssd = (dgated * zsig).astype(jnp.bfloat16)
    zpart = proj[:, :INNER].astype(jnp.float32)
    dzpart = dgated * ssd * dsilu(zpart)
    xh = mixed[:, :INNER].reshape(count, GROUP, HEADS, HEADDIM)
    bm = mixed[:, INNER : INNER + STATE].reshape(count, GROUP, STATE)
    cm = mixed[:, INNER + STATE :].reshape(count, GROUP, STATE)
    xhf = xh.astype(jnp.float32)
    dyr = dssd.reshape(count, GROUP, HEADS, HEADDIM)
    dyf = dyr.astype(jnp.float32)
    decay = decay_table(cum_t)
    cbm = jnp.einsum("ctn,csn->cts", cm, bm, preferred_element_type=jnp.float32)
    full = cbm[:, None] * decay * step_t[:, :, None, :]
    weights = full.astype(jnp.bfloat16)
    grad_skip = jnp.sum(dyf * xhf, (0, 1, 3))
    dxh = skip[None, None, :, None] * dyf
    dweights = jnp.einsum("cthp,cshp->chts", dyr, xh, preferred_element_type=jnp.float32)
    dxh = dxh + jnp.einsum("chts,cthp->cshp", weights, dyr, preferred_element_type=jnp.float32)
    dcbm = jnp.sum(dweights * decay * step_t[:, :, None, :], 1).astype(jnp.bfloat16)
    dstep = jnp.sum(dweights * cbm[:, None] * decay, 2)
    product = dweights * full
    dcum = jnp.sum(product, 3) - jnp.sum(product, 2)
    dcum = dcum + jnp.sum(dyf * carried, -1).transpose(0, 2, 1)
    exp_cum = jnp.exp(cum_t).transpose(0, 2, 1)
    dcarry = (dyf * exp_cum[..., None]).astype(jnp.bfloat16)
    dcm = jnp.einsum("cthp,chpn->ctn", dcarry, state_low, preferred_element_type=jnp.float32)
    dstate_low = jnp.einsum("cthp,ctn->chpn", dcarry, cm, preferred_element_type=jnp.float32)
    last = cum_t[:, :, -1]
    block_decay = jnp.exp(last)
    total_decay = jnp.ones((HEADS,), jnp.float32)
    running = jnp.zeros((HEADS, HEADDIM, STATE), jnp.float32)
    for block in reversed(range(count)):
        running = running * block_decay[block][:, None, None] + dstate_low[block]
        total_decay = total_decay * block_decay[block]
    identity = (jnp.ones((HEADS,), jnp.float32), jnp.zeros((HEADS, HEADDIM, STATE), jnp.float32))
    _, later = prefix((total_decay, running), "seq", merge_states, identity, True)
    leaving = [later] * count
    running = later
    for block in reversed(range(count)):
        leaving[block] = running
        running = running * block_decay[block][:, None, None] + dstate_low[block]
    grad_state = jnp.stack(leaving)
    dlast = block_decay * jnp.sum(grad_state * state_in, (2, 3))
    scale_t = jnp.exp(last[:, :, None] - cum_t) * step_t
    scale = scale_t.transpose(0, 2, 1)
    x_scaled = (xhf * scale[..., None]).astype(jnp.bfloat16)
    grad_low = grad_state.astype(jnp.bfloat16)
    dxs = jnp.einsum("csn,chpn->cshp", bm, grad_low, preferred_element_type=jnp.float32)
    dbm = jnp.einsum("cshp,chpn->csn", x_scaled, grad_low, preferred_element_type=jnp.float32)
    dxh = dxh + dxs * scale[..., None]
    dscale = jnp.sum(dxs * xhf, -1).transpose(0, 2, 1)
    dstep = dstep + dscale * jnp.exp(last[:, :, None] - cum_t)
    dlast = dlast + jnp.sum(dscale * scale_t, -1)
    dcum = dcum - dscale * scale_t
    final = (lax.broadcasted_iota(jnp.int32, (GROUP,), 0) == GROUP - 1).astype(jnp.float32)
    dcum = dcum + dlast[:, :, None] * final
    dlog = jnp.flip(jnp.cumsum(jnp.flip(dcum, -1), -1), -1)
    dstep = dstep + dlog * rate[None, :, None]
    grad_alog = jnp.sum(dlog * step_t, (0, 2)) * rate
    dcm = dcm + jnp.einsum("cts,csn->ctn", dcbm, bm, preferred_element_type=jnp.float32)
    dbm = dbm + jnp.einsum("cts,ctn->csn", dcbm, cm, preferred_element_type=jnp.float32)
    dmixed = jnp.concatenate(
        [dxh.reshape(length, INNER), dbm.reshape(length, STATE), dcm.reshape(length, STATE)], -1
    )
    dmixed = dmixed.astype(jnp.bfloat16).astype(jnp.float32)
    dconv = dmixed * dsilu(conv_out)
    grad_cbias = jnp.sum(dconv, 0)
    grad_cweight = jnp.stack(
        [jnp.sum(dconv * padded[tap : tap + length], 0) for tap in range(KCONV)]
    )
    rim_back = shifted(dconv[: KCONV - 1], "seq", -1)
    extended = jnp.concatenate([dconv, rim_back], 0)
    taps = w_conv.astype(jnp.float32)
    dconv_in = jnp.zeros((length, CONVW), jnp.float32)
    for tap in range(KCONV):
        dconv_in = dconv_in + taps[tap] * extended[KCONV - 1 - tap : KCONV - 1 - tap + length]
    dt_raw = proj[:, INNER + CONVW :].astype(jnp.float32)
    ddt_raw = dstep.transpose(0, 2, 1).reshape(length, HEADS) * jax.nn.sigmoid(dt_raw + dt_bias)
    grad_dtb = jnp.sum(ddt_raw, 0)
    dproj = jnp.concatenate([dzpart, dconv_in, ddt_raw], -1).astype(jnp.bfloat16)
    grad_win = tdot(normed, dproj)
    dnormed = ndot(dproj, w_in)
    scaled_in = gain_in.astype(jnp.float32) * dnormed
    grad_gin = jnp.sum(dnormed * xf * r_in, 0)
    dx_in = (
        r_in * scaled_in
        - xf * r_in**3 * jnp.mean(scaled_in * xf, -1, keepdims=True)
        + cot.astype(jnp.float32)
    )
    head_terms = jnp.stack([grad_dtb, grad_alog, grad_skip]).reshape(1, 3 * HEADS)
    return (
        dx_in.astype(jnp.bfloat16),
        (grad_gin, grad_win, grad_cweight, grad_cbias, grad_ggain, grad_wout, head_terms),
    )


PAIR = 2 * HEADDIM
WIDE = 768
TAIL = 384
LOW = -1e30


def silu_parts(value):
    sig = 0.5 * jnp.tanh(0.5 * value) + 0.5
    return (sig, value * sig)


def split_dot(value, right):
    top = value.astype(jnp.bfloat16)
    rest = (value - top.astype(jnp.float32)).astype(jnp.bfloat16)
    return jnp.dot(top, right, preferred_element_type=jnp.float32) + jnp.dot(
        rest, right, preferred_element_type=jnp.float32
    )


def exact_dot(left, value):
    total = None
    for _ in range(3):
        part = value.astype(jnp.bfloat16)
        value = value - part.astype(jnp.float32)
        term = jnp.dot(left, part, preferred_element_type=jnp.float32)
        total = term if total is None else total + term
    return total


def lower_ones(size, flipped):
    rows = lax.broadcasted_iota(jnp.int32, (size, size), 0)
    cols = lax.broadcasted_iota(jnp.int32, (size, size), 1)
    return rows <= cols if flipped else rows >= cols


def step_sizes(raw, heads_ref):
    shifted_raw = raw.astype(jnp.float32) + heads_ref[0:1, :]
    dt = jnp.maximum(shifted_raw, 0.0) + jnp.log1p(jnp.exp(-jnp.abs(shifted_raw)))
    ones = lower_ones(GROUP, False).astype(jnp.float32).astype(jnp.bfloat16)
    cum = exact_dot(ones, dt * heads_ref[1:2, :])
    return (shifted_raw, dt, cum, cum - jnp.log(dt))


def spread_lanes(table, head, rows):
    return jnp.broadcast_to(table[:, head : head + 1], (rows, PAIR))


def forward_kernel(
    z_ref, xr_ref, bcd_ref, x_ref, go_ref, wout_ref, taps_ref, heads_ref, lanes_ref, seg_ref,
    y_ref, gn_ref, dz_ref, dssd_ref, mixed_ref, slope_ref, state_ref, delta_ref, ggain_ref,
    run_ref, cin_ref, cb_ref, ssd_ref, dgn_ref, high_ref, rest_ref,
):
    half = GROUP // 2

    @pl.when(pl.program_id(0) == 0)
    def _():
        run_ref[...] = jnp.zeros_like(run_ref)
        cin_ref[0:8, :] = jnp.zeros((8, CONVW), jnp.float32)
        ggain_ref[...] = jnp.zeros_like(ggain_ref)

    cin_ref[8 : 8 + GROUP, 0:INNER] = xr_ref[...].astype(jnp.float32)
    cin_ref[8 : 8 + GROUP, INNER:CONVW] = bcd_ref[:, 0 : 2 * STATE].astype(jnp.float32)

    def conv_chunk(chunk, carry):
        at = pl.ds(pl.multiple_of(chunk * PAIR, PAIR), PAIR)
        total = taps_ref[KCONV : KCONV + 1, at] + taps_ref[0:1, at] * cin_ref[5 : 5 + GROUP, at]
        for tap in range(1, KCONV):
            total = total + taps_ref[tap : tap + 1, at] * cin_ref[5 + tap : 5 + tap + GROUP, at]
        sig, value = silu_parts(total)
        mixed_ref[:, at] = value.astype(jnp.bfloat16)
        slope_ref[:, at] = sig + value * (1.0 - sig)
        return carry

    lax.fori_loop(0, CONVW // PAIR, conv_chunk, 0)
    cin_ref[0:8, :] = cin_ref[GROUP : GROUP + 8, :]

    bm = mixed_ref[:, INNER : INNER + STATE]
    cm = mixed_ref[:, INNER + STATE : CONVW]
    bm_t = bm.astype(jnp.float32).T.astype(jnp.bfloat16)
    cb_ref[...] = ndot(cm, bm)
    _, _, cum, late = step_sizes(bcd_ref[:, 2 * STATE :], heads_ref)
    late_t = late.T
    dgn_ref[...] = ndot(go_ref[...], wout_ref[...])
    lower = lower_ones(half, False)
    first = lax.broadcasted_iota(jnp.int32, (1, PAIR), 1) < HEADDIM
    for pair in range(HEADS // 2):
        at = slice(pair * PAIR, (pair + 1) * PAIR)
        xp = mixed_ref[:, at]
        spread = []
        inside = []
        for head in (2 * pair, 2 * pair + 1):
            here = spread_lanes(cum, head, GROUP)
            row = late_t[head : head + 1, :]
            near = jnp.exp(jnp.where(lower, here[:half] - row[:, :half], LOW))
            far = jnp.exp(here[half:] - row[:, :half])
            last = jnp.exp(jnp.where(lower, here[half:] - row[:, half:], LOW))
            near = (cb_ref[:half, :half] * near).astype(jnp.bfloat16)
            far = (cb_ref[half:, :half] * far).astype(jnp.bfloat16)
            last = (cb_ref[half:, half:] * last).astype(jnp.bfloat16)
            above = jnp.dot(near, xp[:half], preferred_element_type=jnp.float32)
            below = jnp.dot(
                jnp.concatenate([far, last], 1), xp, preferred_element_type=jnp.float32
            )
            inside.append(jnp.concatenate([above, below], 0))
            spread.append(here)
        both = jnp.where(first, spread[0], spread[1])
        end = both[GROUP - 1 : GROUP, :]
        state = run_ref[:, at]
        carried = jnp.exp(both) * jnp.dot(
            cm, state.astype(jnp.bfloat16), preferred_element_type=jnp.float32
        )
        xf = xp.astype(jnp.float32)
        ssd_ref[:, at] = (
            jnp.where(first, inside[0], inside[1]) + carried + lanes_ref[1:2, at] * xf
        )
        both_late = jnp.where(
            first, spread_lanes(late, 2 * pair, GROUP), spread_lanes(late, 2 * pair + 1, GROUP)
        )
        xw = (xf * jnp.exp(end - both_late)).astype(jnp.bfloat16)
        state_ref[:, at] = state
        run_ref[:, at] = jnp.exp(end) * state + jnp.dot(
            bm_t, xw, preferred_element_type=jnp.float32
        )

    def gate_rows(index, total):
        rows = pl.ds(pl.multiple_of(index * 16, 16), 16)
        ssd = ssd_ref[rows, :]
        z = z_ref[rows, :].astype(jnp.float32)
        sig, value = silu_parts(z)
        gated = ssd * value
        scale = lax.rsqrt(jnp.mean(gated * gated, -1, keepdims=True) + EPS)
        unit = gated * scale
        gain = lanes_ref[0:1, :]
        gn_ref[rows, :] = (unit * gain).astype(jnp.bfloat16)
        dgn = dgn_ref[rows, :]
        total = total + dgn * unit
        scaled = gain * dgn
        mean = jnp.mean(scaled * unit, -1, keepdims=True)
        dgated = scale * (scaled - unit * mean)
        dssd = (dgated * value).astype(jnp.bfloat16)
        dssd_ref[rows, :] = dssd
        dz_ref[rows, :] = (dgated * ssd * (sig + value * (1.0 - sig))).astype(jnp.bfloat16)
        xh = mixed_ref[rows, 0:INNER].astype(jnp.float32)
        product = dssd.astype(jnp.float32) * (ssd - lanes_ref[1:2, :] * xh)
        top = product.astype(jnp.bfloat16)
        high_ref[rows, :] = top
        rest_ref[rows, :] = (product - top.astype(jnp.float32)).astype(jnp.bfloat16)
        return total

    total = lax.fori_loop(0, GROUP // 16, gate_rows, jnp.zeros((16, INNER), jnp.float32))
    ggain_ref[...] = ggain_ref[...] + total[0:8] + total[8:16]
    seg = seg_ref[...]
    delta_ref[...] = jnp.dot(
        high_ref[...], seg, preferred_element_type=jnp.float32
    ) + jnp.dot(rest_ref[...], seg, preferred_element_type=jnp.float32)
    y_ref[...] = (
        x_ref[...].astype(jnp.float32)
        + jnp.dot(gn_ref[...], wout_ref[...], preferred_element_type=jnp.float32)
    ).astype(jnp.bfloat16)


def backward_kernel(
    xr_ref, bcd_ref, mixed_ref, slope_ref, dssd_ref, state_ref, delta_ref,
    taps_ref, heads_ref, lanes_ref, seg_ref,
    dxr_ref, dbcd_ref, gconv_ref, ghead_ref, gskip_ref,
    run_ref, dext_ref, cb_ref, dcb_ref, xw_ref, dcarry_ref, high_ref, rest_ref, lane_ref, low_ref,
):
    half = GROUP // 2

    @pl.when(pl.program_id(0) == 0)
    def _():
        run_ref[...] = jnp.zeros_like(run_ref)
        dext_ref[GROUP:, :] = jnp.zeros((8, CONVW), jnp.float32)
        gconv_ref[...] = jnp.zeros_like(gconv_ref)
        ghead_ref[...] = jnp.zeros_like(ghead_ref)
        gskip_ref[...] = jnp.zeros_like(gskip_ref)
        lane_ref[...] = jnp.zeros_like(lane_ref)

    bm = mixed_ref[:, INNER : INNER + STATE]
    cm = mixed_ref[:, INNER + STATE : CONVW]
    cm_t = cm.astype(jnp.float32).T.astype(jnp.bfloat16)
    cb_ref[...] = ndot(bm, cm)
    dcb_ref[...] = jnp.zeros_like(dcb_ref)
    raw, dt, cum, late = step_sizes(bcd_ref[:, 2 * STATE :], heads_ref)
    cum_t = cum.T
    upper = lower_ones(half, True)
    first = lax.broadcasted_iota(jnp.int32, (1, PAIR), 1) < HEADDIM
    masks = (first.astype(jnp.float32), 1.0 - first.astype(jnp.float32))
    for pair in range(HEADS // 2):
        at = slice(pair * PAIR, (pair + 1) * PAIR)
        xp = mixed_ref[:, at]
        dp = dssd_ref[:, at]
        xf = xp.astype(jnp.float32)
        df = dp.astype(jnp.float32)
        spread = []
        inside = []
        for place, head in enumerate((2 * pair, 2 * pair + 1)):
            here = spread_lanes(late, head, GROUP)
            row = cum_t[head : head + 1, :]
            own = (xf * masks[place]).astype(jnp.bfloat16)
            dw_top = ndot(own[:half], dp)
            dw_low = ndot(own[half:], dp[half:])
            near = jnp.exp(jnp.where(upper, row[:, :half] - here[:half], LOW))
            dcb_ref[:half, :half] += dw_top[:, :half] * near
            near = (cb_ref[:half, :half] * near).astype(jnp.bfloat16)
            far = jnp.exp(row[:, half:] - here[:half])
            dcb_ref[:half, half:] += dw_top[:, half:] * far
            far = (cb_ref[:half, half:] * far).astype(jnp.bfloat16)
            last = jnp.exp(jnp.where(upper, row[:, half:] - here[half:], LOW))
            dcb_ref[half:, half:] += dw_low * last
            last = (cb_ref[half:, half:] * last).astype(jnp.bfloat16)
            above = jnp.dot(
                jnp.concatenate([near, far], 1), dp, preferred_element_type=jnp.float32
            )
            below = jnp.dot(last, dp[half:], preferred_element_type=jnp.float32)
            inside.append(jnp.concatenate([above, below], 0))
            spread.append(here)
        both = jnp.where(
            first, spread_lanes(cum, 2 * pair, GROUP), spread_lanes(cum, 2 * pair + 1, GROUP)
        )
        end = both[GROUP - 1 : GROUP, :]
        scale = jnp.exp(end - jnp.where(first, spread[0], spread[1]))
        xw_ref[:, at] = (xf * scale).astype(jnp.bfloat16)
        dcarry = (df * jnp.exp(both)).astype(jnp.bfloat16)
        dcarry_ref[:, at] = dcarry
        grad = run_ref[:, at]
        grad_low = grad.astype(jnp.bfloat16)
        low_ref[:, at] = grad_low
        dxs = jnp.dot(bm, grad_low, preferred_element_type=jnp.float32) * scale
        inner = jnp.where(first, inside[0], inside[1]) + dxs
        gskip_ref[0:1, at] += jnp.sum(df * xf, 0, keepdims=True)
        product = xf * inner
        top = product.astype(jnp.bfloat16)
        high_ref[:, at] = top
        rest_ref[:, at] = (product - top.astype(jnp.float32)).astype(jnp.bfloat16)
        dmixed = (inner + lanes_ref[1:2, at] * df).astype(jnp.bfloat16).astype(jnp.float32)
        dext_ref[0:GROUP, at] = dmixed * slope_ref[:, at]
        decay = jnp.exp(end)
        lane_ref[0:1, at] = jnp.sum(xf * dxs, 0, keepdims=True) + decay * jnp.sum(
            grad * state_ref[:, at], 0, keepdims=True
        )
        run_ref[:, at] = decay * grad + jnp.dot(cm_t, dcarry, preferred_element_type=jnp.float32)

    dcb_t = dcb_ref[...]
    dcb = dcb_t.T.astype(jnp.bfloat16)
    dbm = ndot(xw_ref[...], low_ref[...]) + jnp.dot(
        dcb_t.astype(jnp.bfloat16), cm, preferred_element_type=jnp.float32
    )
    dcm = ndot(dcarry_ref[...], state_ref[...].astype(jnp.bfloat16)) + jnp.dot(
        dcb, bm, preferred_element_type=jnp.float32
    )
    for place, part in enumerate((dbm, dcm)):
        at = slice(INNER + place * STATE, INNER + (place + 1) * STATE)
        dext_ref[0:GROUP, at] = part.astype(jnp.bfloat16).astype(jnp.float32) * slope_ref[:, at]
    seg = seg_ref[...]
    sums = jnp.dot(high_ref[...], seg, preferred_element_type=jnp.float32) + jnp.dot(
        rest_ref[...], seg, preferred_element_type=jnp.float32
    )
    dlast = split_dot(lane_ref[...], seg)[0:1, :]
    final = lax.broadcasted_iota(jnp.int32, (GROUP, 1), 0) == GROUP - 1
    dcum = delta_ref[...] - sums + jnp.where(final, dlast, 0.0)
    ones = lower_ones(GROUP, True).astype(jnp.float32).astype(jnp.bfloat16)
    dlog = exact_dot(ones, dcum)
    rate = heads_ref[1:2, :]
    ddt = jnp.where(dt > 0.0, sums / dt, 0.0) + dlog * rate
    ddt = ddt / (1.0 + jnp.exp(-raw))
    dbcd_ref[:, 2 * STATE :] = ddt.astype(jnp.bfloat16)
    ghead_ref[0:1, :] += jnp.sum(ddt, 0, keepdims=True)
    ghead_ref[1:2, :] += jnp.sum(dlog * dt, 0, keepdims=True) * rate

    def conv_piece(at, source):
        given = source.astype(jnp.float32)
        total = None
        for tap in range(KCONV):
            moved = dext_ref[KCONV - 1 - tap : KCONV - 1 - tap + GROUP, at]
            term = taps_ref[tap : tap + 1, at] * moved
            total = term if total is None else total + term
            gconv_ref[tap : tap + 1, at] += jnp.sum(given * moved, 0, keepdims=True)
            if tap == KCONV - 1:
                gconv_ref[KCONV : KCONV + 1, at] += jnp.sum(moved, 0, keepdims=True)
        return total.astype(jnp.bfloat16)

    def conv_chunk(chunk, carry):
        at = pl.ds(pl.multiple_of(chunk * PAIR, PAIR), PAIR)
        dxr_ref[:, at] = conv_piece(at, xr_ref[:, at])
        return carry

    lax.fori_loop(0, INNER // PAIR, conv_chunk, 0)
    for place in range(2):
        at = slice(INNER + place * STATE, INNER + (place + 1) * STATE)
        inner = slice(place * STATE, (place + 1) * STATE)
        dbcd_ref[:, inner] = conv_piece(at, bcd_ref[:, inner])
    dext_ref[GROUP:, :] = dext_ref[0:8, :]


def run_forward(proj, x, go, wout, taps, heads, lanes, seg):
    length = x.shape[0]
    count = length // GROUP
    tall = lambda width: pl.BlockSpec((GROUP, width), lambda i: (i, 0))
    fixed = lambda a: pl.BlockSpec(a.shape, lambda i: (0, 0))
    f32, b16 = jnp.float32, jnp.bfloat16
    return pl.pallas_call(
        forward_kernel,
        grid=(count,),
        in_specs=[
            pl.BlockSpec((GROUP, INNER), lambda i: (i, 0)),
            pl.BlockSpec((GROUP, INNER), lambda i: (i, 1)),
            pl.BlockSpec((GROUP, TAIL), lambda i: (i, 2 * INNER // TAIL)),
            tall(WIDE), tall(WIDE), fixed(wout), fixed(taps), fixed(heads), fixed(lanes), fixed(seg),
        ],
        out_specs=[
            tall(WIDE), tall(INNER), tall(INNER), tall(INNER), tall(CONVW), tall(CONVW),
            pl.BlockSpec((STATE, INNER), lambda i: (i, 0)), tall(PAIR),
            pl.BlockSpec((8, INNER), lambda i: (0, 0)),
        ],
        out_shape=[
            jax.ShapeDtypeStruct((length, WIDE), b16),
            jax.ShapeDtypeStruct((length, INNER), b16),
            jax.ShapeDtypeStruct((length, INNER), b16),
            jax.ShapeDtypeStruct((length, INNER), b16),
            jax.ShapeDtypeStruct((length, CONVW), b16),
            jax.ShapeDtypeStruct((length, CONVW), f32),
            jax.ShapeDtypeStruct((count * STATE, INNER), f32),
            jax.ShapeDtypeStruct((length, PAIR), f32),
            jax.ShapeDtypeStruct((8, INNER), f32),
        ],
        scratch_shapes=[
            pltpu.VMEM((STATE, INNER), f32), pltpu.VMEM((GROUP + 8, CONVW), f32),
            pltpu.VMEM((GROUP, GROUP), f32), pltpu.VMEM((GROUP, INNER), f32),
            pltpu.VMEM((GROUP, INNER), f32), pltpu.VMEM((GROUP, INNER), b16),
            pltpu.VMEM((GROUP, INNER), b16),
        ],
        compiler_params=pltpu.CompilerParams(
            dimension_semantics=("arbitrary",), vmem_limit_bytes=48 * 1024 * 1024
        ),
        cost_estimate=pl.CostEstimate(flops=12 * 10**9, bytes_accessed=40 * 10**6, transcendentals=10**7),
        name="scan_forward",
    )(proj, proj, proj, x, go, wout, taps, heads, lanes, seg)


def run_backward(proj, mixed, slope, dssd, states, delta, taps, heads, lanes, seg):
    length = proj.shape[0]
    count = length // GROUP
    tall = lambda width: pl.BlockSpec((GROUP, width), lambda i: (count - 1 - i, 0))
    fixed = lambda a: pl.BlockSpec(a.shape, lambda i: (0, 0))
    f32, b16 = jnp.float32, jnp.bfloat16
    return pl.pallas_call(
        backward_kernel,
        grid=(count,),
        in_specs=[
            pl.BlockSpec((GROUP, INNER), lambda i: (count - 1 - i, 1)),
            pl.BlockSpec((GROUP, TAIL), lambda i: (count - 1 - i, 2 * INNER // TAIL)),
            tall(CONVW), tall(CONVW), tall(INNER),
            pl.BlockSpec((STATE, INNER), lambda i: (count - 1 - i, 0)), tall(PAIR),
            fixed(taps), fixed(heads), fixed(lanes), fixed(seg),
        ],
        out_specs=[
            tall(INNER), tall(TAIL),
            pl.BlockSpec((8, CONVW), lambda i: (0, 0)),
            pl.BlockSpec((8, PAIR), lambda i: (0, 0)),
            pl.BlockSpec((8, INNER), lambda i: (0, 0)),
        ],
        out_shape=[
            jax.ShapeDtypeStruct((length, INNER), b16),
            jax.ShapeDtypeStruct((length, TAIL), b16),
            jax.ShapeDtypeStruct((8, CONVW), f32),
            jax.ShapeDtypeStruct((8, PAIR), f32),
            jax.ShapeDtypeStruct((8, INNER), f32),
        ],
        scratch_shapes=[
            pltpu.VMEM((STATE, INNER), f32), pltpu.VMEM((GROUP + 8, CONVW), f32),
            pltpu.VMEM((GROUP, GROUP), f32), pltpu.VMEM((GROUP, GROUP), f32),
            pltpu.VMEM((GROUP, INNER), b16), pltpu.VMEM((GROUP, INNER), b16),
            pltpu.VMEM((GROUP, INNER), b16), pltpu.VMEM((GROUP, INNER), b16),
            pltpu.VMEM((8, INNER), f32), pltpu.VMEM((STATE, INNER), b16),
        ],
        compiler_params=pltpu.CompilerParams(
            dimension_semantics=("arbitrary",), vmem_limit_bytes=48 * 1024 * 1024
        ),
        cost_estimate=pl.CostEstimate(flops=12 * 10**9, bytes_accessed=40 * 10**6, transcendentals=10**7),
        name="scan_backward",
    )(proj, proj, mixed, slope, dssd, states, delta, taps, heads, lanes, seg)


def head_segments():
    rows = lax.broadcasted_iota(jnp.int32, (INNER, PAIR), 0) // HEADDIM
    cols = lax.broadcasted_iota(jnp.int32, (INNER, PAIR), 1)
    return (rows == cols).astype(jnp.bfloat16)


def head_tables(dt_bias, rate, skip):
    pad = lambda v: jnp.pad(v.astype(jnp.float32), (0, PAIR - HEADS))
    zero = jnp.zeros((PAIR,), jnp.float32)
    heads = jnp.stack([pad(dt_bias), pad(rate)] + [zero] * 6)
    return (heads, jnp.repeat(skip, HEADDIM))


def whole_sequence(xb, cot, wts, dt_bias, rate, skip):
    gain_in, w_in, taps_bias, gain_gate, w_out = wts
    xf = xb.astype(jnp.float32)
    r_in = lax.rsqrt(jnp.mean(xf * xf, -1, keepdims=True) + EPS)
    gain = gain_in.astype(jnp.float32)
    normed = (xf * r_in * gain).astype(jnp.bfloat16)
    proj = jnp.dot(normed, w_in, preferred_element_type=jnp.float32).astype(jnp.bfloat16)
    heads, skip_lanes = head_tables(dt_bias, rate, skip)
    lanes = jnp.stack([gain_gate.astype(jnp.float32), skip_lanes] + [jnp.zeros_like(skip_lanes)] * 6)
    seg = head_segments()
    y, gnorm, dz, dssd, mixed, slope, states, delta, ggain = run_forward(
        proj, xb, cot, w_out, taps_bias, heads, lanes, seg
    )
    grad_wout = tdot(gnorm, cot)
    grad_wz = tdot(normed, dz)
    dxr, dbcd, gconv, ghead, gskip = run_backward(
        proj, mixed, slope, dssd, states, delta, taps_bias, heads, lanes, seg
    )
    dnormed = (
        ndot(dz, w_in[:, :INNER]) + ndot(dxr, w_in[:, INNER : 2 * INNER]) + ndot(dbcd, w_in[:, 2 * INNER :])
    )
    scaled = gain * dnormed
    dx = (
        r_in * scaled
        - xf * r_in**3 * jnp.mean(scaled * xf, -1, keepdims=True)
        + cot.astype(jnp.float32)
    ).astype(jnp.bfloat16)
    grad_gin = jnp.sum(dnormed * xf * r_in, 0)
    grad_wx = tdot(normed, dxr)
    grad_wtail = tdot(normed, dbcd)
    head_terms = jnp.concatenate(
        [ghead[0, :HEADS], ghead[1, :HEADS], jnp.sum(gskip[0].reshape(HEADS, HEADDIM), -1)]
    )
    return (
        y, dx,
        (grad_gin, grad_wz, grad_wx, grad_wtail, gconv, jnp.sum(ggain, 0), grad_wout, head_terms),
    )


SMALL = 280


def swap_halves(parts):
    place = lax.axis_index("seq")
    count = lax.axis_size("seq")
    size = parts.shape[1]
    whole = jnp.zeros((count * size,) + parts.shape[2:], parts.dtype)
    own = lax.dynamic_index_in_dim(parts, place, 0, False)
    whole = lax.dynamic_update_slice_in_dim(whole, own, place * size, 0)
    for hop in range(1, count):
        there = lax.rem(place + hop, count)
        source = lax.rem(place + count - hop, count)
        sent = lax.dynamic_index_in_dim(parts, there, 0, False)
        got = lax.ppermute(sent, "seq", [(i, (i + hop) % count) for i in range(count)])
        whole = lax.dynamic_update_slice_in_dim(whole, got, source * size, 0)
    return whole


def gather_weights(norm_gain, in_weight, conv_weight, conv_bias, gate_gain, out_weight):
    devices = lax.axis_size(("dp", "seq"))
    rows = in_weight.shape[0]
    small = jnp.concatenate([norm_gain, conv_weight.reshape(-1), conv_bias, gate_gain])
    sizes = (norm_gain.size, conv_weight.size, conv_bias.size, gate_gain.size)
    line = jnp.pad(small[None], ((0, rows - 1), (0, WIDE - SMALL - small.size)))
    pieces = [in_weight[:, k * WIDE : (k + 1) * WIDE] for k in range(4)]
    pieces.append(jnp.concatenate([in_weight[:, 4 * WIDE :], line], 1))
    pieces.append(out_weight)
    packed = jnp.concatenate(pieces, 0)
    full = lax.all_gather(packed, ("dp", "seq"), axis=0)
    columns = [
        full[:, k * rows : (k + 1) * rows].reshape(devices * rows, WIDE) for k in range(4)
    ]
    last = full[:, 4 * rows : 5 * rows].reshape(devices * rows, WIDE)[:, :SMALL]
    columns.append(jnp.pad(last, ((0, 0), (0, TAIL - SMALL))))
    w_in = jnp.concatenate(columns, 1)
    w_out = full[:, 5 * rows :].reshape(devices * out_weight.shape[0], WIDE)
    table = full[:, 4 * rows, SMALL : SMALL + small.size]
    a, b, c = sizes[0], sizes[0] + sizes[1], sizes[0] + sizes[1] + sizes[2]
    gain_in = table[:, :a].reshape(-1)
    taps = table[:, a:b].reshape(devices, KCONV, -1).transpose(1, 0, 2).reshape(KCONV, -1)
    bias = table[:, b:c].reshape(1, -1)
    gain_gate = table[:, c:].reshape(-1)
    taps_bias = jnp.pad(
        jnp.concatenate([taps, bias], 0).astype(jnp.float32), ((0, 7 - KCONV), (0, 0))
    )
    return (gain_in, w_in, taps_bias, gain_gate, w_out)


def by_owner(grad, devices):
    return grad.astype(jnp.bfloat16).reshape(devices, -1, grad.shape[-1])


def shards(
    x_in, grad_out, norm_gain, in_weight, conv_weight, conv_bias, gate_gain, out_weight, dt_bias, a_log, skip
):
    if x_in.shape[0] != lax.axis_size("seq"):
        return shards_general(
            x_in, grad_out, norm_gain, in_weight, conv_weight, conv_bias, gate_gain, out_weight,
            dt_bias, a_log, skip,
        )
    rate = -jnp.exp(a_log)
    devices = lax.axis_size(("dp", "seq"))
    micro, _, length, _ = x_in.shape
    rows = in_weight.shape[0]
    wts = gather_weights(norm_gain, in_weight, conv_weight, conv_bias, gate_gain, out_weight)
    xb = swap_halves(x_in[:, 0])
    cot = swap_halves(grad_out[:, 0])
    y, dx, terms = whole_sequence(xb, cot, wts, dt_bias, rate, skip)
    y_out = swap_halves(y.reshape(micro, length, WIDE)).reshape(x_in.shape)
    dx_in = swap_halves(dx.reshape(micro, length, WIDE)).reshape(x_in.shape)
    grad_gin, grad_wz, grad_wx, grad_wtail, gconv, ggain, grad_wout, head_terms = terms
    early = jnp.concatenate(
        [
            by_owner(grad_wz[:, :WIDE], devices),
            by_owner(grad_wz[:, WIDE:], devices),
            by_owner(grad_wout, devices),
        ],
        1,
    )
    small = jnp.concatenate(
        [
            grad_gin.reshape(devices, -1),
            gconv[:KCONV].reshape(KCONV, devices, -1).transpose(1, 0, 2).reshape(devices, -1),
            gconv[KCONV].reshape(devices, -1),
            ggain.reshape(devices, -1),
            jnp.broadcast_to(head_terms, (devices, 3 * HEADS)),
        ],
        1,
    ).astype(jnp.bfloat16)
    line = jnp.pad(small[:, None], ((0, 0), (0, rows - 1), (0, WIDE - SMALL - small.shape[1])))
    late = jnp.concatenate(
        [
            by_owner(grad_wx[:, :WIDE], devices),
            by_owner(grad_wx[:, WIDE:], devices),
            jnp.concatenate([by_owner(grad_wtail[:, :SMALL], devices), line], 2),
        ],
        1,
    )
    early = reduce_owned(early).astype(jnp.float32)
    late = reduce_owned(late).astype(jnp.float32)
    own_in = jnp.concatenate(
        [early[:rows], early[rows : 2 * rows], late[:rows], late[rows : 2 * rows], late[2 * rows :, :SMALL]],
        1,
    )
    own = late[2 * rows, SMALL : SMALL + small.shape[1]]
    cuts = [norm_gain.size, conv_weight.size, conv_bias.size, gate_gain.size, HEADS, HEADS, HEADS]
    found = []
    at = 0
    for size in cuts:
        found.append(own[at : at + size])
        at += size
    return (
        y_out,
        dx_in,
        found[0],
        own_in,
        found[1].reshape(conv_weight.shape),
        found[2],
        found[3],
        early[2 * rows :],
        found[4],
        found[5],
        found[6],
    )


def reduce_owned(parts):
    return lax.psum_scatter(parts, ("dp", "seq"), scatter_dimension=0, tiled=False)


def shards_general(
    x_in,
    grad_out,
    norm_gain,
    in_weight,
    conv_weight,
    conv_bias,
    gate_gain,
    out_weight,
    dt_bias,
    a_log,
    skip,
):
    micro = x_in.shape[0]
    rate = -jnp.exp(a_log)
    devices = lax.axis_size(("dp", "seq"))
    results = []
    saves = []
    for index in range(micro):
        wts = (
            lax.all_gather(norm_gain, ("dp", "seq"), axis=0, tiled=True),
            lax.all_gather(in_weight, ("dp", "seq"), axis=0, tiled=True),
            lax.all_gather(conv_weight, ("dp", "seq"), axis=1, tiled=True),
            lax.all_gather(conv_bias, ("dp", "seq"), axis=0, tiled=True),
            lax.all_gather(gate_gain, ("dp", "seq"), axis=0, tiled=True),
            lax.all_gather(out_weight, ("dp", "seq"), axis=0, tiled=True),
        )
        result, saved = forward(x_in[index, 0], wts, dt_bias, rate, skip)
        results.append(result)
        saves.append(saved)
    dx_list = [None] * micro
    summed = None
    for index in reversed(range(micro)):
        wts = (
            lax.all_gather(norm_gain, ("dp", "seq"), axis=0, tiled=True),
            lax.all_gather(in_weight, ("dp", "seq"), axis=0, tiled=True),
            lax.all_gather(conv_weight, ("dp", "seq"), axis=1, tiled=True),
            lax.all_gather(conv_bias, ("dp", "seq"), axis=0, tiled=True),
            lax.all_gather(gate_gain, ("dp", "seq"), axis=0, tiled=True),
            lax.all_gather(out_weight, ("dp", "seq"), axis=0, tiled=True),
        )
        dx_part, terms = backward(saves[index], grad_out[index, 0], wts, dt_bias, rate, skip)
        dx_list[index] = dx_part
        summed = terms if summed is None else jax.tree.map(lambda a, b: a + b, summed, terms)
    spread = summed[:6] + (jnp.broadcast_to(summed[6], (devices, 3 * HEADS)),)
    summed = (
        lax.psum_scatter(spread[0], ("dp", "seq"), scatter_dimension=0, tiled=True),
        lax.psum_scatter(spread[1], ("dp", "seq"), scatter_dimension=0, tiled=True),
        lax.psum_scatter(spread[2], ("dp", "seq"), scatter_dimension=1, tiled=True),
        lax.psum_scatter(spread[3], ("dp", "seq"), scatter_dimension=0, tiled=True),
        lax.psum_scatter(spread[4], ("dp", "seq"), scatter_dimension=0, tiled=True),
        lax.psum_scatter(spread[5], ("dp", "seq"), scatter_dimension=0, tiled=True),
        lax.psum_scatter(spread[6], ("dp", "seq"), scatter_dimension=0, tiled=True),
    )
    heads_sum = summed[6].reshape(3, HEADS)
    y_out = jnp.stack(results)[:, None]
    dx_in = jnp.stack(dx_list)[:, None]
    return (
        y_out,
        dx_in,
        summed[0],
        summed[1],
        summed[2],
        summed[3],
        summed[4],
        summed[5],
        heads_sum[0],
        heads_sum[1],
        heads_sum[2],
    )


def solution(mesh):
    return jax.shard_map(
        shards,
        mesh=mesh,
        in_specs=(
            P(None, "dp", "seq", None),
            P(None, "dp", "seq", None),
            P(("dp", "seq")),
            P(("dp", "seq"), None),
            P(None, ("dp", "seq")),
            P(("dp", "seq")),
            P(("dp", "seq")),
            P(("dp", "seq"), None),
            P(),
            P(),
            P(),
        ),
        out_specs=(
            P(None, "dp", "seq", None),
            P(None, "dp", "seq", None),
            P(("dp", "seq")),
            P(("dp", "seq"), None),
            P(None, ("dp", "seq")),
            P(("dp", "seq")),
            P(("dp", "seq")),
            P(("dp", "seq"), None),
            P(),
            P(),
            P(),
        ),
        check_vma=False,
    )
```

```python
import jax
import jax.numpy as jnp
from jax import lax
from jax.experimental import pallas as pl
from jax.experimental.pallas import tpu as pltpu
from jax.sharding import PartitionSpec as P

HEADS = 24
HEADDIM = 64
STATE = 128
KCONV = 4
GROUP = 256
INNER = 1536
CONVW = 1792


EPS = 1e-05


def shifted(array, axis, by):
    devices = lax.axis_size(axis)
    pairs = [(i, i + by) for i in range(devices) if 0 <= i + by < devices]
    return lax.ppermute(array, axis, pairs)


def prefix(array, axis, join, neutral, backward):
    count = lax.axis_size(axis)
    place = lax.axis_index(axis)
    ahead = count - 1 - place if backward else place
    gathered = jax.tree.map(
        lambda a, kind: lax.all_gather(a.astype(kind), axis), array, (jnp.bfloat16, jnp.bfloat16)
    )
    state = jax.tree.map(lambda a, e: jnp.zeros_like(a) + jnp.asarray(e, a.dtype), array, neutral)

    def one(hop, state):
        source = count - 1 - hop if backward else hop
        return join(
            state,
            jax.tree.map(
                lambda a, own: lax.dynamic_index_in_dim(a, source, 0, False).astype(own.dtype),
                gathered,
                array,
            ),
        )

    return lax.fori_loop(0, ahead, one, state)


def tdot(left, right):
    return lax.dot_general(
        left, right, (((0,), (0,)), ((), ())), preferred_element_type=jnp.float32
    )


def ndot(left, right):
    return lax.dot_general(
        left, right, (((1,), (1,)), ((), ())), preferred_element_type=jnp.float32
    )


def dsilu(value):
    sig = jax.nn.sigmoid(value)
    return sig * (1.0 + value * (1.0 - sig))


def merge_states(earlier, later):
    return (earlier[0] * later[0], earlier[1] * later[0][:, None, None] + later[1])


def decay_table(cum_t):
    size = cum_t.shape[-1]
    rows = lax.broadcasted_iota(jnp.int32, (size, size), 0)
    cols = lax.broadcasted_iota(jnp.int32, (size, size), 1)
    lower = rows >= cols
    diff = cum_t[:, :, :, None] - cum_t[:, :, None, :]
    return jnp.exp(jnp.where(lower, diff, 0.0)) * lower.astype(jnp.float32)


def forward(xb, wts, dt_bias, rate, skip):
    gain_in, w_in, w_conv, b_conv, gain_gate, w_out = wts
    length = xb.shape[0]
    count = length // GROUP
    xf = xb.astype(jnp.float32)
    r_in = lax.rsqrt(jnp.mean(xf * xf, -1, keepdims=True) + EPS)
    normed = (xf * r_in * gain_in.astype(jnp.float32)).astype(jnp.bfloat16)
    proj = jnp.dot(normed, w_in, preferred_element_type=jnp.float32).astype(jnp.bfloat16)
    conv_in = proj[:, INNER : INNER + CONVW]
    rim = shifted(conv_in[length - KCONV + 1 :], "seq", 1)
    padded = jnp.concatenate([rim, conv_in], 0).astype(jnp.float32)
    taps = w_conv.astype(jnp.float32)
    conv_out = b_conv.astype(jnp.float32) + jnp.zeros((length, CONVW), jnp.float32)
    for tap in range(KCONV):
        conv_out = conv_out + taps[tap] * padded[tap : tap + length]
    mixed = jax.nn.silu(conv_out).astype(jnp.bfloat16)
    xh = mixed[:, :INNER].reshape(count, GROUP, HEADS, HEADDIM)
    bm = mixed[:, INNER : INNER + STATE].reshape(count, GROUP, STATE)
    cm = mixed[:, INNER + STATE :].reshape(count, GROUP, STATE)
    dt_raw = proj[:, INNER + CONVW :].astype(jnp.float32)
    step = jax.nn.softplus(dt_raw + dt_bias)
    step_t = step.reshape(count, GROUP, HEADS).transpose(0, 2, 1)
    cum_t = jnp.cumsum(step_t * rate[None, :, None], -1)
    decay = decay_table(cum_t)
    cbm = jnp.einsum("ctn,csn->cts", cm, bm, preferred_element_type=jnp.float32)
    weights = (cbm[:, None] * decay * step_t[:, :, None, :]).astype(jnp.bfloat16)
    inside = jnp.einsum("chts,cshp->cthp", weights, xh, preferred_element_type=jnp.float32)
    last = cum_t[:, :, -1]
    block_decay = jnp.exp(last)
    scale = (jnp.exp(last[:, :, None] - cum_t) * step_t).transpose(0, 2, 1)
    x_scaled = (xh.astype(jnp.float32) * scale[..., None]).astype(jnp.bfloat16)
    local = jnp.einsum("cshp,csn->chpn", x_scaled, bm, preferred_element_type=jnp.float32)
    total_decay = jnp.ones((HEADS,), jnp.float32)
    total_state = jnp.zeros((HEADS, HEADDIM, STATE), jnp.float32)
    for block in range(count):
        total_state = total_state * block_decay[block][:, None, None] + local[block]
        total_decay = total_decay * block_decay[block]
    identity = (jnp.ones((HEADS,), jnp.float32), jnp.zeros((HEADS, HEADDIM, STATE), jnp.float32))
    _, incoming = prefix((total_decay, total_state), "seq", merge_states, identity, False)
    entering = []
    running = incoming
    for block in range(count):
        entering.append(running)
        running = running * block_decay[block][:, None, None] + local[block]
    state_in = jnp.stack(entering)
    state_low = state_in.astype(jnp.bfloat16)
    exp_cum = jnp.exp(cum_t).transpose(0, 2, 1)
    carried = exp_cum[..., None] * jnp.einsum(
        "ctn,chpn->cthp", cm, state_low, preferred_element_type=jnp.float32
    )
    ssd = (inside + carried + skip[None, None, :, None] * xh.astype(jnp.float32)).reshape(
        length, INNER
    )
    zsig = jax.nn.silu(proj[:, :INNER].astype(jnp.float32))
    gated = ssd * zsig
    r_gate = lax.rsqrt(jnp.mean(gated * gated, -1, keepdims=True) + EPS)
    gnorm = (gated * r_gate * gain_gate.astype(jnp.float32)).astype(jnp.bfloat16)
    result = (xf + jnp.dot(gnorm, w_out, preferred_element_type=jnp.float32)).astype(jnp.bfloat16)
    saved = (
        xf,
        r_in,
        normed,
        proj,
        padded,
        conv_out,
        mixed,
        step_t,
        cum_t,
        state_in,
        state_low,
        carried,
        ssd,
        zsig,
        gated,
        r_gate,
        gnorm,
    )
    return (result, saved)


def backward(saved, cot, wts, dt_bias, rate, skip):
    gain_in, w_in, w_conv, b_conv, gain_gate, w_out = wts
    (
        xf,
        r_in,
        normed,
        proj,
        padded,
        conv_out,
        mixed,
        step_t,
        cum_t,
        state_in,
        state_low,
        carried,
        ssd,
        zsig,
        gated,
        r_gate,
        gnorm,
    ) = saved
    length = xf.shape[0]
    count = length // GROUP
    grad_wout = tdot(gnorm, cot)
    dgnorm = ndot(cot, w_out)
    scaled_g = gain_gate.astype(jnp.float32) * dgnorm
    grad_ggain = jnp.sum(dgnorm * gated * r_gate, 0)
    dgated = r_gate * scaled_g - gated * r_gate**3 * jnp.mean(scaled_g * gated, -1, keepdims=True)
    dssd = (dgated * zsig).astype(jnp.bfloat16)
    zpart = proj[:, :INNER].astype(jnp.float32)
    dzpart = dgated * ssd * dsilu(zpart)
    xh = mixed[:, :INNER].reshape(count, GROUP, HEADS, HEADDIM)
    bm = mixed[:, INNER : INNER + STATE].reshape(count, GROUP, STATE)
    cm = mixed[:, INNER + STATE :].reshape(count, GROUP, STATE)
    xhf = xh.astype(jnp.float32)
    dyr = dssd.reshape(count, GROUP, HEADS, HEADDIM)
    dyf = dyr.astype(jnp.float32)
    decay = decay_table(cum_t)
    cbm = jnp.einsum("ctn,csn->cts", cm, bm, preferred_element_type=jnp.float32)
    full = cbm[:, None] * decay * step_t[:, :, None, :]
    weights = full.astype(jnp.bfloat16)
    grad_skip = jnp.sum(dyf * xhf, (0, 1, 3))
    dxh = skip[None, None, :, None] * dyf
    dweights = jnp.einsum("cthp,cshp->chts", dyr, xh, preferred_element_type=jnp.float32)
    dxh = dxh + jnp.einsum("chts,cthp->cshp", weights, dyr, preferred_element_type=jnp.float32)
    dcbm = jnp.sum(dweights * decay * step_t[:, :, None, :], 1).astype(jnp.bfloat16)
    dstep = jnp.sum(dweights * cbm[:, None] * decay, 2)
    product = dweights * full
    dcum = jnp.sum(product, 3) - jnp.sum(product, 2)
    dcum = dcum + jnp.sum(dyf * carried, -1).transpose(0, 2, 1)
    exp_cum = jnp.exp(cum_t).transpose(0, 2, 1)
    dcarry = (dyf * exp_cum[..., None]).astype(jnp.bfloat16)
    dcm = jnp.einsum("cthp,chpn->ctn", dcarry, state_low, preferred_element_type=jnp.float32)
    dstate_low = jnp.einsum("cthp,ctn->chpn", dcarry, cm, preferred_element_type=jnp.float32)
    last = cum_t[:, :, -1]
    block_decay = jnp.exp(last)
    total_decay = jnp.ones((HEADS,), jnp.float32)
    running = jnp.zeros((HEADS, HEADDIM, STATE), jnp.float32)
    for block in reversed(range(count)):
        running = running * block_decay[block][:, None, None] + dstate_low[block]
        total_decay = total_decay * block_decay[block]
    identity = (jnp.ones((HEADS,), jnp.float32), jnp.zeros((HEADS, HEADDIM, STATE), jnp.float32))
    _, later = prefix((total_decay, running), "seq", merge_states, identity, True)
    leaving = [later] * count
    running = later
    for block in reversed(range(count)):
        leaving[block] = running
        running = running * block_decay[block][:, None, None] + dstate_low[block]
    grad_state = jnp.stack(leaving)
    dlast = block_decay * jnp.sum(grad_state * state_in, (2, 3))
    scale_t = jnp.exp(last[:, :, None] - cum_t) * step_t
    scale = scale_t.transpose(0, 2, 1)
    x_scaled = (xhf * scale[..., None]).astype(jnp.bfloat16)
    grad_low = grad_state.astype(jnp.bfloat16)
    dxs = jnp.einsum("csn,chpn->cshp", bm, grad_low, preferred_element_type=jnp.float32)
    dbm = jnp.einsum("cshp,chpn->csn", x_scaled, grad_low, preferred_element_type=jnp.float32)
    dxh = dxh + dxs * scale[..., None]
    dscale = jnp.sum(dxs * xhf, -1).transpose(0, 2, 1)
    dstep = dstep + dscale * jnp.exp(last[:, :, None] - cum_t)
    dlast = dlast + jnp.sum(dscale * scale_t, -1)
    dcum = dcum - dscale * scale_t
    final = (lax.broadcasted_iota(jnp.int32, (GROUP,), 0) == GROUP - 1).astype(jnp.float32)
    dcum = dcum + dlast[:, :, None] * final
    dlog = jnp.flip(jnp.cumsum(jnp.flip(dcum, -1), -1), -1)
    dstep = dstep + dlog * rate[None, :, None]
    grad_alog = jnp.sum(dlog * step_t, (0, 2)) * rate
    dcm = dcm + jnp.einsum("cts,csn->ctn", dcbm, bm, preferred_element_type=jnp.float32)
    dbm = dbm + jnp.einsum("cts,ctn->csn", dcbm, cm, preferred_element_type=jnp.float32)
    dmixed = jnp.concatenate(
        [dxh.reshape(length, INNER), dbm.reshape(length, STATE), dcm.reshape(length, STATE)], -1
    )
    dmixed = dmixed.astype(jnp.bfloat16).astype(jnp.float32)
    dconv = dmixed * dsilu(conv_out)
    grad_cbias = jnp.sum(dconv, 0)
    grad_cweight = jnp.stack(
        [jnp.sum(dconv * padded[tap : tap + length], 0) for tap in range(KCONV)]
    )
    rim_back = shifted(dconv[: KCONV - 1], "seq", -1)
    extended = jnp.concatenate([dconv, rim_back], 0)
    taps = w_conv.astype(jnp.float32)
    dconv_in = jnp.zeros((length, CONVW), jnp.float32)
    for tap in range(KCONV):
        dconv_in = dconv_in + taps[tap] * extended[KCONV - 1 - tap : KCONV - 1 - tap + length]
    dt_raw = proj[:, INNER + CONVW :].astype(jnp.float32)
    ddt_raw = dstep.transpose(0, 2, 1).reshape(length, HEADS) * jax.nn.sigmoid(dt_raw + dt_bias)
    grad_dtb = jnp.sum(ddt_raw, 0)
    dproj = jnp.concatenate([dzpart, dconv_in, ddt_raw], -1).astype(jnp.bfloat16)
    grad_win = tdot(normed, dproj)
    dnormed = ndot(dproj, w_in)
    scaled_in = gain_in.astype(jnp.float32) * dnormed
    grad_gin = jnp.sum(dnormed * xf * r_in, 0)
    dx_in = (
        r_in * scaled_in
        - xf * r_in**3 * jnp.mean(scaled_in * xf, -1, keepdims=True)
        + cot.astype(jnp.float32)
    )
    head_terms = jnp.stack([grad_dtb, grad_alog, grad_skip]).reshape(1, 3 * HEADS)
    return (
        dx_in.astype(jnp.bfloat16),
        (grad_gin, grad_win, grad_cweight, grad_cbias, grad_ggain, grad_wout, head_terms),
    )


PAIR = 2 * HEADDIM
WIDE = 768
XTAIL = 1920
LOW = -1e30


def silu_parts(value):
    sig = 0.5 * jnp.tanh(0.5 * value) + 0.5
    return (sig, value * sig)


def split_dot(value, right):
    top = value.astype(jnp.bfloat16)
    rest = (value - top.astype(jnp.float32)).astype(jnp.bfloat16)
    return jnp.dot(top, right, preferred_element_type=jnp.float32) + jnp.dot(
        rest, right, preferred_element_type=jnp.float32
    )


def exact_dot(left, value):
    total = None
    for _ in range(3):
        part = value.astype(jnp.bfloat16)
        value = value - part.astype(jnp.float32)
        term = jnp.dot(left, part, preferred_element_type=jnp.float32)
        total = term if total is None else total + term
    return total


def lower_ones(size, flipped):
    rows = lax.broadcasted_iota(jnp.int32, (size, size), 0)
    cols = lax.broadcasted_iota(jnp.int32, (size, size), 1)
    return rows <= cols if flipped else rows >= cols


def step_sizes(raw, heads_ref):
    shifted_raw = raw.astype(jnp.float32) + heads_ref[0:1, :]
    dt = jnp.maximum(shifted_raw, 0.0) + jnp.log1p(jnp.exp(-jnp.abs(shifted_raw)))
    ones = lower_ones(GROUP, False).astype(jnp.float32).astype(jnp.bfloat16)
    cum = exact_dot(ones, dt * heads_ref[1:2, :])
    return (shifted_raw, dt, cum, cum - jnp.log(dt))


def spread_lanes(table, head, rows):
    return jnp.broadcast_to(table[:, head : head + 1], (rows, PAIR))


def scan_kernel(
    xt_ref, taps_ref, heads_ref, lanes_ref,
    mixed_ref, slope_ref, state_ref, ssd_ref,
    run_ref, cin_ref, cb_ref,
):
    half = GROUP // 2

    @pl.when(pl.program_id(0) == 0)
    def _():
        run_ref[...] = jnp.zeros_like(run_ref)
        cin_ref[0:8, :] = jnp.zeros((8, CONVW), jnp.float32)

    cin_ref[8 : 8 + GROUP, :] = xt_ref[:, 0:CONVW].astype(jnp.float32)

    def conv_chunk(chunk, carry):
        at = pl.ds(pl.multiple_of(chunk * PAIR, PAIR), PAIR)
        total = taps_ref[KCONV : KCONV + 1, at] + taps_ref[0:1, at] * cin_ref[5 : 5 + GROUP, at]
        for tap in range(1, KCONV):
            total = total + taps_ref[tap : tap + 1, at] * cin_ref[5 + tap : 5 + tap + GROUP, at]
        sig, value = silu_parts(total)
        mixed_ref[:, at] = value.astype(jnp.bfloat16)
        slope_ref[:, at] = sig + value * (1.0 - sig)
        return carry

    lax.fori_loop(0, CONVW // PAIR, conv_chunk, 0)
    cin_ref[0:8, :] = cin_ref[GROUP : GROUP + 8, :]

    bm = mixed_ref[:, INNER : INNER + STATE]
    cm = mixed_ref[:, INNER + STATE : CONVW]
    bm_t = bm.astype(jnp.float32).T.astype(jnp.bfloat16)
    cb_ref[...] = ndot(cm, bm)
    _, _, cum, late = step_sizes(xt_ref[:, CONVW:], heads_ref)
    late_t = late.T
    lower = lower_ones(half, False)
    first = lax.broadcasted_iota(jnp.int32, (1, PAIR), 1) < HEADDIM
    for pair in range(HEADS // 2):
        at = slice(pair * PAIR, (pair + 1) * PAIR)
        xp = mixed_ref[:, at]
        spread = []
        inside = []
        for head in (2 * pair, 2 * pair + 1):
            here = spread_lanes(cum, head, GROUP)
            row = late_t[head : head + 1, :]
            near = jnp.exp(jnp.where(lower, here[:half] - row[:, :half], LOW))
            far = jnp.exp(here[half:] - row[:, :half])
            last = jnp.exp(jnp.where(lower, here[half:] - row[:, half:], LOW))
            near = (cb_ref[:half, :half] * near).astype(jnp.bfloat16)
            far = (cb_ref[half:, :half] * far).astype(jnp.bfloat16)
            last = (cb_ref[half:, half:] * last).astype(jnp.bfloat16)
            above = jnp.dot(near, xp[:half], preferred_element_type=jnp.float32)
            below = jnp.dot(
                jnp.concatenate([far, last], 1), xp, preferred_element_type=jnp.float32
            )
            inside.append(jnp.concatenate([above, below], 0))
            spread.append(here)
        both = jnp.where(first, spread[0], spread[1])
        end = both[GROUP - 1 : GROUP, :]
        state = run_ref[:, at]
        carried = jnp.exp(both) * jnp.dot(
            cm, state.astype(jnp.bfloat16), preferred_element_type=jnp.float32
        )
        xf = xp.astype(jnp.float32)
        ssd_ref[:, at] = (
            jnp.where(first, inside[0], inside[1]) + carried + lanes_ref[1:2, at] * xf
        )
        both_late = jnp.where(
            first, spread_lanes(late, 2 * pair, GROUP), spread_lanes(late, 2 * pair + 1, GROUP)
        )
        xw = (xf * jnp.exp(end - both_late)).astype(jnp.bfloat16)
        state_ref[:, at] = state
        run_ref[:, at] = jnp.exp(end) * state + jnp.dot(
            bm_t, xw, preferred_element_type=jnp.float32
        )


def gate_kernel(
    z_ref, ssd_ref, xh_ref, x_ref, go_ref, wout_ref, lanes_ref, seg_ref,
    y_ref, gn_ref, dz_ref, dssd_ref, delta_ref, ggain_ref,
    dgn_ref, high_ref, rest_ref,
):
    @pl.when(pl.program_id(0) == 0)
    def _():
        ggain_ref[...] = jnp.zeros_like(ggain_ref)

    dgn_ref[...] = ndot(go_ref[...], wout_ref[...])

    def gate_rows(index, total):
        rows = pl.ds(pl.multiple_of(index * 16, 16), 16)
        ssd = ssd_ref[rows, :]
        z = z_ref[rows, :].astype(jnp.float32)
        sig, value = silu_parts(z)
        gated = ssd * value
        scale = lax.rsqrt(jnp.mean(gated * gated, -1, keepdims=True) + EPS)
        unit = gated * scale
        gain = lanes_ref[0:1, :]
        gn_ref[rows, :] = (unit * gain).astype(jnp.bfloat16)
        dgn = dgn_ref[rows, :]
        total = total + dgn * unit
        scaled = gain * dgn
        mean = jnp.mean(scaled * unit, -1, keepdims=True)
        dgated = scale * (scaled - unit * mean)
        dssd = (dgated * value).astype(jnp.bfloat16)
        dssd_ref[rows, :] = dssd
        dz_ref[rows, :] = (dgated * ssd * (sig + value * (1.0 - sig))).astype(jnp.bfloat16)
        xh = xh_ref[rows, :].astype(jnp.float32)
        product = dssd.astype(jnp.float32) * (ssd - lanes_ref[1:2, :] * xh)
        top = product.astype(jnp.bfloat16)
        high_ref[rows, :] = top
        rest_ref[rows, :] = (product - top.astype(jnp.float32)).astype(jnp.bfloat16)
        return total

    total = lax.fori_loop(0, GROUP // 16, gate_rows, jnp.zeros((16, INNER), jnp.float32))
    ggain_ref[...] = ggain_ref[...] + total[0:8] + total[8:16]
    seg = seg_ref[...]
    delta_ref[...] = jnp.dot(
        high_ref[...], seg, preferred_element_type=jnp.float32
    ) + jnp.dot(rest_ref[...], seg, preferred_element_type=jnp.float32)
    y_ref[...] = (
        x_ref[...].astype(jnp.float32)
        + jnp.dot(gn_ref[...], wout_ref[...], preferred_element_type=jnp.float32)
    ).astype(jnp.bfloat16)


def backward_kernel(
    xt_ref, mixed_ref, slope_ref, dssd_ref, state_ref, delta_ref,
    taps_ref, heads_ref, lanes_ref, seg_ref,
    dxt_ref, gconv_ref, ghead_ref, gskip_ref,
    run_ref, dext_ref, cb_ref, dcb_ref, xw_ref, dcarry_ref, high_ref, rest_ref, lane_ref, low_ref,
):
    half = GROUP // 2

    @pl.when(pl.program_id(0) == 0)
    def _():
        run_ref[...] = jnp.zeros_like(run_ref)
        dext_ref[GROUP:, :] = jnp.zeros((8, CONVW), jnp.float32)
        gconv_ref[...] = jnp.zeros_like(gconv_ref)
        ghead_ref[...] = jnp.zeros_like(ghead_ref)
        gskip_ref[...] = jnp.zeros_like(gskip_ref)
        lane_ref[...] = jnp.zeros_like(lane_ref)

    bm = mixed_ref[:, INNER : INNER + STATE]
    cm = mixed_ref[:, INNER + STATE : CONVW]
    cm_t = cm.astype(jnp.float32).T.astype(jnp.bfloat16)
    cb_ref[...] = ndot(bm, cm)
    dcb_ref[...] = jnp.zeros_like(dcb_ref)
    raw, dt, cum, late = step_sizes(xt_ref[:, CONVW:], heads_ref)
    cum_t = cum.T
    upper = lower_ones(half, True)
    first = lax.broadcasted_iota(jnp.int32, (1, PAIR), 1) < HEADDIM
    masks = (first.astype(jnp.float32), 1.0 - first.astype(jnp.float32))
    for pair in range(HEADS // 2):
        at = slice(pair * PAIR, (pair + 1) * PAIR)
        xp = mixed_ref[:, at]
        dp = dssd_ref[:, at]
        xf = xp.astype(jnp.float32)
        df = dp.astype(jnp.float32)
        spread = []
        inside = []
        for place, head in enumerate((2 * pair, 2 * pair + 1)):
            here = spread_lanes(late, head, GROUP)
            row = cum_t[head : head + 1, :]
            own = (xf * masks[place]).astype(jnp.bfloat16)
            dw_top = ndot(own[:half], dp)
            dw_low = ndot(own[half:], dp[half:])
            near = jnp.exp(jnp.where(upper, row[:, :half] - here[:half], LOW))
            dcb_ref[:half, :half] += dw_top[:, :half] * near
            near = (cb_ref[:half, :half] * near).astype(jnp.bfloat16)
            far = jnp.exp(row[:, half:] - here[:half])
            dcb_ref[:half, half:] += dw_top[:, half:] * far
            far = (cb_ref[:half, half:] * far).astype(jnp.bfloat16)
            last = jnp.exp(jnp.where(upper, row[:, half:] - here[half:], LOW))
            dcb_ref[half:, half:] += dw_low * last
            last = (cb_ref[half:, half:] * last).astype(jnp.bfloat16)
            above = jnp.dot(
                jnp.concatenate([near, far], 1), dp, preferred_element_type=jnp.float32
            )
            below = jnp.dot(last, dp[half:], preferred_element_type=jnp.float32)
            inside.append(jnp.concatenate([above, below], 0))
            spread.append(here)
        both = jnp.where(
            first, spread_lanes(cum, 2 * pair, GROUP), spread_lanes(cum, 2 * pair + 1, GROUP)
        )
        end = both[GROUP - 1 : GROUP, :]
        scale = jnp.exp(end - jnp.where(first, spread[0], spread[1]))
        xw_ref[:, at] = (xf * scale).astype(jnp.bfloat16)
        dcarry = (df * jnp.exp(both)).astype(jnp.bfloat16)
        dcarry_ref[:, at] = dcarry
        grad = run_ref[:, at]
        grad_low = grad.astype(jnp.bfloat16)
        low_ref[:, at] = grad_low
        dxs = jnp.dot(bm, grad_low, preferred_element_type=jnp.float32) * scale
        inner = jnp.where(first, inside[0], inside[1]) + dxs
        gskip_ref[0:1, at] += jnp.sum(df * xf, 0, keepdims=True)
        product = xf * inner
        top = product.astype(jnp.bfloat16)
        high_ref[:, at] = top
        rest_ref[:, at] = (product - top.astype(jnp.float32)).astype(jnp.bfloat16)
        dmixed = (inner + lanes_ref[1:2, at] * df).astype(jnp.bfloat16).astype(jnp.float32)
        dext_ref[0:GROUP, at] = dmixed * slope_ref[:, at]
        decay = jnp.exp(end)
        lane_ref[0:1, at] = jnp.sum(xf * dxs, 0, keepdims=True) + decay * jnp.sum(
            grad * state_ref[:, at], 0, keepdims=True
        )
        run_ref[:, at] = decay * grad + jnp.dot(cm_t, dcarry, preferred_element_type=jnp.float32)

    dcb_t = dcb_ref[...]
    dcb = dcb_t.T.astype(jnp.bfloat16)
    dbm = ndot(xw_ref[...], low_ref[...]) + jnp.dot(
        dcb_t.astype(jnp.bfloat16), cm, preferred_element_type=jnp.float32
    )
    dcm = ndot(dcarry_ref[...], state_ref[...].astype(jnp.bfloat16)) + jnp.dot(
        dcb, bm, preferred_element_type=jnp.float32
    )
    for place, part in enumerate((dbm, dcm)):
        at = slice(INNER + place * STATE, INNER + (place + 1) * STATE)
        dext_ref[0:GROUP, at] = part.astype(jnp.bfloat16).astype(jnp.float32) * slope_ref[:, at]
    seg = seg_ref[...]
    sums = jnp.dot(high_ref[...], seg, preferred_element_type=jnp.float32) + jnp.dot(
        rest_ref[...], seg, preferred_element_type=jnp.float32
    )
    dlast = split_dot(lane_ref[...], seg)[0:1, :]
    final = lax.broadcasted_iota(jnp.int32, (GROUP, 1), 0) == GROUP - 1
    dcum = delta_ref[...] - sums + jnp.where(final, dlast, 0.0)
    ones = lower_ones(GROUP, True).astype(jnp.float32).astype(jnp.bfloat16)
    dlog = exact_dot(ones, dcum)
    rate = heads_ref[1:2, :]
    ddt = jnp.where(dt > 0.0, sums / dt, 0.0) + dlog * rate
    ddt = ddt / (1.0 + jnp.exp(-raw))
    dxt_ref[:, CONVW:] = ddt.astype(jnp.bfloat16)
    ghead_ref[0:1, :] += jnp.sum(ddt, 0, keepdims=True)
    ghead_ref[1:2, :] += jnp.sum(dlog * dt, 0, keepdims=True) * rate

    def conv_chunk(chunk, carry):
        at = pl.ds(pl.multiple_of(chunk * PAIR, PAIR), PAIR)
        given = xt_ref[:, at].astype(jnp.float32)
        total = None
        for tap in range(KCONV):
            moved = dext_ref[KCONV - 1 - tap : KCONV - 1 - tap + GROUP, at]
            term = taps_ref[tap : tap + 1, at] * moved
            total = term if total is None else total + term
            gconv_ref[tap : tap + 1, at] += jnp.sum(given * moved, 0, keepdims=True)
            if tap == KCONV - 1:
                gconv_ref[KCONV : KCONV + 1, at] += jnp.sum(moved, 0, keepdims=True)
        dxt_ref[:, at] = total.astype(jnp.bfloat16)
        return carry

    lax.fori_loop(0, CONVW // PAIR, conv_chunk, 0)
    dext_ref[GROUP:, :] = dext_ref[0:8, :]


def tall_block(width, count=None):
    if count is None:
        return pl.BlockSpec((GROUP, width), lambda i: (i, 0))
    return pl.BlockSpec((GROUP, width), lambda i: (count - 1 - i, 0))


def fixed_block(shape):
    return pl.BlockSpec(shape, lambda i: (0, 0))


def kernel_options():
    return pltpu.CompilerParams(
        dimension_semantics=("arbitrary",), vmem_limit_bytes=48 * 1024 * 1024
    )


def shape_of(rows, width, kind):
    return jax.ShapeDtypeStruct((rows, width), kind)


def run_scan(xt, taps, heads, lanes):
    length = xt.shape[0]
    count = length // GROUP
    f32, b16 = jnp.float32, jnp.bfloat16
    return pl.pallas_call(
        scan_kernel,
        grid=(count,),
        in_specs=[
            tall_block(XTAIL), fixed_block(taps.shape), fixed_block(heads.shape), fixed_block(lanes.shape),
        ],
        out_specs=[
            tall_block(CONVW), tall_block(CONVW), pl.BlockSpec((STATE, INNER), lambda i: (i, 0)),
            tall_block(INNER),
        ],
        out_shape=[
            shape_of(length, CONVW, b16), shape_of(length, CONVW, f32),
            shape_of(count * STATE, INNER, f32), shape_of(length, INNER, f32),
        ],
        scratch_shapes=[
            pltpu.VMEM((STATE, INNER), f32), pltpu.VMEM((GROUP + 8, CONVW), f32),
            pltpu.VMEM((GROUP, GROUP), f32),
        ],
        compiler_params=kernel_options(),
        cost_estimate=pl.CostEstimate(flops=25 * 10**9, bytes_accessed=30 * 10**6, transcendentals=10**7),
        name="scan_forward",
    )(xt, taps, heads, lanes)


def run_gate(z, ssd, mixed, x, go, wout, lanes, seg):
    length = x.shape[0]
    f32, b16 = jnp.float32, jnp.bfloat16
    return pl.pallas_call(
        gate_kernel,
        grid=(length // GROUP,),
        in_specs=[
            tall_block(INNER), tall_block(INNER), tall_block(INNER), tall_block(WIDE), tall_block(WIDE),
            fixed_block(wout.shape), fixed_block(lanes.shape), fixed_block(seg.shape),
        ],
        out_specs=[
            tall_block(WIDE), tall_block(INNER), tall_block(INNER), tall_block(INNER), tall_block(PAIR),
            fixed_block((8, INNER)),
        ],
        out_shape=[
            shape_of(length, WIDE, b16), shape_of(length, INNER, b16), shape_of(length, INNER, b16),
            shape_of(length, INNER, b16), shape_of(length, PAIR, f32), shape_of(8, INNER, f32),
        ],
        scratch_shapes=[
            pltpu.VMEM((GROUP, INNER), f32), pltpu.VMEM((GROUP, INNER), b16),
            pltpu.VMEM((GROUP, INNER), b16),
        ],
        compiler_params=kernel_options(),
        cost_estimate=pl.CostEstimate(flops=20 * 10**9, bytes_accessed=30 * 10**6, transcendentals=10**7),
        name="gate_both_ways",
    )(z, ssd, mixed, x, go, wout, lanes, seg)


def run_backward(xt, mixed, slope, dssd, states, delta, taps, heads, lanes, seg):
    length = xt.shape[0]
    count = length // GROUP
    f32, b16 = jnp.float32, jnp.bfloat16
    return pl.pallas_call(
        backward_kernel,
        grid=(count,),
        in_specs=[
            tall_block(XTAIL, count), tall_block(CONVW, count), tall_block(CONVW, count),
            tall_block(INNER, count), pl.BlockSpec((STATE, INNER), lambda i: (count - 1 - i, 0)),
            tall_block(PAIR, count), fixed_block(taps.shape), fixed_block(heads.shape),
            fixed_block(lanes.shape), fixed_block(seg.shape),
        ],
        out_specs=[
            tall_block(XTAIL, count), fixed_block((8, CONVW)), fixed_block((8, PAIR)),
            fixed_block((8, INNER)),
        ],
        out_shape=[
            shape_of(length, XTAIL, b16), shape_of(8, CONVW, f32), shape_of(8, PAIR, f32),
            shape_of(8, INNER, f32),
        ],
        scratch_shapes=[
            pltpu.VMEM((STATE, INNER), f32), pltpu.VMEM((GROUP + 8, CONVW), f32),
            pltpu.VMEM((GROUP, GROUP), f32), pltpu.VMEM((GROUP, GROUP), f32),
            pltpu.VMEM((GROUP, INNER), b16), pltpu.VMEM((GROUP, INNER), b16),
            pltpu.VMEM((GROUP, INNER), b16), pltpu.VMEM((GROUP, INNER), b16),
            pltpu.VMEM((8, INNER), f32), pltpu.VMEM((STATE, INNER), b16),
        ],
        compiler_params=kernel_options(),
        cost_estimate=pl.CostEstimate(flops=30 * 10**9, bytes_accessed=30 * 10**6, transcendentals=10**7),
        name="scan_backward",
    )(xt, mixed, slope, dssd, states, delta, taps, heads, lanes, seg)


def head_segments():
    rows = lax.broadcasted_iota(jnp.int32, (INNER, PAIR), 0) // HEADDIM
    cols = lax.broadcasted_iota(jnp.int32, (INNER, PAIR), 1)
    return (rows == cols).astype(jnp.bfloat16)


def head_tables(dt_bias, rate, skip):
    pad = lambda v: jnp.pad(v.astype(jnp.float32), (0, PAIR - HEADS))
    zero = jnp.zeros((PAIR,), jnp.float32)
    heads = jnp.stack([pad(dt_bias), pad(rate)] + [zero] * 6)
    return (heads, jnp.repeat(skip, HEADDIM))


def input_norm(xb, gain_in):
    xf = xb.astype(jnp.float32)
    r_in = lax.rsqrt(jnp.mean(xf * xf, -1, keepdims=True) + EPS)
    return (xf, r_in, (xf * r_in * gain_in.astype(jnp.float32)).astype(jnp.bfloat16))


def input_grad(xf, r_in, gain_in, dnormed, cot):
    scaled = gain_in.astype(jnp.float32) * dnormed
    dx = (
        r_in * scaled
        - xf * r_in**3 * jnp.mean(scaled * xf, -1, keepdims=True)
        + cot.astype(jnp.float32)
    ).astype(jnp.bfloat16)
    return (dx, jnp.sum(dnormed * xf * r_in, 0))


def low_dot(left, right):
    return jnp.dot(left, right, preferred_element_type=jnp.float32).astype(jnp.bfloat16)


SPARE = 1816


def grid_place():
    dp = lax.axis_index("dp")
    return (dp // 4, lax.rem(dp // 2, 2), lax.rem(dp, 2), lax.axis_index("seq"))


def grid_moves(step):
    high = lax.axis_size("dp") // 4
    pairs = []
    for z in range(high):
        for y in range(2):
            for c in range(2):
                for x in range(2):
                    to = ((z + step[0]) % high, y ^ step[1], c ^ step[2], x ^ step[3])
                    pairs.append((((z * 2 + y) * 2 + c) * 2 + x, ((to[0] * 2 + to[1]) * 2 + to[2]) * 2 + to[3]))
    return pairs


def grid_send(array, step):
    return lax.ppermute(array, ("dp", "seq"), grid_moves(step))


def pick(array, axes, places):
    start = [0] * array.ndim
    size = list(array.shape)
    for axis, place in zip(axes, places):
        start[axis] = place
        size[axis] = 1
    out = lax.dynamic_slice(array, start, size)
    return out.reshape([n for axis, n in enumerate(array.shape) if axis not in axes])


def add_up(parts):
    total = parts[0].astype(jnp.float32)
    for part in parts[1:]:
        total = total + part.astype(jnp.float32)
    return total


FLIPS = ((0, 1), (1, 0), (1, 1))


def reduce_core(parts, kind=jnp.bfloat16):
    high = lax.axis_size("dp") // 4
    _, _, c, _ = grid_place()
    parts = parts.reshape((high, 2, 2, 2, -1) + parts.shape[1:])
    got = grid_send(pick(parts, (2,), (1 - c,)), (0, 0, 1, 0))
    return add_up([pick(parts, (2,), (c,)), got]).astype(kind)


def plane_parts(parts):
    _, y, _, x = grid_place()
    found = [pick(parts, (1, 2), (y, x))]
    for fy, fx in FLIPS:
        piece = pick(parts, (1, 2), (y ^ fy, x ^ fx))
        found.append(grid_send(piece, (0, fy, 0, fx)))
    return found


def reduce_plane(parts, kind=jnp.bfloat16):
    return add_up(plane_parts(parts)).astype(kind)


def reduce_line(parts):
    high = lax.axis_size("dp") // 4
    z, _, _, _ = grid_place()
    found = [pick(parts, (0,), (z,))]
    for hop in range(1, high):
        piece = pick(parts, (0,), (lax.rem(z + hop, high),))
        found.append(grid_send(piece, (hop, 0, 0, 0)))
    return add_up(found)


def place_in(array, axis, places, pieces):
    for place, piece in zip(places, pieces):
        array = lax.dynamic_update_slice_in_dim(array, jnp.expand_dims(piece, axis), place, axis)
    return array


def gather_line(own):
    high = lax.axis_size("dp") // 4
    z, _, _, _ = grid_place()
    places = [z] + [lax.rem(z + high - hop, high) for hop in range(1, high)]
    pieces = [own] + [grid_send(own, (hop, 0, 0, 0)) for hop in range(1, high)]
    return place_in(jnp.zeros((high,) + own.shape, own.dtype), 0, places, pieces)


def gather_plane(tall):
    return [tall] + [grid_send(tall, (0, fy, 0, fx)) for fy, fx in FLIPS]


def gather_core(pieces, cuts):
    _, y, c, x = grid_place()
    high, rows, _ = pieces[0].shape
    found = []
    for cut in cuts:
        shape = (high, 2, 2, 2, len(cut) * rows, cut[0].stop - cut[0].start)
        found.append(jnp.zeros(shape, pieces[0].dtype))
    for (fy, fx), piece in zip(((0, 0),) + FLIPS, pieces):
        other = grid_send(piece, (0, 0, 1, 0))
        for core, value in ((c, piece), (1 - c, other)):
            for k, cut in enumerate(cuts):
                for j, columns in enumerate(cut):
                    part = value[:, :, columns].reshape(high, 1, 1, 1, rows, -1)
                    start = (0, y ^ fy, core, x ^ fx, j * rows, 0)
                    found[k] = lax.dynamic_update_slice(found[k], part, start)
    return [full.reshape((-1, full.shape[-1])) for full in found]


def gather_small(own):
    high = lax.axis_size("dp") // 4
    z, y, c, x = grid_place()
    flat = own.reshape(1, -1)
    held = jnp.concatenate([flat] + [grid_send(flat, (hop, 0, 0, 0)) for hop in range(1, high)], 0)
    held = jnp.concatenate([held] + [grid_send(held, (0, fy, 0, fx)) for fy, fx in FLIPS], 0)
    held = jnp.concatenate([held, grid_send(held, (0, 0, 1, 0))], 0)
    owner = lax.broadcasted_iota(jnp.int32, (high * 8, high * 8), 0)
    slot = lax.broadcasted_iota(jnp.int32, (high * 8, high * 8), 1)
    hop, flip, core = slot % high, slot // high % 4, slot // (4 * high)
    source = ((z + high - hop) % high * 2 + (y ^ (flip // 2))) * 2 + (c ^ core)
    match = owner == source * 2 + (x ^ (flip % 2))
    order = match.astype(own.dtype)
    return jnp.dot(order, held, preferred_element_type=jnp.float32).reshape((-1,) + own.shape)


def reduce_all(parts, kind=jnp.bfloat16):
    return reduce_line(reduce_plane(reduce_core(parts, kind), kind))


def after(value, *others):
    return lax.optimization_barrier((value,) + others)[0]


def swap_send(parts):
    place = lax.axis_index("seq")
    return grid_send(lax.dynamic_index_in_dim(parts, 1 - place, 0, False), (0, 0, 0, 1))


def swap_join(parts, got):
    place = lax.axis_index("seq")
    own = lax.dynamic_index_in_dim(parts, place, 0, False)
    return jnp.concatenate([jnp.where(place == 0, own, got), jnp.where(place == 0, got, own)], 0)


def swap_halves(parts, *guards):
    return swap_join(parts, after(swap_send(parts), *guards))


def pack_small(gain, taps, bias, gate, heads):
    lines = [taps, bias[None], gate[None], gain[None], heads[None]]
    lines = [jnp.pad(line, ((0, 0), (0, PAIR - line.shape[1]))) for line in lines]
    return jnp.concatenate(lines, 0)


def unpack_small(block, sizes):
    taps = block[..., :KCONV, : sizes[0]]
    return [taps] + [block[..., KCONV + k, :size] for k, size in enumerate(sizes[1:])]


def fast_shards(
    x_in, grad_out, norm_gain, in_weight, conv_weight, conv_bias, gate_gain, out_weight, dt_bias, a_log, skip
):
    rate = -jnp.exp(a_log)
    devices = lax.axis_size(("dp", "seq"))
    micro, _, length, _ = x_in.shape
    rows = in_weight.shape[0]
    sizes = (conv_weight.shape[1], conv_bias.size, gate_gain.size, norm_gain.size)
    first = jnp.pad(in_weight[:, INNER:], ((0, 0), (0, XTAIL - SPARE)))
    second = jnp.concatenate([in_weight[:, :INNER], out_weight[:rows], out_weight[rows:]], 1)
    small = pack_small(norm_gain, conv_weight, conv_bias, gate_gain, jnp.zeros((8,), norm_gain.dtype))

    line_first = gather_line(first)
    xb = swap_halves(x_in[:, 0])
    small = gather_small(small)
    plane_first = gather_plane(line_first)
    line_second = gather_line(after(second, xb))
    (w_xt,) = gather_core(plane_first, [[slice(0, XTAIL)]])
    plane_second = gather_plane(after(line_second, *plane_first))

    taps, bias, gate, gain_in = unpack_small(small, sizes)
    gain_in = gain_in.reshape(-1)
    gate = gate.reshape(-1).astype(jnp.float32)
    taps = taps.transpose(1, 0, 2).reshape(KCONV, -1)
    taps_bias = jnp.concatenate([taps, bias.reshape(1, -1)], 0).astype(jnp.float32)
    taps_bias = jnp.pad(taps_bias, ((0, 7 - KCONV), (0, 0)))
    xf, r_in, normed = input_norm(xb, gain_in)
    heads, skip_lanes = head_tables(dt_bias, rate, skip)
    lanes = jnp.stack([gate, skip_lanes] + [jnp.zeros_like(skip_lanes)] * 6)
    seg = head_segments()
    xt = low_dot(normed, w_xt)
    mixed, slope, states, ssd = run_scan(xt, taps_bias, heads, lanes)
    cot = swap_halves(after(grad_out[:, 0], *plane_first), ssd)

    w_z, w_out = gather_core(
        plane_second,
        [[slice(0, INNER)], [slice(INNER, INNER + WIDE), slice(INNER + WIDE, 2 * INNER)]],
    )
    z = low_dot(normed, w_z)
    y, gnorm, dz, dssd, delta, ggain = run_gate(z, ssd, mixed, xb, cot, w_out, lanes, seg)
    grad_wout = tdot(gnorm, cot).astype(jnp.bfloat16).reshape(devices, 2, rows, WIDE)
    grad_wz = tdot(normed, dz).astype(jnp.bfloat16)
    early = [grad_wz] + [grad_wout[:, k].reshape(WIDE, WIDE) for k in range(2)]
    early = reduce_core(jnp.concatenate(early, 1))
    dssd = after(dssd, early)
    y_got = swap_send(y.reshape(micro, length, WIDE))
    early = plane_parts(early)
    dxt, gconv, ghead, gskip = run_backward(
        xt, mixed, slope, dssd, states, delta, taps_bias, heads, lanes, seg
    )
    dxt, y_got = lax.optimization_barrier((dxt, y_got) + tuple(early))[:2]
    y_out = swap_join(y.reshape(micro, length, WIDE), y_got).reshape(x_in.shape)
    grad_wxt = tdot(normed, dxt).astype(jnp.bfloat16)
    late = reduce_core(grad_wxt)
    dnormed = ndot(after(dz, late), w_z) + ndot(after(dxt, late), w_xt)
    late = plane_parts(late)
    dx, grad_gin = input_grad(xf, r_in, gain_in, dnormed, cot)
    dx_in = swap_halves(after(dx.reshape(micro, length, WIDE), *late)).reshape(x_in.shape)
    late_pieces = late
    both = [add_up(parts).astype(jnp.bfloat16) for parts in (early, late)]
    both = reduce_line(jnp.concatenate(both, -1))
    early, late = both[:, : 2 * INNER], both[:, 2 * INNER :]
    head_terms = jnp.concatenate(
        [ghead[0, :HEADS], ghead[1, :HEADS], jnp.sum(gskip[0].reshape(HEADS, HEADDIM), -1)]
    )
    grad_gin = after(grad_gin, *late_pieces)
    tiny = jax.vmap(pack_small)(
        grad_gin.reshape(devices, -1),
        gconv[:KCONV].reshape(KCONV, devices, -1).transpose(1, 0, 2),
        gconv[KCONV].reshape(devices, -1),
        jnp.sum(ggain, 0).reshape(devices, -1),
        jnp.broadcast_to(head_terms, (devices, 3 * HEADS)),
    )
    own = reduce_all(tiny.reshape(devices * (KCONV + 4), PAIR), jnp.float32)
    own_in = jnp.concatenate([early[:, :INNER], late[:, :SPARE]], 1)
    own_out = jnp.concatenate([early[:, INNER : INNER + WIDE], early[:, INNER + WIDE :]], 0)
    found = unpack_small(own, sizes)
    heads_sum = own[KCONV + 3]
    return (
        y_out, dx_in, found[3], own_in, found[0], found[1], found[2], own_out,
        heads_sum[:HEADS], heads_sum[HEADS : 2 * HEADS], heads_sum[2 * HEADS : 3 * HEADS],
    )


def shards(x_in, *rest):
    dp, seq = lax.axis_size("dp"), lax.axis_size("seq")
    if x_in.shape[0] == seq == 2 and dp % 4 == 0 and rest[1].size * dp * seq == WIDE:
        return fast_shards(x_in, *rest)
    return shards_general(x_in, *rest)


def shards_general(
    x_in,
    grad_out,
    norm_gain,
    in_weight,
    conv_weight,
    conv_bias,
    gate_gain,
    out_weight,
    dt_bias,
    a_log,
    skip,
):
    micro = x_in.shape[0]
    rate = -jnp.exp(a_log)
    devices = lax.axis_size(("dp", "seq"))
    results = []
    saves = []
    for index in range(micro):
        wts = (
            lax.all_gather(norm_gain, ("dp", "seq"), axis=0, tiled=True),
            lax.all_gather(in_weight, ("dp", "seq"), axis=0, tiled=True),
            lax.all_gather(conv_weight, ("dp", "seq"), axis=1, tiled=True),
            lax.all_gather(conv_bias, ("dp", "seq"), axis=0, tiled=True),
            lax.all_gather(gate_gain, ("dp", "seq"), axis=0, tiled=True),
            lax.all_gather(out_weight, ("dp", "seq"), axis=0, tiled=True),
        )
        result, saved = forward(x_in[index, 0], wts, dt_bias, rate, skip)
        results.append(result)
        saves.append(saved)
    dx_list = [None] * micro
    summed = None
    for index in reversed(range(micro)):
        wts = (
            lax.all_gather(norm_gain, ("dp", "seq"), axis=0, tiled=True),
            lax.all_gather(in_weight, ("dp", "seq"), axis=0, tiled=True),
            lax.all_gather(conv_weight, ("dp", "seq"), axis=1, tiled=True),
            lax.all_gather(conv_bias, ("dp", "seq"), axis=0, tiled=True),
            lax.all_gather(gate_gain, ("dp", "seq"), axis=0, tiled=True),
            lax.all_gather(out_weight, ("dp", "seq"), axis=0, tiled=True),
        )
        dx_part, terms = backward(saves[index], grad_out[index, 0], wts, dt_bias, rate, skip)
        dx_list[index] = dx_part
        summed = terms if summed is None else jax.tree.map(lambda a, b: a + b, summed, terms)
    spread = summed[:6] + (jnp.broadcast_to(summed[6], (devices, 3 * HEADS)),)
    summed = (
        lax.psum_scatter(spread[0], ("dp", "seq"), scatter_dimension=0, tiled=True),
        lax.psum_scatter(spread[1], ("dp", "seq"), scatter_dimension=0, tiled=True),
        lax.psum_scatter(spread[2], ("dp", "seq"), scatter_dimension=1, tiled=True),
        lax.psum_scatter(spread[3], ("dp", "seq"), scatter_dimension=0, tiled=True),
        lax.psum_scatter(spread[4], ("dp", "seq"), scatter_dimension=0, tiled=True),
        lax.psum_scatter(spread[5], ("dp", "seq"), scatter_dimension=0, tiled=True),
        lax.psum_scatter(spread[6], ("dp", "seq"), scatter_dimension=0, tiled=True),
    )
    heads_sum = summed[6].reshape(3, HEADS)
    y_out = jnp.stack(results)[:, None]
    dx_in = jnp.stack(dx_list)[:, None]
    return (
        y_out,
        dx_in,
        summed[0],
        summed[1],
        summed[2],
        summed[3],
        summed[4],
        summed[5],
        heads_sum[0],
        heads_sum[1],
        heads_sum[2],
    )


def solution(mesh):
    return jax.shard_map(
        shards,
        mesh=mesh,
        in_specs=(
            P(None, "dp", "seq", None),
            P(None, "dp", "seq", None),
            P(("dp", "seq")),
            P(("dp", "seq"), None),
            P(None, ("dp", "seq")),
            P(("dp", "seq")),
            P(("dp", "seq")),
            P(("dp", "seq"), None),
            P(),
            P(),
            P(),
        ),
        out_specs=(
            P(None, "dp", "seq", None),
            P(None, "dp", "seq", None),
            P(("dp", "seq")),
            P(("dp", "seq"), None),
            P(None, ("dp", "seq")),
            P(("dp", "seq")),
            P(("dp", "seq")),
            P(("dp", "seq"), None),
            P(),
            P(),
            P(),
        ),
        check_vma=False,
    )
```

```python
import jax
import jax.numpy as jnp
from jax import lax
from jax.experimental import pallas as pl
from jax.experimental.pallas import tpu as pltpu
from jax.sharding import PartitionSpec as P

HEADS = 24
HEADDIM = 64
STATE = 128
KCONV = 4
GROUP = 256
INNER = 1536
CONVW = 1792


EPS = 1e-05


def shifted(array, axis, by):
    devices = lax.axis_size(axis)
    pairs = [(i, i + by) for i in range(devices) if 0 <= i + by < devices]
    return lax.ppermute(array, axis, pairs)


def prefix(array, axis, join, neutral, backward):
    count = lax.axis_size(axis)
    place = lax.axis_index(axis)
    ahead = count - 1 - place if backward else place
    gathered = jax.tree.map(
        lambda a, kind: lax.all_gather(a.astype(kind), axis), array, (jnp.bfloat16, jnp.bfloat16)
    )
    state = jax.tree.map(lambda a, e: jnp.zeros_like(a) + jnp.asarray(e, a.dtype), array, neutral)

    def one(hop, state):
        source = count - 1 - hop if backward else hop
        return join(
            state,
            jax.tree.map(
                lambda a, own: lax.dynamic_index_in_dim(a, source, 0, False).astype(own.dtype),
                gathered,
                array,
            ),
        )

    return lax.fori_loop(0, ahead, one, state)


def tdot(left, right):
    return lax.dot_general(
        left, right, (((0,), (0,)), ((), ())), preferred_element_type=jnp.float32
    )


def ndot(left, right):
    return lax.dot_general(
        left, right, (((1,), (1,)), ((), ())), preferred_element_type=jnp.float32
    )


def dsilu(value):
    sig = jax.nn.sigmoid(value)
    return sig * (1.0 + value * (1.0 - sig))


def merge_states(earlier, later):
    return (earlier[0] * later[0], earlier[1] * later[0][:, None, None] + later[1])


def decay_table(cum_t):
    size = cum_t.shape[-1]
    rows = lax.broadcasted_iota(jnp.int32, (size, size), 0)
    cols = lax.broadcasted_iota(jnp.int32, (size, size), 1)
    lower = rows >= cols
    diff = cum_t[:, :, :, None] - cum_t[:, :, None, :]
    return jnp.exp(jnp.where(lower, diff, 0.0)) * lower.astype(jnp.float32)


def forward(xb, wts, dt_bias, rate, skip):
    gain_in, w_in, w_conv, b_conv, gain_gate, w_out = wts
    length = xb.shape[0]
    count = length // GROUP
    xf = xb.astype(jnp.float32)
    r_in = lax.rsqrt(jnp.mean(xf * xf, -1, keepdims=True) + EPS)
    normed = (xf * r_in * gain_in.astype(jnp.float32)).astype(jnp.bfloat16)
    proj = jnp.dot(normed, w_in, preferred_element_type=jnp.float32).astype(jnp.bfloat16)
    conv_in = proj[:, INNER : INNER + CONVW]
    rim = shifted(conv_in[length - KCONV + 1 :], "seq", 1)
    padded = jnp.concatenate([rim, conv_in], 0).astype(jnp.float32)
    taps = w_conv.astype(jnp.float32)
    conv_out = b_conv.astype(jnp.float32) + jnp.zeros((length, CONVW), jnp.float32)
    for tap in range(KCONV):
        conv_out = conv_out + taps[tap] * padded[tap : tap + length]
    mixed = jax.nn.silu(conv_out).astype(jnp.bfloat16)
    xh = mixed[:, :INNER].reshape(count, GROUP, HEADS, HEADDIM)
    bm = mixed[:, INNER : INNER + STATE].reshape(count, GROUP, STATE)
    cm = mixed[:, INNER + STATE :].reshape(count, GROUP, STATE)
    dt_raw = proj[:, INNER + CONVW :].astype(jnp.float32)
    step = jax.nn.softplus(dt_raw + dt_bias)
    step_t = step.reshape(count, GROUP, HEADS).transpose(0, 2, 1)
    cum_t = jnp.cumsum(step_t * rate[None, :, None], -1)
    decay = decay_table(cum_t)
    cbm = jnp.einsum("ctn,csn->cts", cm, bm, preferred_element_type=jnp.float32)
    weights = (cbm[:, None] * decay * step_t[:, :, None, :]).astype(jnp.bfloat16)
    inside = jnp.einsum("chts,cshp->cthp", weights, xh, preferred_element_type=jnp.float32)
    last = cum_t[:, :, -1]
    block_decay = jnp.exp(last)
    scale = (jnp.exp(last[:, :, None] - cum_t) * step_t).transpose(0, 2, 1)
    x_scaled = (xh.astype(jnp.float32) * scale[..., None]).astype(jnp.bfloat16)
    local = jnp.einsum("cshp,csn->chpn", x_scaled, bm, preferred_element_type=jnp.float32)
    total_decay = jnp.ones((HEADS,), jnp.float32)
    total_state = jnp.zeros((HEADS, HEADDIM, STATE), jnp.float32)
    for block in range(count):
        total_state = total_state * block_decay[block][:, None, None] + local[block]
        total_decay = total_decay * block_decay[block]
    identity = (jnp.ones((HEADS,), jnp.float32), jnp.zeros((HEADS, HEADDIM, STATE), jnp.float32))
    _, incoming = prefix((total_decay, total_state), "seq", merge_states, identity, False)
    entering = []
    running = incoming
    for block in range(count):
        entering.append(running)
        running = running * block_decay[block][:, None, None] + local[block]
    state_in = jnp.stack(entering)
    state_low = state_in.astype(jnp.bfloat16)
    exp_cum = jnp.exp(cum_t).transpose(0, 2, 1)
    carried = exp_cum[..., None] * jnp.einsum(
        "ctn,chpn->cthp", cm, state_low, preferred_element_type=jnp.float32
    )
    ssd = (inside + carried + skip[None, None, :, None] * xh.astype(jnp.float32)).reshape(
        length, INNER
    )
    zsig = jax.nn.silu(proj[:, :INNER].astype(jnp.float32))
    gated = ssd * zsig
    r_gate = lax.rsqrt(jnp.mean(gated * gated, -1, keepdims=True) + EPS)
    gnorm = (gated * r_gate * gain_gate.astype(jnp.float32)).astype(jnp.bfloat16)
    result = (xf + jnp.dot(gnorm, w_out, preferred_element_type=jnp.float32)).astype(jnp.bfloat16)
    saved = (
        xf,
        r_in,
        normed,
        proj,
        padded,
        conv_out,
        mixed,
        step_t,
        cum_t,
        state_in,
        state_low,
        carried,
        ssd,
        zsig,
        gated,
        r_gate,
        gnorm,
    )
    return (result, saved)


def backward(saved, cot, wts, dt_bias, rate, skip):
    gain_in, w_in, w_conv, b_conv, gain_gate, w_out = wts
    (
        xf,
        r_in,
        normed,
        proj,
        padded,
        conv_out,
        mixed,
        step_t,
        cum_t,
        state_in,
        state_low,
        carried,
        ssd,
        zsig,
        gated,
        r_gate,
        gnorm,
    ) = saved
    length = xf.shape[0]
    count = length // GROUP
    grad_wout = tdot(gnorm, cot)
    dgnorm = ndot(cot, w_out)
    scaled_g = gain_gate.astype(jnp.float32) * dgnorm
    grad_ggain = jnp.sum(dgnorm * gated * r_gate, 0)
    dgated = r_gate * scaled_g - gated * r_gate**3 * jnp.mean(scaled_g * gated, -1, keepdims=True)
    dssd = (dgated * zsig).astype(jnp.bfloat16)
    zpart = proj[:, :INNER].astype(jnp.float32)
    dzpart = dgated * ssd * dsilu(zpart)
    xh = mixed[:, :INNER].reshape(count, GROUP, HEADS, HEADDIM)
    bm = mixed[:, INNER : INNER + STATE].reshape(count, GROUP, STATE)
    cm = mixed[:, INNER + STATE :].reshape(count, GROUP, STATE)
    xhf = xh.astype(jnp.float32)
    dyr = dssd.reshape(count, GROUP, HEADS, HEADDIM)
    dyf = dyr.astype(jnp.float32)
    decay = decay_table(cum_t)
    cbm = jnp.einsum("ctn,csn->cts", cm, bm, preferred_element_type=jnp.float32)
    full = cbm[:, None] * decay * step_t[:, :, None, :]
    weights = full.astype(jnp.bfloat16)
    grad_skip = jnp.sum(dyf * xhf, (0, 1, 3))
    dxh = skip[None, None, :, None] * dyf
    dweights = jnp.einsum("cthp,cshp->chts", dyr, xh, preferred_element_type=jnp.float32)
    dxh = dxh + jnp.einsum("chts,cthp->cshp", weights, dyr, preferred_element_type=jnp.float32)
    dcbm = jnp.sum(dweights * decay * step_t[:, :, None, :], 1).astype(jnp.bfloat16)
    dstep = jnp.sum(dweights * cbm[:, None] * decay, 2)
    product = dweights * full
    dcum = jnp.sum(product, 3) - jnp.sum(product, 2)
    dcum = dcum + jnp.sum(dyf * carried, -1).transpose(0, 2, 1)
    exp_cum = jnp.exp(cum_t).transpose(0, 2, 1)
    dcarry = (dyf * exp_cum[..., None]).astype(jnp.bfloat16)
    dcm = jnp.einsum("cthp,chpn->ctn", dcarry, state_low, preferred_element_type=jnp.float32)
    dstate_low = jnp.einsum("cthp,ctn->chpn", dcarry, cm, preferred_element_type=jnp.float32)
    last = cum_t[:, :, -1]
    block_decay = jnp.exp(last)
    total_decay = jnp.ones((HEADS,), jnp.float32)
    running = jnp.zeros((HEADS, HEADDIM, STATE), jnp.float32)
    for block in reversed(range(count)):
        running = running * block_decay[block][:, None, None] + dstate_low[block]
        total_decay = total_decay * block_decay[block]
    identity = (jnp.ones((HEADS,), jnp.float32), jnp.zeros((HEADS, HEADDIM, STATE), jnp.float32))
    _, later = prefix((total_decay, running), "seq", merge_states, identity, True)
    leaving = [later] * count
    running = later
    for block in reversed(range(count)):
        leaving[block] = running
        running = running * block_decay[block][:, None, None] + dstate_low[block]
    grad_state = jnp.stack(leaving)
    dlast = block_decay * jnp.sum(grad_state * state_in, (2, 3))
    scale_t = jnp.exp(last[:, :, None] - cum_t) * step_t
    scale = scale_t.transpose(0, 2, 1)
    x_scaled = (xhf * scale[..., None]).astype(jnp.bfloat16)
    grad_low = grad_state.astype(jnp.bfloat16)
    dxs = jnp.einsum("csn,chpn->cshp", bm, grad_low, preferred_element_type=jnp.float32)
    dbm = jnp.einsum("cshp,chpn->csn", x_scaled, grad_low, preferred_element_type=jnp.float32)
    dxh = dxh + dxs * scale[..., None]
    dscale = jnp.sum(dxs * xhf, -1).transpose(0, 2, 1)
    dstep = dstep + dscale * jnp.exp(last[:, :, None] - cum_t)
    dlast = dlast + jnp.sum(dscale * scale_t, -1)
    dcum = dcum - dscale * scale_t
    final = (lax.broadcasted_iota(jnp.int32, (GROUP,), 0) == GROUP - 1).astype(jnp.float32)
    dcum = dcum + dlast[:, :, None] * final
    dlog = jnp.flip(jnp.cumsum(jnp.flip(dcum, -1), -1), -1)
    dstep = dstep + dlog * rate[None, :, None]
    grad_alog = jnp.sum(dlog * step_t, (0, 2)) * rate
    dcm = dcm + jnp.einsum("cts,csn->ctn", dcbm, bm, preferred_element_type=jnp.float32)
    dbm = dbm + jnp.einsum("cts,ctn->csn", dcbm, cm, preferred_element_type=jnp.float32)
    dmixed = jnp.concatenate(
        [dxh.reshape(length, INNER), dbm.reshape(length, STATE), dcm.reshape(length, STATE)], -1
    )
    dmixed = dmixed.astype(jnp.bfloat16).astype(jnp.float32)
    dconv = dmixed * dsilu(conv_out)
    grad_cbias = jnp.sum(dconv, 0)
    grad_cweight = jnp.stack(
        [jnp.sum(dconv * padded[tap : tap + length], 0) for tap in range(KCONV)]
    )
    rim_back = shifted(dconv[: KCONV - 1], "seq", -1)
    extended = jnp.concatenate([dconv, rim_back], 0)
    taps = w_conv.astype(jnp.float32)
    dconv_in = jnp.zeros((length, CONVW), jnp.float32)
    for tap in range(KCONV):
        dconv_in = dconv_in + taps[tap] * extended[KCONV - 1 - tap : KCONV - 1 - tap + length]
    dt_raw = proj[:, INNER + CONVW :].astype(jnp.float32)
    ddt_raw = dstep.transpose(0, 2, 1).reshape(length, HEADS) * jax.nn.sigmoid(dt_raw + dt_bias)
    grad_dtb = jnp.sum(ddt_raw, 0)
    dproj = jnp.concatenate([dzpart, dconv_in, ddt_raw], -1).astype(jnp.bfloat16)
    grad_win = tdot(normed, dproj)
    dnormed = ndot(dproj, w_in)
    scaled_in = gain_in.astype(jnp.float32) * dnormed
    grad_gin = jnp.sum(dnormed * xf * r_in, 0)
    dx_in = (
        r_in * scaled_in
        - xf * r_in**3 * jnp.mean(scaled_in * xf, -1, keepdims=True)
        + cot.astype(jnp.float32)
    )
    head_terms = jnp.stack([grad_dtb, grad_alog, grad_skip]).reshape(1, 3 * HEADS)
    return (
        dx_in.astype(jnp.bfloat16),
        (grad_gin, grad_win, grad_cweight, grad_cbias, grad_ggain, grad_wout, head_terms),
    )


PAIR = 2 * HEADDIM
WIDE = 768
XTAIL = 1920
LOW = -1e30


def silu_parts(value):
    sig = 0.5 * jnp.tanh(0.5 * value) + 0.5
    return (sig, value * sig)


def split_dot(value, right):
    top = value.astype(jnp.bfloat16)
    rest = (value - top.astype(jnp.float32)).astype(jnp.bfloat16)
    return jnp.dot(top, right, preferred_element_type=jnp.float32) + jnp.dot(
        rest, right, preferred_element_type=jnp.float32
    )


def exact_dot(left, value):
    total = None
    for _ in range(3):
        part = value.astype(jnp.bfloat16)
        value = value - part.astype(jnp.float32)
        term = jnp.dot(left, part, preferred_element_type=jnp.float32)
        total = term if total is None else total + term
    return total


def lower_ones(size, flipped):
    rows = lax.broadcasted_iota(jnp.int32, (size, size), 0)
    cols = lax.broadcasted_iota(jnp.int32, (size, size), 1)
    return rows <= cols if flipped else rows >= cols


def step_sizes(raw, heads_ref):
    shifted_raw = raw.astype(jnp.float32) + heads_ref[0:1, :]
    dt = jnp.maximum(shifted_raw, 0.0) + jnp.log1p(jnp.exp(-jnp.abs(shifted_raw)))
    ones = lower_ones(GROUP, False).astype(jnp.float32).astype(jnp.bfloat16)
    cum = exact_dot(ones, dt * heads_ref[1:2, :])
    return (shifted_raw, dt, cum, cum - jnp.log(dt))


def spread_lanes(table, head, rows):
    return jnp.broadcast_to(table[:, head : head + 1], (rows, PAIR))


def scan_kernel(
    xt_ref, taps_ref, heads_ref, lanes_ref,
    mixed_ref, slope_ref, state_ref, ssd_ref,
    run_ref, cin_ref, cb_ref,
):
    half = GROUP // 2

    @pl.when(pl.program_id(0) == 0)
    def _():
        run_ref[...] = jnp.zeros_like(run_ref)
        cin_ref[0:8, :] = jnp.zeros((8, CONVW), jnp.float32)

    cin_ref[8 : 8 + GROUP, :] = xt_ref[:, 0:CONVW].astype(jnp.float32)

    def conv_chunk(chunk, carry):
        at = pl.ds(pl.multiple_of(chunk * PAIR, PAIR), PAIR)
        total = taps_ref[KCONV : KCONV + 1, at] + taps_ref[0:1, at] * cin_ref[5 : 5 + GROUP, at]
        for tap in range(1, KCONV):
            total = total + taps_ref[tap : tap + 1, at] * cin_ref[5 + tap : 5 + tap + GROUP, at]
        sig, value = silu_parts(total)
        mixed_ref[:, at] = value.astype(jnp.bfloat16)
        slope_ref[:, at] = sig + value * (1.0 - sig)
        return carry

    lax.fori_loop(0, CONVW // PAIR, conv_chunk, 0)
    cin_ref[0:8, :] = cin_ref[GROUP : GROUP + 8, :]

    bm = mixed_ref[:, INNER : INNER + STATE]
    cm = mixed_ref[:, INNER + STATE : CONVW]
    bm_t = bm.astype(jnp.float32).T.astype(jnp.bfloat16)
    cb_ref[...] = ndot(cm, bm)
    _, _, cum, late = step_sizes(xt_ref[:, CONVW:], heads_ref)
    late_t = late.T
    lower = lower_ones(half, False)
    first = lax.broadcasted_iota(jnp.int32, (1, PAIR), 1) < HEADDIM
    for pair in range(HEADS // 2):
        at = slice(pair * PAIR, (pair + 1) * PAIR)
        xp = mixed_ref[:, at]
        spread = []
        inside = []
        for head in (2 * pair, 2 * pair + 1):
            here = spread_lanes(cum, head, GROUP)
            row = late_t[head : head + 1, :]
            near = jnp.exp(jnp.where(lower, here[:half] - row[:, :half], LOW))
            far = jnp.exp(here[half:] - row[:, :half])
            last = jnp.exp(jnp.where(lower, here[half:] - row[:, half:], LOW))
            near = (cb_ref[:half, :half] * near).astype(jnp.bfloat16)
            far = (cb_ref[half:, :half] * far).astype(jnp.bfloat16)
            last = (cb_ref[half:, half:] * last).astype(jnp.bfloat16)
            above = jnp.dot(near, xp[:half], preferred_element_type=jnp.float32)
            below = jnp.dot(
                jnp.concatenate([far, last], 1), xp, preferred_element_type=jnp.float32
            )
            inside.append(jnp.concatenate([above, below], 0))
            spread.append(here)
        both = jnp.where(first, spread[0], spread[1])
        end = both[GROUP - 1 : GROUP, :]
        state = run_ref[:, at]
        carried = jnp.exp(both) * jnp.dot(
            cm, state.astype(jnp.bfloat16), preferred_element_type=jnp.float32
        )
        xf = xp.astype(jnp.float32)
        ssd_ref[:, at] = (
            jnp.where(first, inside[0], inside[1]) + carried + lanes_ref[1:2, at] * xf
        )
        both_late = jnp.where(
            first, spread_lanes(late, 2 * pair, GROUP), spread_lanes(late, 2 * pair + 1, GROUP)
        )
        xw = (xf * jnp.exp(end - both_late)).astype(jnp.bfloat16)
        state_ref[:, at] = state
        run_ref[:, at] = jnp.exp(end) * state + jnp.dot(
            bm_t, xw, preferred_element_type=jnp.float32
        )


def gate_kernel(
    z_ref, ssd_ref, xh_ref, x_ref, go_ref, wout_ref, lanes_ref, seg_ref,
    y_ref, gn_ref, dz_ref, dssd_ref, delta_ref, ggain_ref,
    dgn_ref, high_ref, rest_ref,
):
    @pl.when(pl.program_id(0) == 0)
    def _():
        ggain_ref[...] = jnp.zeros_like(ggain_ref)

    dgn_ref[...] = ndot(go_ref[...], wout_ref[...])

    def gate_rows(index, total):
        rows = pl.ds(pl.multiple_of(index * 16, 16), 16)
        ssd = ssd_ref[rows, :]
        z = z_ref[rows, :].astype(jnp.float32)
        sig, value = silu_parts(z)
        gated = ssd * value
        scale = lax.rsqrt(jnp.mean(gated * gated, -1, keepdims=True) + EPS)
        unit = gated * scale
        gain = lanes_ref[0:1, :]
        gn_ref[rows, :] = (unit * gain).astype(jnp.bfloat16)
        dgn = dgn_ref[rows, :]
        total = total + dgn * unit
        scaled = gain * dgn
        mean = jnp.mean(scaled * unit, -1, keepdims=True)
        dgated = scale * (scaled - unit * mean)
        dssd = (dgated * value).astype(jnp.bfloat16)
        dssd_ref[rows, :] = dssd
        dz_ref[rows, :] = (dgated * ssd * (sig + value * (1.0 - sig))).astype(jnp.bfloat16)
        xh = xh_ref[rows, :].astype(jnp.float32)
        product = dssd.astype(jnp.float32) * (ssd - lanes_ref[1:2, :] * xh)
        top = product.astype(jnp.bfloat16)
        high_ref[rows, :] = top
        rest_ref[rows, :] = (product - top.astype(jnp.float32)).astype(jnp.bfloat16)
        return total

    total = lax.fori_loop(0, GROUP // 16, gate_rows, jnp.zeros((16, INNER), jnp.float32))
    ggain_ref[...] = ggain_ref[...] + total[0:8] + total[8:16]
    seg = seg_ref[...]
    delta_ref[...] = jnp.dot(
        high_ref[...], seg, preferred_element_type=jnp.float32
    ) + jnp.dot(rest_ref[...], seg, preferred_element_type=jnp.float32)
    y_ref[...] = (
        x_ref[...].astype(jnp.float32)
        + jnp.dot(gn_ref[...], wout_ref[...], preferred_element_type=jnp.float32)
    ).astype(jnp.bfloat16)


def backward_kernel(
    xt_ref, mixed_ref, slope_ref, dssd_ref, state_ref, delta_ref,
    taps_ref, heads_ref, lanes_ref, seg_ref,
    dxt_ref, gconv_ref, ghead_ref, gskip_ref,
    run_ref, dext_ref, cb_ref, dcb_ref, xw_ref, dcarry_ref, high_ref, rest_ref, lane_ref, low_ref,
):
    half = GROUP // 2

    @pl.when(pl.program_id(0) == 0)
    def _():
        run_ref[...] = jnp.zeros_like(run_ref)
        dext_ref[GROUP:, :] = jnp.zeros((8, CONVW), jnp.float32)
        gconv_ref[...] = jnp.zeros_like(gconv_ref)
        ghead_ref[...] = jnp.zeros_like(ghead_ref)
        gskip_ref[...] = jnp.zeros_like(gskip_ref)
        lane_ref[...] = jnp.zeros_like(lane_ref)

    bm = mixed_ref[:, INNER : INNER + STATE]
    cm = mixed_ref[:, INNER + STATE : CONVW]
    cm_t = cm.astype(jnp.float32).T.astype(jnp.bfloat16)
    cb_ref[...] = ndot(bm, cm)
    dcb_ref[...] = jnp.zeros_like(dcb_ref)
    raw, dt, cum, late = step_sizes(xt_ref[:, CONVW:], heads_ref)
    cum_t = cum.T
    upper = lower_ones(half, True)
    first = lax.broadcasted_iota(jnp.int32, (1, PAIR), 1) < HEADDIM
    masks = (first.astype(jnp.float32), 1.0 - first.astype(jnp.float32))
    for pair in range(HEADS // 2):
        at = slice(pair * PAIR, (pair + 1) * PAIR)
        xp = mixed_ref[:, at]
        dp = dssd_ref[:, at]
        xf = xp.astype(jnp.float32)
        df = dp.astype(jnp.float32)
        spread = []
        inside = []
        for place, head in enumerate((2 * pair, 2 * pair + 1)):
            here = spread_lanes(late, head, GROUP)
            row = cum_t[head : head + 1, :]
            own = (xf * masks[place]).astype(jnp.bfloat16)
            dw_top = ndot(own[:half], dp)
            dw_low = ndot(own[half:], dp[half:])
            near = jnp.exp(jnp.where(upper, row[:, :half] - here[:half], LOW))
            dcb_ref[:half, :half] += dw_top[:, :half] * near
            near = (cb_ref[:half, :half] * near).astype(jnp.bfloat16)
            far = jnp.exp(row[:, half:] - here[:half])
            dcb_ref[:half, half:] += dw_top[:, half:] * far
            far = (cb_ref[:half, half:] * far).astype(jnp.bfloat16)
            last = jnp.exp(jnp.where(upper, row[:, half:] - here[half:], LOW))
            dcb_ref[half:, half:] += dw_low * last
            last = (cb_ref[half:, half:] * last).astype(jnp.bfloat16)
            above = jnp.dot(
                jnp.concatenate([near, far], 1), dp, preferred_element_type=jnp.float32
            )
            below = jnp.dot(last, dp[half:], preferred_element_type=jnp.float32)
            inside.append(jnp.concatenate([above, below], 0))
            spread.append(here)
        both = jnp.where(
            first, spread_lanes(cum, 2 * pair, GROUP), spread_lanes(cum, 2 * pair + 1, GROUP)
        )
        end = both[GROUP - 1 : GROUP, :]
        scale = jnp.exp(end - jnp.where(first, spread[0], spread[1]))
        xw_ref[:, at] = (xf * scale).astype(jnp.bfloat16)
        dcarry = (df * jnp.exp(both)).astype(jnp.bfloat16)
        dcarry_ref[:, at] = dcarry
        grad = run_ref[:, at]
        grad_low = grad.astype(jnp.bfloat16)
        low_ref[:, at] = grad_low
        dxs = jnp.dot(bm, grad_low, preferred_element_type=jnp.float32) * scale
        inner = jnp.where(first, inside[0], inside[1]) + dxs
        gskip_ref[0:1, at] += jnp.sum(df * xf, 0, keepdims=True)
        product = xf * inner
        top = product.astype(jnp.bfloat16)
        high_ref[:, at] = top
        rest_ref[:, at] = (product - top.astype(jnp.float32)).astype(jnp.bfloat16)
        dmixed = (inner + lanes_ref[1:2, at] * df).astype(jnp.bfloat16).astype(jnp.float32)
        dext_ref[0:GROUP, at] = dmixed * slope_ref[:, at]
        decay = jnp.exp(end)
        lane_ref[0:1, at] = jnp.sum(xf * dxs, 0, keepdims=True) + decay * jnp.sum(
            grad * state_ref[:, at], 0, keepdims=True
        )
        run_ref[:, at] = decay * grad + jnp.dot(cm_t, dcarry, preferred_element_type=jnp.float32)

    dcb_t = dcb_ref[...]
    dcb = dcb_t.T.astype(jnp.bfloat16)
    dbm = ndot(xw_ref[...], low_ref[...]) + jnp.dot(
        dcb_t.astype(jnp.bfloat16), cm, preferred_element_type=jnp.float32
    )
    dcm = ndot(dcarry_ref[...], state_ref[...].astype(jnp.bfloat16)) + jnp.dot(
        dcb, bm, preferred_element_type=jnp.float32
    )
    for place, part in enumerate((dbm, dcm)):
        at = slice(INNER + place * STATE, INNER + (place + 1) * STATE)
        dext_ref[0:GROUP, at] = part.astype(jnp.bfloat16).astype(jnp.float32) * slope_ref[:, at]
    seg = seg_ref[...]
    sums = jnp.dot(high_ref[...], seg, preferred_element_type=jnp.float32) + jnp.dot(
        rest_ref[...], seg, preferred_element_type=jnp.float32
    )
    dlast = split_dot(lane_ref[...], seg)[0:1, :]
    final = lax.broadcasted_iota(jnp.int32, (GROUP, 1), 0) == GROUP - 1
    dcum = delta_ref[...] - sums + jnp.where(final, dlast, 0.0)
    ones = lower_ones(GROUP, True).astype(jnp.float32).astype(jnp.bfloat16)
    dlog = exact_dot(ones, dcum)
    rate = heads_ref[1:2, :]
    ddt = jnp.where(dt > 0.0, sums / dt, 0.0) + dlog * rate
    ddt = ddt / (1.0 + jnp.exp(-raw))
    dxt_ref[:, CONVW:] = ddt.astype(jnp.bfloat16)
    ghead_ref[0:1, :] += jnp.sum(ddt, 0, keepdims=True)
    ghead_ref[1:2, :] += jnp.sum(dlog * dt, 0, keepdims=True) * rate

    def conv_chunk(chunk, carry):
        at = pl.ds(pl.multiple_of(chunk * PAIR, PAIR), PAIR)
        given = xt_ref[:, at].astype(jnp.float32)
        total = None
        for tap in range(KCONV):
            moved = dext_ref[KCONV - 1 - tap : KCONV - 1 - tap + GROUP, at]
            term = taps_ref[tap : tap + 1, at] * moved
            total = term if total is None else total + term
            gconv_ref[tap : tap + 1, at] += jnp.sum(given * moved, 0, keepdims=True)
            if tap == KCONV - 1:
                gconv_ref[KCONV : KCONV + 1, at] += jnp.sum(moved, 0, keepdims=True)
        dxt_ref[:, at] = total.astype(jnp.bfloat16)
        return carry

    lax.fori_loop(0, CONVW // PAIR, conv_chunk, 0)
    dext_ref[GROUP:, :] = dext_ref[0:8, :]


def tall_block(width, count=None):
    if count is None:
        return pl.BlockSpec((GROUP, width), lambda i: (i, 0))
    return pl.BlockSpec((GROUP, width), lambda i: (count - 1 - i, 0))


def fixed_block(shape):
    return pl.BlockSpec(shape, lambda i: (0, 0))


def kernel_options():
    return pltpu.CompilerParams(
        dimension_semantics=("arbitrary",), vmem_limit_bytes=48 * 1024 * 1024
    )


def shape_of(rows, width, kind):
    return jax.ShapeDtypeStruct((rows, width), kind)


def run_scan(xt, taps, heads, lanes):
    length = xt.shape[0]
    count = length // GROUP
    f32, b16 = jnp.float32, jnp.bfloat16
    return pl.pallas_call(
        scan_kernel,
        grid=(count,),
        in_specs=[
            tall_block(XTAIL), fixed_block(taps.shape), fixed_block(heads.shape), fixed_block(lanes.shape),
        ],
        out_specs=[
            tall_block(CONVW), tall_block(CONVW), pl.BlockSpec((STATE, INNER), lambda i: (i, 0)),
            tall_block(INNER),
        ],
        out_shape=[
            shape_of(length, CONVW, b16), shape_of(length, CONVW, f32),
            shape_of(count * STATE, INNER, f32), shape_of(length, INNER, f32),
        ],
        scratch_shapes=[
            pltpu.VMEM((STATE, INNER), f32), pltpu.VMEM((GROUP + 8, CONVW), f32),
            pltpu.VMEM((GROUP, GROUP), f32),
        ],
        compiler_params=kernel_options(),
        cost_estimate=pl.CostEstimate(flops=25 * 10**9, bytes_accessed=30 * 10**6, transcendentals=10**7),
        name="scan_forward",
    )(xt, taps, heads, lanes)


def run_gate(z, ssd, mixed, x, go, wout, lanes, seg):
    length = x.shape[0]
    f32, b16 = jnp.float32, jnp.bfloat16
    return pl.pallas_call(
        gate_kernel,
        grid=(length // GROUP,),
        in_specs=[
            tall_block(INNER), tall_block(INNER), tall_block(INNER), tall_block(WIDE), tall_block(WIDE),
            fixed_block(wout.shape), fixed_block(lanes.shape), fixed_block(seg.shape),
        ],
        out_specs=[
            tall_block(WIDE), tall_block(INNER), tall_block(INNER), tall_block(INNER), tall_block(PAIR),
            fixed_block((8, INNER)),
        ],
        out_shape=[
            shape_of(length, WIDE, b16), shape_of(length, INNER, b16), shape_of(length, INNER, b16),
            shape_of(length, INNER, b16), shape_of(length, PAIR, f32), shape_of(8, INNER, f32),
        ],
        scratch_shapes=[
            pltpu.VMEM((GROUP, INNER), f32), pltpu.VMEM((GROUP, INNER), b16),
            pltpu.VMEM((GROUP, INNER), b16),
        ],
        compiler_params=kernel_options(),
        cost_estimate=pl.CostEstimate(flops=20 * 10**9, bytes_accessed=30 * 10**6, transcendentals=10**7),
        name="gate_both_ways",
    )(z, ssd, mixed, x, go, wout, lanes, seg)


def run_backward(xt, mixed, slope, dssd, states, delta, taps, heads, lanes, seg):
    length = xt.shape[0]
    count = length // GROUP
    f32, b16 = jnp.float32, jnp.bfloat16
    return pl.pallas_call(
        backward_kernel,
        grid=(count,),
        in_specs=[
            tall_block(XTAIL, count), tall_block(CONVW, count), tall_block(CONVW, count),
            tall_block(INNER, count), pl.BlockSpec((STATE, INNER), lambda i: (count - 1 - i, 0)),
            tall_block(PAIR, count), fixed_block(taps.shape), fixed_block(heads.shape),
            fixed_block(lanes.shape), fixed_block(seg.shape),
        ],
        out_specs=[
            tall_block(XTAIL, count), fixed_block((8, CONVW)), fixed_block((8, PAIR)),
            fixed_block((8, INNER)),
        ],
        out_shape=[
            shape_of(length, XTAIL, b16), shape_of(8, CONVW, f32), shape_of(8, PAIR, f32),
            shape_of(8, INNER, f32),
        ],
        scratch_shapes=[
            pltpu.VMEM((STATE, INNER), f32), pltpu.VMEM((GROUP + 8, CONVW), f32),
            pltpu.VMEM((GROUP, GROUP), f32), pltpu.VMEM((GROUP, GROUP), f32),
            pltpu.VMEM((GROUP, INNER), b16), pltpu.VMEM((GROUP, INNER), b16),
            pltpu.VMEM((GROUP, INNER), b16), pltpu.VMEM((GROUP, INNER), b16),
            pltpu.VMEM((8, INNER), f32), pltpu.VMEM((STATE, INNER), b16),
        ],
        compiler_params=kernel_options(),
        cost_estimate=pl.CostEstimate(flops=30 * 10**9, bytes_accessed=30 * 10**6, transcendentals=10**7),
        name="scan_backward",
    )(xt, mixed, slope, dssd, states, delta, taps, heads, lanes, seg)


def head_segments():
    rows = lax.broadcasted_iota(jnp.int32, (INNER, PAIR), 0) // HEADDIM
    cols = lax.broadcasted_iota(jnp.int32, (INNER, PAIR), 1)
    return (rows == cols).astype(jnp.bfloat16)


def head_tables(dt_bias, rate, skip):
    pad = lambda v: jnp.pad(v.astype(jnp.float32), (0, PAIR - HEADS))
    zero = jnp.zeros((PAIR,), jnp.float32)
    heads = jnp.stack([pad(dt_bias), pad(rate)] + [zero] * 6)
    return (heads, jnp.repeat(skip, HEADDIM))


def input_norm(xb, gain_in):
    xf = xb.astype(jnp.float32)
    r_in = lax.rsqrt(jnp.mean(xf * xf, -1, keepdims=True) + EPS)
    return (xf, r_in, (xf * r_in * gain_in.astype(jnp.float32)).astype(jnp.bfloat16))


def input_grad(xf, r_in, gain_in, dnormed, cot):
    scaled = gain_in.astype(jnp.float32) * dnormed
    return (
        r_in * scaled
        - xf * r_in**3 * jnp.mean(scaled * xf, -1, keepdims=True)
        + cot.astype(jnp.float32)
    ).astype(jnp.bfloat16)


def low_dot(left, right):
    return jnp.dot(left, right, preferred_element_type=jnp.float32).astype(jnp.bfloat16)


SPARE = 1816


def grid_place():
    dp = lax.axis_index("dp")
    return (dp // 4, lax.rem(dp // 2, 2), lax.rem(dp, 2), lax.axis_index("seq"))


def grid_moves(step):
    high = lax.axis_size("dp") // 4
    pairs = []
    for z in range(high):
        for y in range(2):
            for c in range(2):
                for x in range(2):
                    to = ((z + step[0]) % high, y ^ step[1], c ^ step[2], x ^ step[3])
                    pairs.append((((z * 2 + y) * 2 + c) * 2 + x, ((to[0] * 2 + to[1]) * 2 + to[2]) * 2 + to[3]))
    return pairs


def grid_send(array, step):
    return lax.ppermute(array, ("dp", "seq"), grid_moves(step))


def pick(array, axes, places):
    start = [0] * array.ndim
    size = list(array.shape)
    for axis, place in zip(axes, places):
        start[axis] = place
        size[axis] = 1
    out = lax.dynamic_slice(array, start, size)
    return out.reshape([n for axis, n in enumerate(array.shape) if axis not in axes])


def add_up(parts):
    total = parts[0].astype(jnp.float32)
    for part in parts[1:]:
        total = total + part.astype(jnp.float32)
    return total


FLIPS = ((0, 1), (1, 0), (1, 1))


def reduce_core(parts, kind=jnp.bfloat16):
    high = lax.axis_size("dp") // 4
    _, _, c, _ = grid_place()
    parts = parts.reshape((high, 2, 2, 2, -1) + parts.shape[1:])
    got = grid_send(pick(parts, (2,), (1 - c,)), (0, 0, 1, 0))
    return add_up([pick(parts, (2,), (c,)), got]).astype(kind)


def plane_parts(parts):
    _, y, _, x = grid_place()
    found = [pick(parts, (1, 2), (y, x))]
    for fy, fx in FLIPS:
        piece = pick(parts, (1, 2), (y ^ fy, x ^ fx))
        found.append(grid_send(piece, (0, fy, 0, fx)))
    return found


def line_parts(parts):
    high = lax.axis_size("dp") // 4
    z, _, _, _ = grid_place()
    found = [pick(parts, (0,), (z,))]
    for hop in range(1, high):
        piece = pick(parts, (0,), (lax.rem(z + hop, high),))
        found.append(grid_send(piece, (hop, 0, 0, 0)))
    return found


def place_in(array, axis, places, pieces):
    for place, piece in zip(places, pieces):
        array = lax.dynamic_update_slice_in_dim(array, jnp.expand_dims(piece, axis), place, axis)
    return array


def gather_line(own):
    high = lax.axis_size("dp") // 4
    z, _, _, _ = grid_place()
    places = [z] + [lax.rem(z + high - hop, high) for hop in range(1, high)]
    pieces = [own] + [grid_send(own, (hop, 0, 0, 0)) for hop in range(1, high)]
    return place_in(jnp.zeros((high,) + own.shape, own.dtype), 0, places, pieces)


def gather_plane(tall):
    return [tall] + [grid_send(tall, (0, fy, 0, fx)) for fy, fx in FLIPS]


def gather_core(pieces, cuts):
    _, y, c, x = grid_place()
    high, rows, _ = pieces[0].shape
    found = []
    for cut in cuts:
        shape = (high, 2, 2, 2, len(cut) * rows, cut[0].stop - cut[0].start)
        found.append(jnp.zeros(shape, pieces[0].dtype))
    for (fy, fx), piece in zip(((0, 0),) + FLIPS, pieces):
        other = grid_send(piece, (0, 0, 1, 0))
        for core, value in ((c, piece), (1 - c, other)):
            for k, cut in enumerate(cuts):
                for j, columns in enumerate(cut):
                    part = value[:, :, columns].reshape(high, 1, 1, 1, rows, -1)
                    start = (0, y ^ fy, core, x ^ fx, j * rows, 0)
                    found[k] = lax.dynamic_update_slice(found[k], part, start)
    return [full.reshape((-1, full.shape[-1])) for full in found]


def gather_small(own):
    high = lax.axis_size("dp") // 4
    z, y, c, x = grid_place()
    flat = own.reshape(1, -1)
    held = jnp.concatenate([flat] + [grid_send(flat, (hop, 0, 0, 0)) for hop in range(1, high)], 0)
    held = jnp.concatenate([held] + [grid_send(held, (0, fy, 0, fx)) for fy, fx in FLIPS], 0)
    held = jnp.concatenate([held, grid_send(held, (0, 0, 1, 0))], 0)
    owner = lax.broadcasted_iota(jnp.int32, (high * 8, high * 8), 0)
    slot = lax.broadcasted_iota(jnp.int32, (high * 8, high * 8), 1)
    hop, flip, core = slot % high, slot // high % 4, slot // (4 * high)
    source = ((z + high - hop) % high * 2 + (y ^ (flip // 2))) * 2 + (c ^ core)
    match = owner == source * 2 + (x ^ (flip % 2))
    order = match.astype(own.dtype)
    return jnp.dot(order, held, preferred_element_type=jnp.float32).reshape((-1,) + own.shape)


def after(value, *others):
    return lax.optimization_barrier((value,) + others)[0]


def swap_send(parts):
    place = lax.axis_index("seq")
    return grid_send(lax.dynamic_index_in_dim(parts, 1 - place, 0, False), (0, 0, 0, 1))


def swap_join(parts, got):
    place = lax.axis_index("seq")
    own = lax.dynamic_index_in_dim(parts, place, 0, False)
    return jnp.concatenate([jnp.where(place == 0, own, got), jnp.where(place == 0, got, own)], 0)


def swap_halves(parts, *guards):
    return swap_join(parts, after(swap_send(parts), *guards))


def pack_small(gain, taps, bias, gate, heads):
    lines = [taps, bias[None], gate[None], gain[None], heads[None]]
    lines = [jnp.pad(line, ((0, 0), (0, PAIR - line.shape[1]))) for line in lines]
    return jnp.concatenate(lines, 0)


def unpack_small(block, sizes):
    taps = block[..., :KCONV, : sizes[0]]
    return [taps] + [block[..., KCONV + k, :size] for k, size in enumerate(sizes[1:])]


def fast_shards(
    x_in, grad_out, norm_gain, in_weight, conv_weight, conv_bias, gate_gain, out_weight, dt_bias, a_log, skip
):
    rate = -jnp.exp(a_log)
    devices = lax.axis_size(("dp", "seq"))
    micro, _, length, _ = x_in.shape
    rows = in_weight.shape[0]
    sizes = (conv_weight.shape[1], conv_bias.size, gate_gain.size, norm_gain.size)
    first = jnp.pad(in_weight[:, INNER:], ((0, 0), (0, XTAIL - SPARE)))
    second = jnp.concatenate([in_weight[:, :INNER], out_weight[:rows], out_weight[rows:]], 1)
    small = pack_small(norm_gain, conv_weight, conv_bias, gate_gain, jnp.zeros((8,), norm_gain.dtype))

    line_first = gather_line(first)
    xb = swap_halves(x_in[:, 0])
    small = gather_small(after(small, line_first))
    plane_first = gather_plane(line_first)
    line_second = gather_line(after(second, line_first))
    (w_xt,) = gather_core(plane_first, [[slice(0, XTAIL)]])
    plane_second = gather_plane(after(line_second, *plane_first))

    taps, bias, gate, gain_in = unpack_small(small, sizes)
    gain_in = gain_in.reshape(-1)
    gate = gate.reshape(-1).astype(jnp.float32)
    taps = taps.transpose(1, 0, 2).reshape(KCONV, -1)
    taps_bias = jnp.concatenate([taps, bias.reshape(1, -1)], 0).astype(jnp.float32)
    taps_bias = jnp.pad(taps_bias, ((0, 7 - KCONV), (0, 0)))
    xf, r_in, normed = input_norm(xb, gain_in)
    heads, skip_lanes = head_tables(dt_bias, rate, skip)
    lanes = jnp.stack([gate, skip_lanes] + [jnp.zeros_like(skip_lanes)] * 6)
    seg = head_segments()
    xt = low_dot(normed, w_xt)
    mixed, slope, states, ssd = run_scan(xt, taps_bias, heads, lanes)
    cot = swap_halves(after(grad_out[:, 0], *plane_first), ssd)

    w_z, w_out = gather_core(
        plane_second,
        [[slice(0, INNER)], [slice(INNER, INNER + WIDE), slice(INNER + WIDE, 2 * INNER)]],
    )
    z = low_dot(normed, w_z)
    y, gnorm, dz, dssd, delta, ggain = run_gate(z, ssd, mixed, xb, cot, w_out, lanes, seg)
    grad_wout = tdot(gnorm, cot).astype(jnp.bfloat16).reshape(devices, 2, rows, WIDE)
    grad_wz = tdot(normed, dz).astype(jnp.bfloat16)
    early = [grad_wz] + [grad_wout[:, k].reshape(WIDE, WIDE) for k in range(2)]
    early = reduce_core(jnp.concatenate(early, 1))
    dssd = after(dssd, early)
    y_got = swap_send(y.reshape(micro, length, WIDE))
    early = plane_parts(early)
    dxt, gconv, ghead, gskip = run_backward(
        xt, mixed, slope, dssd, states, delta, taps_bias, heads, lanes, seg
    )
    dxt, y_got = lax.optimization_barrier((dxt, y_got) + tuple(early))[:2]
    y_out = swap_join(y.reshape(micro, length, WIDE), y_got).reshape(x_in.shape)
    grad_wxt = tdot(normed, dxt).astype(jnp.bfloat16)
    late = reduce_core(grad_wxt)
    head_terms = jnp.concatenate(
        [ghead[0, :HEADS], ghead[1, :HEADS], jnp.sum(gskip[0].reshape(HEADS, HEADDIM), -1)]
    )
    tiny = jax.vmap(pack_small)(
        jnp.zeros((devices, 8), jnp.float32),
        gconv[:KCONV].reshape(KCONV, devices, -1).transpose(1, 0, 2),
        gconv[KCONV].reshape(devices, -1),
        jnp.sum(ggain, 0).reshape(devices, -1),
        jnp.broadcast_to(head_terms, (devices, 3 * HEADS)),
    )[:, :, : XTAIL - SPARE]
    tiny = reduce_core(tiny.reshape(devices * (KCONV + 4), -1), jnp.float32)
    tiny = jnp.pad(tiny, ((0, 0),) * 3 + ((0, rows - KCONV - 4), (SPARE, 0)))
    late = (late.astype(jnp.float32) + tiny).astype(jnp.bfloat16)
    dnormed = ndot(after(dz, late), w_z) + ndot(after(dxt, late), w_xt)
    late = plane_parts(late)
    dx = input_grad(xf, r_in, gain_in, dnormed, cot)
    dx_got = swap_send(after(dx.reshape(micro, length, WIDE), *late))
    both = [add_up(parts).astype(jnp.bfloat16) for parts in (early, late)]
    both = line_parts(jnp.concatenate(both, -1))
    both = add_up(lax.optimization_barrier(tuple(both) + (dx_got,))[:-1])
    dx_in = swap_join(dx.reshape(micro, length, WIDE), dx_got).reshape(x_in.shape)
    early, late = both[:, : 2 * INNER], both[:, 2 * INNER :]
    own_in = jnp.concatenate([early[:, :INNER], late[:, :SPARE]], 1)
    own_out = jnp.concatenate([early[:, INNER : INNER + WIDE], early[:, INNER + WIDE :]], 0)
    own = late[:, SPARE:]
    found = unpack_small(own, sizes)
    heads_sum = own[KCONV + 3]
    weighted = jnp.sum(own_in * in_weight.astype(jnp.float32), -1)
    grad_gain = weighted / norm_gain.astype(jnp.float32)
    return (
        y_out, dx_in, grad_gain, own_in, found[0], found[1], found[2], own_out,
        heads_sum[:HEADS], heads_sum[HEADS : 2 * HEADS], heads_sum[2 * HEADS : 3 * HEADS],
    )


def shards(x_in, *rest):
    dp, seq = lax.axis_size("dp"), lax.axis_size("seq")
    if x_in.shape[0] == seq == 2 and dp % 4 == 0 and rest[1].size * dp * seq == WIDE:
        return fast_shards(x_in, *rest)
    return shards_general(x_in, *rest)


def shards_general(
    x_in,
    grad_out,
    norm_gain,
    in_weight,
    conv_weight,
    conv_bias,
    gate_gain,
    out_weight,
    dt_bias,
    a_log,
    skip,
):
    micro = x_in.shape[0]
    rate = -jnp.exp(a_log)
    devices = lax.axis_size(("dp", "seq"))
    results = []
    saves = []
    for index in range(micro):
        wts = (
            lax.all_gather(norm_gain, ("dp", "seq"), axis=0, tiled=True),
            lax.all_gather(in_weight, ("dp", "seq"), axis=0, tiled=True),
            lax.all_gather(conv_weight, ("dp", "seq"), axis=1, tiled=True),
            lax.all_gather(conv_bias, ("dp", "seq"), axis=0, tiled=True),
            lax.all_gather(gate_gain, ("dp", "seq"), axis=0, tiled=True),
            lax.all_gather(out_weight, ("dp", "seq"), axis=0, tiled=True),
        )
        result, saved = forward(x_in[index, 0], wts, dt_bias, rate, skip)
        results.append(result)
        saves.append(saved)
    dx_list = [None] * micro
    summed = None
    for index in reversed(range(micro)):
        wts = (
            lax.all_gather(norm_gain, ("dp", "seq"), axis=0, tiled=True),
            lax.all_gather(in_weight, ("dp", "seq"), axis=0, tiled=True),
            lax.all_gather(conv_weight, ("dp", "seq"), axis=1, tiled=True),
            lax.all_gather(conv_bias, ("dp", "seq"), axis=0, tiled=True),
            lax.all_gather(gate_gain, ("dp", "seq"), axis=0, tiled=True),
            lax.all_gather(out_weight, ("dp", "seq"), axis=0, tiled=True),
        )
        dx_part, terms = backward(saves[index], grad_out[index, 0], wts, dt_bias, rate, skip)
        dx_list[index] = dx_part
        summed = terms if summed is None else jax.tree.map(lambda a, b: a + b, summed, terms)
    spread = summed[:6] + (jnp.broadcast_to(summed[6], (devices, 3 * HEADS)),)
    summed = (
        lax.psum_scatter(spread[0], ("dp", "seq"), scatter_dimension=0, tiled=True),
        lax.psum_scatter(spread[1], ("dp", "seq"), scatter_dimension=0, tiled=True),
        lax.psum_scatter(spread[2], ("dp", "seq"), scatter_dimension=1, tiled=True),
        lax.psum_scatter(spread[3], ("dp", "seq"), scatter_dimension=0, tiled=True),
        lax.psum_scatter(spread[4], ("dp", "seq"), scatter_dimension=0, tiled=True),
        lax.psum_scatter(spread[5], ("dp", "seq"), scatter_dimension=0, tiled=True),
        lax.psum_scatter(spread[6], ("dp", "seq"), scatter_dimension=0, tiled=True),
    )
    heads_sum = summed[6].reshape(3, HEADS)
    y_out = jnp.stack(results)[:, None]
    dx_in = jnp.stack(dx_list)[:, None]
    return (
        y_out,
        dx_in,
        summed[0],
        summed[1],
        summed[2],
        summed[3],
        summed[4],
        summed[5],
        heads_sum[0],
        heads_sum[1],
        heads_sum[2],
    )


def solution(mesh):
    return jax.shard_map(
        shards,
        mesh=mesh,
        in_specs=(
            P(None, "dp", "seq", None),
            P(None, "dp", "seq", None),
            P(("dp", "seq")),
            P(("dp", "seq"), None),
            P(None, ("dp", "seq")),
            P(("dp", "seq")),
            P(("dp", "seq")),
            P(("dp", "seq"), None),
            P(),
            P(),
            P(),
        ),
        out_specs=(
            P(None, "dp", "seq", None),
            P(None, "dp", "seq", None),
            P(("dp", "seq")),
            P(("dp", "seq"), None),
            P(None, ("dp", "seq")),
            P(("dp", "seq")),
            P(("dp", "seq")),
            P(("dp", "seq"), None),
            P(),
            P(),
            P(),
        ),
        check_vma=False,
    )
```

```python
import functools

import jax
import jax.numpy as jnp
from jax import lax
from jax.experimental import pallas as pl
from jax.experimental.pallas import tpu as pltpu
from jax.sharding import PartitionSpec as P

HEADS = 24
HEADDIM = 64
STATE = 128
KCONV = 4
GROUP = 256
INNER = 1536
CONVW = 1792


EPS = 1e-05


def shifted(array, axis, by):
    devices = lax.axis_size(axis)
    pairs = [(i, i + by) for i in range(devices) if 0 <= i + by < devices]
    return lax.ppermute(array, axis, pairs)


def prefix(array, axis, join, neutral, backward):
    count = lax.axis_size(axis)
    place = lax.axis_index(axis)
    ahead = count - 1 - place if backward else place
    gathered = jax.tree.map(
        lambda a, kind: lax.all_gather(a.astype(kind), axis), array, (jnp.bfloat16, jnp.bfloat16)
    )
    state = jax.tree.map(lambda a, e: jnp.zeros_like(a) + jnp.asarray(e, a.dtype), array, neutral)

    def one(hop, state):
        source = count - 1 - hop if backward else hop
        return join(
            state,
            jax.tree.map(
                lambda a, own: lax.dynamic_index_in_dim(a, source, 0, False).astype(own.dtype),
                gathered,
                array,
            ),
        )

    return lax.fori_loop(0, ahead, one, state)


def tdot(left, right):
    return lax.dot_general(
        left, right, (((0,), (0,)), ((), ())), preferred_element_type=jnp.float32
    )


def ndot(left, right):
    return lax.dot_general(
        left, right, (((1,), (1,)), ((), ())), preferred_element_type=jnp.float32
    )


def dsilu(value):
    sig = jax.nn.sigmoid(value)
    return sig * (1.0 + value * (1.0 - sig))


def merge_states(earlier, later):
    return (earlier[0] * later[0], earlier[1] * later[0][:, None, None] + later[1])


def decay_table(cum_t):
    size = cum_t.shape[-1]
    rows = lax.broadcasted_iota(jnp.int32, (size, size), 0)
    cols = lax.broadcasted_iota(jnp.int32, (size, size), 1)
    lower = rows >= cols
    diff = cum_t[:, :, :, None] - cum_t[:, :, None, :]
    return jnp.exp(jnp.where(lower, diff, 0.0)) * lower.astype(jnp.float32)


def forward(xb, wts, dt_bias, rate, skip):
    gain_in, w_in, w_conv, b_conv, gain_gate, w_out = wts
    length = xb.shape[0]
    count = length // GROUP
    xf = xb.astype(jnp.float32)
    r_in = lax.rsqrt(jnp.mean(xf * xf, -1, keepdims=True) + EPS)
    normed = (xf * r_in * gain_in.astype(jnp.float32)).astype(jnp.bfloat16)
    proj = jnp.dot(normed, w_in, preferred_element_type=jnp.float32).astype(jnp.bfloat16)
    conv_in = proj[:, INNER : INNER + CONVW]
    rim = shifted(conv_in[length - KCONV + 1 :], "seq", 1)
    padded = jnp.concatenate([rim, conv_in], 0).astype(jnp.float32)
    taps = w_conv.astype(jnp.float32)
    conv_out = b_conv.astype(jnp.float32) + jnp.zeros((length, CONVW), jnp.float32)
    for tap in range(KCONV):
        conv_out = conv_out + taps[tap] * padded[tap : tap + length]
    mixed = jax.nn.silu(conv_out).astype(jnp.bfloat16)
    xh = mixed[:, :INNER].reshape(count, GROUP, HEADS, HEADDIM)
    bm = mixed[:, INNER : INNER + STATE].reshape(count, GROUP, STATE)
    cm = mixed[:, INNER + STATE :].reshape(count, GROUP, STATE)
    dt_raw = proj[:, INNER + CONVW :].astype(jnp.float32)
    step = jax.nn.softplus(dt_raw + dt_bias)
    step_t = step.reshape(count, GROUP, HEADS).transpose(0, 2, 1)
    cum_t = jnp.cumsum(step_t * rate[None, :, None], -1)
    decay = decay_table(cum_t)
    cbm = jnp.einsum("ctn,csn->cts", cm, bm, preferred_element_type=jnp.float32)
    weights = (cbm[:, None] * decay * step_t[:, :, None, :]).astype(jnp.bfloat16)
    inside = jnp.einsum("chts,cshp->cthp", weights, xh, preferred_element_type=jnp.float32)
    last = cum_t[:, :, -1]
    block_decay = jnp.exp(last)
    scale = (jnp.exp(last[:, :, None] - cum_t) * step_t).transpose(0, 2, 1)
    x_scaled = (xh.astype(jnp.float32) * scale[..., None]).astype(jnp.bfloat16)
    local = jnp.einsum("cshp,csn->chpn", x_scaled, bm, preferred_element_type=jnp.float32)
    total_decay = jnp.ones((HEADS,), jnp.float32)
    total_state = jnp.zeros((HEADS, HEADDIM, STATE), jnp.float32)
    for block in range(count):
        total_state = total_state * block_decay[block][:, None, None] + local[block]
        total_decay = total_decay * block_decay[block]
    identity = (jnp.ones((HEADS,), jnp.float32), jnp.zeros((HEADS, HEADDIM, STATE), jnp.float32))
    _, incoming = prefix((total_decay, total_state), "seq", merge_states, identity, False)
    entering = []
    running = incoming
    for block in range(count):
        entering.append(running)
        running = running * block_decay[block][:, None, None] + local[block]
    state_in = jnp.stack(entering)
    state_low = state_in.astype(jnp.bfloat16)
    exp_cum = jnp.exp(cum_t).transpose(0, 2, 1)
    carried = exp_cum[..., None] * jnp.einsum(
        "ctn,chpn->cthp", cm, state_low, preferred_element_type=jnp.float32
    )
    ssd = (inside + carried + skip[None, None, :, None] * xh.astype(jnp.float32)).reshape(
        length, INNER
    )
    zsig = jax.nn.silu(proj[:, :INNER].astype(jnp.float32))
    gated = ssd * zsig
    r_gate = lax.rsqrt(jnp.mean(gated * gated, -1, keepdims=True) + EPS)
    gnorm = (gated * r_gate * gain_gate.astype(jnp.float32)).astype(jnp.bfloat16)
    result = (xf + jnp.dot(gnorm, w_out, preferred_element_type=jnp.float32)).astype(jnp.bfloat16)
    saved = (
        xf,
        r_in,
        normed,
        proj,
        padded,
        conv_out,
        mixed,
        step_t,
        cum_t,
        state_in,
        state_low,
        carried,
        ssd,
        zsig,
        gated,
        r_gate,
        gnorm,
    )
    return (result, saved)


def backward(saved, cot, wts, dt_bias, rate, skip):
    gain_in, w_in, w_conv, b_conv, gain_gate, w_out = wts
    (
        xf,
        r_in,
        normed,
        proj,
        padded,
        conv_out,
        mixed,
        step_t,
        cum_t,
        state_in,
        state_low,
        carried,
        ssd,
        zsig,
        gated,
        r_gate,
        gnorm,
    ) = saved
    length = xf.shape[0]
    count = length // GROUP
    grad_wout = tdot(gnorm, cot)
    dgnorm = ndot(cot, w_out)
    scaled_g = gain_gate.astype(jnp.float32) * dgnorm
    grad_ggain = jnp.sum(dgnorm * gated * r_gate, 0)
    dgated = r_gate * scaled_g - gated * r_gate**3 * jnp.mean(scaled_g * gated, -1, keepdims=True)
    dssd = (dgated * zsig).astype(jnp.bfloat16)
    zpart = proj[:, :INNER].astype(jnp.float32)
    dzpart = dgated * ssd * dsilu(zpart)
    xh = mixed[:, :INNER].reshape(count, GROUP, HEADS, HEADDIM)
    bm = mixed[:, INNER : INNER + STATE].reshape(count, GROUP, STATE)
    cm = mixed[:, INNER + STATE :].reshape(count, GROUP, STATE)
    xhf = xh.astype(jnp.float32)
    dyr = dssd.reshape(count, GROUP, HEADS, HEADDIM)
    dyf = dyr.astype(jnp.float32)
    decay = decay_table(cum_t)
    cbm = jnp.einsum("ctn,csn->cts", cm, bm, preferred_element_type=jnp.float32)
    full = cbm[:, None] * decay * step_t[:, :, None, :]
    weights = full.astype(jnp.bfloat16)
    grad_skip = jnp.sum(dyf * xhf, (0, 1, 3))
    dxh = skip[None, None, :, None] * dyf
    dweights = jnp.einsum("cthp,cshp->chts", dyr, xh, preferred_element_type=jnp.float32)
    dxh = dxh + jnp.einsum("chts,cthp->cshp", weights, dyr, preferred_element_type=jnp.float32)
    dcbm = jnp.sum(dweights * decay * step_t[:, :, None, :], 1).astype(jnp.bfloat16)
    dstep = jnp.sum(dweights * cbm[:, None] * decay, 2)
    product = dweights * full
    dcum = jnp.sum(product, 3) - jnp.sum(product, 2)
    dcum = dcum + jnp.sum(dyf * carried, -1).transpose(0, 2, 1)
    exp_cum = jnp.exp(cum_t).transpose(0, 2, 1)
    dcarry = (dyf * exp_cum[..., None]).astype(jnp.bfloat16)
    dcm = jnp.einsum("cthp,chpn->ctn", dcarry, state_low, preferred_element_type=jnp.float32)
    dstate_low = jnp.einsum("cthp,ctn->chpn", dcarry, cm, preferred_element_type=jnp.float32)
    last = cum_t[:, :, -1]
    block_decay = jnp.exp(last)
    total_decay = jnp.ones((HEADS,), jnp.float32)
    running = jnp.zeros((HEADS, HEADDIM, STATE), jnp.float32)
    for block in reversed(range(count)):
        running = running * block_decay[block][:, None, None] + dstate_low[block]
        total_decay = total_decay * block_decay[block]
    identity = (jnp.ones((HEADS,), jnp.float32), jnp.zeros((HEADS, HEADDIM, STATE), jnp.float32))
    _, later = prefix((total_decay, running), "seq", merge_states, identity, True)
    leaving = [later] * count
    running = later
    for block in reversed(range(count)):
        leaving[block] = running
        running = running * block_decay[block][:, None, None] + dstate_low[block]
    grad_state = jnp.stack(leaving)
    dlast = block_decay * jnp.sum(grad_state * state_in, (2, 3))
    scale_t = jnp.exp(last[:, :, None] - cum_t) * step_t
    scale = scale_t.transpose(0, 2, 1)
    x_scaled = (xhf * scale[..., None]).astype(jnp.bfloat16)
    grad_low = grad_state.astype(jnp.bfloat16)
    dxs = jnp.einsum("csn,chpn->cshp", bm, grad_low, preferred_element_type=jnp.float32)
    dbm = jnp.einsum("cshp,chpn->csn", x_scaled, grad_low, preferred_element_type=jnp.float32)
    dxh = dxh + dxs * scale[..., None]
    dscale = jnp.sum(dxs * xhf, -1).transpose(0, 2, 1)
    dstep = dstep + dscale * jnp.exp(last[:, :, None] - cum_t)
    dlast = dlast + jnp.sum(dscale * scale_t, -1)
    dcum = dcum - dscale * scale_t
    final = (lax.broadcasted_iota(jnp.int32, (GROUP,), 0) == GROUP - 1).astype(jnp.float32)
    dcum = dcum + dlast[:, :, None] * final
    dlog = jnp.flip(jnp.cumsum(jnp.flip(dcum, -1), -1), -1)
    dstep = dstep + dlog * rate[None, :, None]
    grad_alog = jnp.sum(dlog * step_t, (0, 2)) * rate
    dcm = dcm + jnp.einsum("cts,csn->ctn", dcbm, bm, preferred_element_type=jnp.float32)
    dbm = dbm + jnp.einsum("cts,ctn->csn", dcbm, cm, preferred_element_type=jnp.float32)
    dmixed = jnp.concatenate(
        [dxh.reshape(length, INNER), dbm.reshape(length, STATE), dcm.reshape(length, STATE)], -1
    )
    dmixed = dmixed.astype(jnp.bfloat16).astype(jnp.float32)
    dconv = dmixed * dsilu(conv_out)
    grad_cbias = jnp.sum(dconv, 0)
    grad_cweight = jnp.stack(
        [jnp.sum(dconv * padded[tap : tap + length], 0) for tap in range(KCONV)]
    )
    rim_back = shifted(dconv[: KCONV - 1], "seq", -1)
    extended = jnp.concatenate([dconv, rim_back], 0)
    taps = w_conv.astype(jnp.float32)
    dconv_in = jnp.zeros((length, CONVW), jnp.float32)
    for tap in range(KCONV):
        dconv_in = dconv_in + taps[tap] * extended[KCONV - 1 - tap : KCONV - 1 - tap + length]
    dt_raw = proj[:, INNER + CONVW :].astype(jnp.float32)
    ddt_raw = dstep.transpose(0, 2, 1).reshape(length, HEADS) * jax.nn.sigmoid(dt_raw + dt_bias)
    grad_dtb = jnp.sum(ddt_raw, 0)
    dproj = jnp.concatenate([dzpart, dconv_in, ddt_raw], -1).astype(jnp.bfloat16)
    grad_win = tdot(normed, dproj)
    dnormed = ndot(dproj, w_in)
    scaled_in = gain_in.astype(jnp.float32) * dnormed
    grad_gin = jnp.sum(dnormed * xf * r_in, 0)
    dx_in = (
        r_in * scaled_in
        - xf * r_in**3 * jnp.mean(scaled_in * xf, -1, keepdims=True)
        + cot.astype(jnp.float32)
    )
    head_terms = jnp.stack([grad_dtb, grad_alog, grad_skip]).reshape(1, 3 * HEADS)
    return (
        dx_in.astype(jnp.bfloat16),
        (grad_gin, grad_win, grad_cweight, grad_cbias, grad_ggain, grad_wout, head_terms),
    )


PAIR = 2 * HEADDIM
WIDE = 768
XTAIL = 1920
STRIP = 64
LOW = -1e30


def silu_parts(value):
    sig = 0.5 * jnp.tanh(0.5 * value) + 0.5
    return (sig, value * sig)


def split_dot(value, right):
    top = value.astype(jnp.bfloat16)
    rest = (value - top.astype(jnp.float32)).astype(jnp.bfloat16)
    return jnp.dot(top, right, preferred_element_type=jnp.float32) + jnp.dot(
        rest, right, preferred_element_type=jnp.float32
    )


def exact_dot(left, value):
    total = None
    for _ in range(3):
        part = value.astype(jnp.bfloat16)
        value = value - part.astype(jnp.float32)
        term = jnp.dot(left, part, preferred_element_type=jnp.float32)
        total = term if total is None else total + term
    return total


def lower_ones(size, flipped):
    rows = lax.broadcasted_iota(jnp.int32, (size, size), 0)
    cols = lax.broadcasted_iota(jnp.int32, (size, size), 1)
    return rows <= cols if flipped else rows >= cols


def step_sizes(raw, heads_ref):
    shifted_raw = raw.astype(jnp.float32) + heads_ref[0:1, :]
    dt = jnp.maximum(shifted_raw, 0.0) + jnp.log1p(jnp.exp(-jnp.abs(shifted_raw)))
    ones = lower_ones(GROUP, False).astype(jnp.float32).astype(jnp.bfloat16)
    cum = exact_dot(ones, dt * heads_ref[1:2, :])
    return (shifted_raw, dt, cum, cum - jnp.log(dt))


def spread_lanes(table, head, rows):
    return jnp.broadcast_to(table[:, head : head + 1], (rows, PAIR))


def scan_kernel(
    xt_ref, taps_ref, heads_ref, lanes_ref,
    mixed_ref, slope_ref, state_ref, ssd_ref,
    run_ref, cin_ref, cb_ref,
):
    half = GROUP // 2

    @pl.when(pl.program_id(0) == 0)
    def _():
        run_ref[...] = jnp.zeros_like(run_ref)
        cin_ref[:, 0:8, :] = jnp.zeros((CONVW // PAIR, 8, PAIR), jnp.float32)

    def conv_chunk(chunk, carry):
        at = pl.ds(pl.multiple_of(chunk * PAIR, PAIR), PAIR)
        cin_ref[chunk, 8 : 8 + GROUP, :] = xt_ref[:, at].astype(jnp.float32)
        for row in range(0, GROUP, STRIP):
            total = taps_ref[KCONV : KCONV + 1, at]
            for tap in range(KCONV):
                total = total + taps_ref[tap : tap + 1, at] * cin_ref[chunk, 5 + tap + row : 5 + tap + row + STRIP, :]
            sig, value = silu_parts(total)
            mixed_ref[row : row + STRIP, at] = value.astype(jnp.bfloat16)
            slope_ref[row : row + STRIP, at] = sig + value * (1.0 - sig)
        cin_ref[chunk, 0:8, :] = cin_ref[chunk, GROUP : GROUP + 8, :]
        return carry

    lax.fori_loop(0, CONVW // PAIR, conv_chunk, 0)

    bm = mixed_ref[:, INNER : INNER + STATE]
    cm = mixed_ref[:, INNER + STATE : CONVW]
    bm_t = bm.astype(jnp.float32).T.astype(jnp.bfloat16)
    cb_ref[...] = ndot(cm, bm)
    _, _, cum, late = step_sizes(xt_ref[:, CONVW:], heads_ref)
    late_t = late.T
    lower = lower_ones(half, False)
    first = lax.broadcasted_iota(jnp.int32, (1, PAIR), 1) < HEADDIM
    for pair in range(HEADS // 2):
        at = slice(pair * PAIR, (pair + 1) * PAIR)
        xp = mixed_ref[:, at]
        spread = []
        inside = []
        for head in (2 * pair, 2 * pair + 1):
            here = spread_lanes(cum, head, GROUP)
            row = late_t[head : head + 1, :]
            near = jnp.exp(jnp.where(lower, here[:half] - row[:, :half], LOW))
            far = jnp.exp(here[half:] - row[:, :half])
            last = jnp.exp(jnp.where(lower, here[half:] - row[:, half:], LOW))
            near = (cb_ref[:half, :half] * near).astype(jnp.bfloat16)
            far = (cb_ref[half:, :half] * far).astype(jnp.bfloat16)
            last = (cb_ref[half:, half:] * last).astype(jnp.bfloat16)
            above = jnp.dot(near, xp[:half], preferred_element_type=jnp.float32)
            below = jnp.dot(
                jnp.concatenate([far, last], 1), xp, preferred_element_type=jnp.float32
            )
            inside.append(jnp.concatenate([above, below], 0))
            spread.append(here)
        both = jnp.where(first, spread[0], spread[1])
        end = both[GROUP - 1 : GROUP, :]
        state = run_ref[:, at]
        carried = jnp.exp(both) * jnp.dot(
            cm, state.astype(jnp.bfloat16), preferred_element_type=jnp.float32
        )
        xf = xp.astype(jnp.float32)
        ssd_ref[:, at] = (
            jnp.where(first, inside[0], inside[1]) + carried + lanes_ref[1:2, at] * xf
        )
        both_late = jnp.where(
            first, spread_lanes(late, 2 * pair, GROUP), spread_lanes(late, 2 * pair + 1, GROUP)
        )
        xw = (xf * jnp.exp(end - both_late)).astype(jnp.bfloat16)
        state_ref[:, at] = state
        run_ref[:, at] = jnp.exp(end) * state + jnp.dot(
            bm_t, xw, preferred_element_type=jnp.float32
        )


def gate_kernel(
    z_ref, ssd_ref, xh_ref, x_ref, go_ref, wout_ref, lanes_ref, seg_ref,
    y_ref, gn_ref, dz_ref, dssd_ref, delta_ref, ggain_ref,
    dgn_ref, high_ref, rest_ref,
):
    @pl.when(pl.program_id(0) == 0)
    def _():
        ggain_ref[...] = jnp.zeros_like(ggain_ref)

    dgn_ref[...] = ndot(go_ref[...], wout_ref[...])

    def gate_rows(index, carry):
        rows = pl.ds(pl.multiple_of(index * 16, 16), 16)
        kept = []
        square = jnp.zeros((16, PAIR), jnp.float32)
        cross = jnp.zeros((16, PAIR), jnp.float32)
        for chunk in range(INNER // PAIR):
            at = slice(chunk * PAIR, (chunk + 1) * PAIR)
            sig, value = silu_parts(z_ref[rows, at].astype(jnp.float32))
            gated = ssd_ref[rows, at] * value
            square = square + gated * gated
            cross = cross + lanes_ref[0:1, at] * dgn_ref[rows, at] * gated
            kept.append((sig, value, gated))
        scale = lax.rsqrt(jnp.sum(square, -1, keepdims=True) * (1.0 / INNER) + EPS)
        pull = scale * scale * scale * (jnp.sum(cross, -1, keepdims=True) * (1.0 / INNER))
        for chunk in range(INNER // PAIR):
            at = slice(chunk * PAIR, (chunk + 1) * PAIR)
            sig, value, gated = kept[chunk]
            gain = lanes_ref[0:1, at]
            ssd = ssd_ref[rows, at]
            unit = gated * scale
            gn_ref[rows, at] = (unit * gain).astype(jnp.bfloat16)
            dgn = dgn_ref[rows, at]
            term = dgn * unit
            ggain_ref[:, at] += term[0:8] + term[8:16]
            dgated = scale * (gain * dgn) - gated * pull
            dssd = (dgated * value).astype(jnp.bfloat16)
            dssd_ref[rows, at] = dssd
            dz_ref[rows, at] = (dgated * ssd * (sig + value * (1.0 - sig))).astype(jnp.bfloat16)
            xh = xh_ref[rows, at].astype(jnp.float32)
            product = dssd.astype(jnp.float32) * (ssd - lanes_ref[1:2, at] * xh)
            top = product.astype(jnp.bfloat16)
            high_ref[rows, at] = top
            rest_ref[rows, at] = (product - top.astype(jnp.float32)).astype(jnp.bfloat16)
        return carry

    lax.fori_loop(0, GROUP // 16, gate_rows, 0, unroll=4)
    seg = seg_ref[...]
    delta_ref[...] = jnp.dot(
        high_ref[...], seg, preferred_element_type=jnp.float32
    ) + jnp.dot(rest_ref[...], seg, preferred_element_type=jnp.float32)
    y_ref[...] = (
        x_ref[...].astype(jnp.float32)
        + jnp.dot(gn_ref[...], wout_ref[...], preferred_element_type=jnp.float32)
    ).astype(jnp.bfloat16)


def backward_kernel(
    xt_ref, mixed_ref, slope_ref, dssd_ref, state_ref, delta_ref,
    taps_ref, heads_ref, lanes_ref, seg_ref,
    dxt_ref, gconv_ref, ghead_ref, gskip_ref,
    run_ref, dext_ref, cb_ref, dcb_ref, xw_ref, dcarry_ref, high_ref, rest_ref, lane_ref, low_ref,
):
    half = GROUP // 2

    @pl.when(pl.program_id(0) == 0)
    def _():
        run_ref[...] = jnp.zeros_like(run_ref)
        dext_ref[:, GROUP:, :] = jnp.zeros((CONVW // PAIR, 8, PAIR), jnp.float32)
        gconv_ref[...] = jnp.zeros_like(gconv_ref)
        ghead_ref[...] = jnp.zeros_like(ghead_ref)
        gskip_ref[...] = jnp.zeros_like(gskip_ref)
        lane_ref[...] = jnp.zeros_like(lane_ref)

    bm = mixed_ref[:, INNER : INNER + STATE]
    cm = mixed_ref[:, INNER + STATE : CONVW]
    cm_t = cm.astype(jnp.float32).T.astype(jnp.bfloat16)
    cb_ref[...] = ndot(bm, cm)
    dcb_ref[...] = jnp.zeros_like(dcb_ref)
    raw, dt, cum, late = step_sizes(xt_ref[:, CONVW:], heads_ref)
    cum_t = cum.T
    upper = lower_ones(half, True)
    first = lax.broadcasted_iota(jnp.int32, (1, PAIR), 1) < HEADDIM
    masks = (first.astype(jnp.float32), 1.0 - first.astype(jnp.float32))
    for pair in range(HEADS // 2):
        at = slice(pair * PAIR, (pair + 1) * PAIR)
        xp = mixed_ref[:, at]
        dp = dssd_ref[:, at]
        xf = xp.astype(jnp.float32)
        df = dp.astype(jnp.float32)
        spread = []
        inside = []
        for place, head in enumerate((2 * pair, 2 * pair + 1)):
            here = spread_lanes(late, head, GROUP)
            row = cum_t[head : head + 1, :]
            own = (xf * masks[place]).astype(jnp.bfloat16)
            dw_top = ndot(own[:half], dp)
            dw_low = ndot(own[half:], dp[half:])
            near = jnp.exp(jnp.where(upper, row[:, :half] - here[:half], LOW))
            dcb_ref[:half, :half] += dw_top[:, :half] * near
            near = (cb_ref[:half, :half] * near).astype(jnp.bfloat16)
            far = jnp.exp(row[:, half:] - here[:half])
            dcb_ref[:half, half:] += dw_top[:, half:] * far
            far = (cb_ref[:half, half:] * far).astype(jnp.bfloat16)
            last = jnp.exp(jnp.where(upper, row[:, half:] - here[half:], LOW))
            dcb_ref[half:, half:] += dw_low * last
            last = (cb_ref[half:, half:] * last).astype(jnp.bfloat16)
            above = jnp.dot(
                jnp.concatenate([near, far], 1), dp, preferred_element_type=jnp.float32
            )
            below = jnp.dot(last, dp[half:], preferred_element_type=jnp.float32)
            inside.append(jnp.concatenate([above, below], 0))
            spread.append(here)
        both = jnp.where(
            first, spread_lanes(cum, 2 * pair, GROUP), spread_lanes(cum, 2 * pair + 1, GROUP)
        )
        end = both[GROUP - 1 : GROUP, :]
        scale = jnp.exp(end - jnp.where(first, spread[0], spread[1]))
        xw_ref[:, at] = (xf * scale).astype(jnp.bfloat16)
        dcarry = (df * jnp.exp(both)).astype(jnp.bfloat16)
        dcarry_ref[:, at] = dcarry
        grad = run_ref[:, at]
        grad_low = grad.astype(jnp.bfloat16)
        low_ref[:, at] = grad_low
        dxs = jnp.dot(bm, grad_low, preferred_element_type=jnp.float32) * scale
        inner = jnp.where(first, inside[0], inside[1]) + dxs
        gskip_ref[0:1, at] += jnp.sum(df * xf, 0, keepdims=True)
        product = xf * inner
        top = product.astype(jnp.bfloat16)
        high_ref[:, at] = top
        rest_ref[:, at] = (product - top.astype(jnp.float32)).astype(jnp.bfloat16)
        dmixed = (inner + lanes_ref[1:2, at] * df).astype(jnp.bfloat16).astype(jnp.float32)
        dext_ref[pair, 0:GROUP, :] = dmixed * slope_ref[:, at]
        decay = jnp.exp(end)
        lane_ref[0:1, at] = jnp.sum(xf * dxs, 0, keepdims=True) + decay * jnp.sum(
            grad * state_ref[:, at], 0, keepdims=True
        )
        run_ref[:, at] = decay * grad + jnp.dot(cm_t, dcarry, preferred_element_type=jnp.float32)

    dcb_t = dcb_ref[...]
    dcb = dcb_t.T.astype(jnp.bfloat16)
    dbm = ndot(xw_ref[...], low_ref[...]) + jnp.dot(
        dcb_t.astype(jnp.bfloat16), cm, preferred_element_type=jnp.float32
    )
    dcm = ndot(dcarry_ref[...], state_ref[...].astype(jnp.bfloat16)) + jnp.dot(
        dcb, bm, preferred_element_type=jnp.float32
    )
    for place, part in enumerate((dbm, dcm)):
        at = slice(INNER + place * STATE, INNER + (place + 1) * STATE)
        dext_ref[INNER // PAIR + place, 0:GROUP, :] = part.astype(jnp.bfloat16).astype(jnp.float32) * slope_ref[:, at]
    seg = seg_ref[...]
    sums = jnp.dot(high_ref[...], seg, preferred_element_type=jnp.float32) + jnp.dot(
        rest_ref[...], seg, preferred_element_type=jnp.float32
    )
    dlast = split_dot(lane_ref[...], seg)[0:1, :]
    final = lax.broadcasted_iota(jnp.int32, (GROUP, 1), 0) == GROUP - 1
    dcum = delta_ref[...] - sums + jnp.where(final, dlast, 0.0)
    ones = lower_ones(GROUP, True).astype(jnp.float32).astype(jnp.bfloat16)
    dlog = exact_dot(ones, dcum)
    rate = heads_ref[1:2, :]
    ddt = jnp.where(dt > 0.0, sums / dt, 0.0) + dlog * rate
    ddt = ddt / (1.0 + jnp.exp(-raw))
    dxt_ref[:, CONVW:] = ddt.astype(jnp.bfloat16)
    ghead_ref[0:1, :] += jnp.sum(ddt, 0, keepdims=True)
    ghead_ref[1:2, :] += jnp.sum(dlog * dt, 0, keepdims=True) * rate

    def conv_chunk(chunk, carry):
        at = pl.ds(pl.multiple_of(chunk * PAIR, PAIR), PAIR)
        sums = [jnp.zeros((8, PAIR), jnp.float32)] * (KCONV + 1)
        for row in range(0, GROUP, STRIP):
            given = xt_ref[row : row + STRIP, at].astype(jnp.float32)
            total = None
            for tap in range(KCONV):
                start = KCONV - 1 - tap + row
                moved = dext_ref[chunk, start : start + STRIP, :]
                term = taps_ref[tap : tap + 1, at] * moved
                total = term if total is None else total + term
                sums[tap] = sums[tap] + jnp.sum((given * moved).reshape(-1, 8, PAIR), 0)
                if tap == KCONV - 1:
                    sums[KCONV] = sums[KCONV] + jnp.sum(moved.reshape(-1, 8, PAIR), 0)
            dxt_ref[row : row + STRIP, at] = total.astype(jnp.bfloat16)
        for k in range(KCONV + 1):
            gconv_ref[k : k + 1, at] += jnp.sum(sums[k], 0, keepdims=True)
        return carry

    lax.fori_loop(0, CONVW // PAIR, conv_chunk, 0)
    dext_ref[:, GROUP:, :] = dext_ref[:, 0:8, :]


def tall_block(width, count=None):
    if count is None:
        return pl.BlockSpec((GROUP, width), lambda i: (i, 0))
    return pl.BlockSpec((GROUP, width), lambda i: (count - 1 - i, 0))


def fixed_block(shape):
    return pl.BlockSpec(shape, lambda i: (0, 0))


def kernel_options():
    return pltpu.CompilerParams(
        dimension_semantics=("arbitrary",), vmem_limit_bytes=48 * 1024 * 1024
    )


def shape_of(rows, width, kind):
    return jax.ShapeDtypeStruct((rows, width), kind)


def run_scan(xt, taps, heads, lanes):
    length = xt.shape[0]
    count = length // GROUP
    f32, b16 = jnp.float32, jnp.bfloat16
    return pl.pallas_call(
        scan_kernel,
        grid=(count,),
        in_specs=[
            tall_block(XTAIL), fixed_block(taps.shape), fixed_block(heads.shape), fixed_block(lanes.shape),
        ],
        out_specs=[
            tall_block(CONVW), tall_block(CONVW), pl.BlockSpec((STATE, INNER), lambda i: (i, 0)),
            tall_block(INNER),
        ],
        out_shape=[
            shape_of(length, CONVW, b16), shape_of(length, CONVW, f32),
            shape_of(count * STATE, INNER, f32), shape_of(length, INNER, f32),
        ],
        scratch_shapes=[
            pltpu.VMEM((STATE, INNER), f32), pltpu.VMEM((CONVW // PAIR, GROUP + 8, PAIR), f32),
            pltpu.VMEM((GROUP, GROUP), f32),
        ],
        compiler_params=kernel_options(),
        cost_estimate=pl.CostEstimate(flops=25 * 10**9, bytes_accessed=30 * 10**6, transcendentals=10**7),
        name="scan_forward",
    )(xt, taps, heads, lanes)


def run_gate(z, ssd, mixed, x, go, wout, lanes, seg):
    length = x.shape[0]
    f32, b16 = jnp.float32, jnp.bfloat16
    return pl.pallas_call(
        gate_kernel,
        grid=(length // GROUP,),
        in_specs=[
            tall_block(INNER), tall_block(INNER), tall_block(INNER), tall_block(WIDE), tall_block(WIDE),
            fixed_block(wout.shape), fixed_block(lanes.shape), fixed_block(seg.shape),
        ],
        out_specs=[
            tall_block(WIDE), tall_block(INNER), tall_block(INNER), tall_block(INNER), tall_block(PAIR),
            fixed_block((8, INNER)),
        ],
        out_shape=[
            shape_of(length, WIDE, b16), shape_of(length, INNER, b16), shape_of(length, INNER, b16),
            shape_of(length, INNER, b16), shape_of(length, PAIR, f32), shape_of(8, INNER, f32),
        ],
        scratch_shapes=[
            pltpu.VMEM((GROUP, INNER), f32), pltpu.VMEM((GROUP, INNER), b16),
            pltpu.VMEM((GROUP, INNER), b16),
        ],
        compiler_params=kernel_options(),
        cost_estimate=pl.CostEstimate(flops=20 * 10**9, bytes_accessed=30 * 10**6, transcendentals=10**7),
        name="gate_both_ways",
    )(z, ssd, mixed, x, go, wout, lanes, seg)


def run_backward(xt, mixed, slope, dssd, states, delta, taps, heads, lanes, seg):
    length = xt.shape[0]
    count = length // GROUP
    f32, b16 = jnp.float32, jnp.bfloat16
    return pl.pallas_call(
        backward_kernel,
        grid=(count,),
        in_specs=[
            tall_block(XTAIL, count), tall_block(CONVW, count), tall_block(CONVW, count),
            tall_block(INNER, count), pl.BlockSpec((STATE, INNER), lambda i: (count - 1 - i, 0)),
            tall_block(PAIR, count), fixed_block(taps.shape), fixed_block(heads.shape),
            fixed_block(lanes.shape), fixed_block(seg.shape),
        ],
        out_specs=[
            tall_block(XTAIL, count), fixed_block((8, CONVW)), fixed_block((8, PAIR)),
            fixed_block((8, INNER)),
        ],
        out_shape=[
            shape_of(length, XTAIL, b16), shape_of(8, CONVW, f32), shape_of(8, PAIR, f32),
            shape_of(8, INNER, f32),
        ],
        scratch_shapes=[
            pltpu.VMEM((STATE, INNER), f32), pltpu.VMEM((CONVW // PAIR, GROUP + 8, PAIR), f32),
            pltpu.VMEM((GROUP, GROUP), f32), pltpu.VMEM((GROUP, GROUP), f32),
            pltpu.VMEM((GROUP, INNER), b16), pltpu.VMEM((GROUP, INNER), b16),
            pltpu.VMEM((GROUP, INNER), b16), pltpu.VMEM((GROUP, INNER), b16),
            pltpu.VMEM((8, INNER), f32), pltpu.VMEM((STATE, INNER), b16),
        ],
        compiler_params=kernel_options(),
        cost_estimate=pl.CostEstimate(flops=30 * 10**9, bytes_accessed=30 * 10**6, transcendentals=10**7),
        name="scan_backward",
    )(xt, mixed, slope, dssd, states, delta, taps, heads, lanes, seg)


def head_segments():
    rows = lax.broadcasted_iota(jnp.int32, (INNER, PAIR), 0) // HEADDIM
    cols = lax.broadcasted_iota(jnp.int32, (INNER, PAIR), 1)
    return (rows == cols).astype(jnp.bfloat16)


def head_tables(dt_bias, rate, skip):
    pad = lambda v: jnp.pad(v.astype(jnp.float32), (0, PAIR - HEADS))
    zero = jnp.zeros((PAIR,), jnp.float32)
    heads = jnp.stack([pad(dt_bias), pad(rate)] + [zero] * 6)
    return (heads, jnp.repeat(skip, HEADDIM))


def input_norm(xb, gain_in):
    xf = xb.astype(jnp.float32)
    r_in = lax.rsqrt(jnp.mean(xf * xf, -1, keepdims=True) + EPS)
    return (xf, r_in, (xf * r_in * gain_in.astype(jnp.float32)).astype(jnp.bfloat16))


def input_grad(xf, r_in, gain_in, dnormed, cot):
    scaled = gain_in.astype(jnp.float32) * dnormed
    return (
        r_in * scaled
        - xf * r_in**3 * jnp.mean(scaled * xf, -1, keepdims=True)
        + cot.astype(jnp.float32)
    ).astype(jnp.bfloat16)


def low_dot(left, right):
    return jnp.dot(left, right, preferred_element_type=jnp.float32).astype(jnp.bfloat16)


SPARE = 1816


def grid_place():
    dp = lax.axis_index("dp")
    return (dp // 4, lax.rem(dp // 2, 2), lax.rem(dp, 2), lax.axis_index("seq"))


def grid_moves(step):
    high = lax.axis_size("dp") // 4
    pairs = []
    for z in range(high):
        for y in range(2):
            for c in range(2):
                for x in range(2):
                    to = ((z + step[0]) % high, y ^ step[1], c ^ step[2], x ^ step[3])
                    pairs.append((((z * 2 + y) * 2 + c) * 2 + x, ((to[0] * 2 + to[1]) * 2 + to[2]) * 2 + to[3]))
    return pairs


def grid_send(array, step):
    return lax.ppermute(array, ("dp", "seq"), grid_moves(step))


def pick(array, axes, places):
    start = [0] * array.ndim
    size = list(array.shape)
    for axis, place in zip(axes, places):
        start[axis] = place
        size[axis] = 1
    out = lax.dynamic_slice(array, start, size)
    return out.reshape([n for axis, n in enumerate(array.shape) if axis not in axes])


def add_up(parts):
    total = parts[0].astype(jnp.float32)
    for part in parts[1:]:
        total = total + part.astype(jnp.float32)
    return total


FLIPS = ((0, 1), (1, 0), (1, 1))


def reduce_core(grads, kind=jnp.bfloat16):
    high = lax.axis_size("dp") // 4
    _, _, c, _ = grid_place()
    grads = [grad.reshape((high, 2, 2, 2) + grad.shape[1:]) for grad in grads]
    sent = jnp.concatenate([pick(grad, (2,), (1 - c,)) for grad in grads], -1)
    kept = jnp.concatenate([pick(grad, (2,), (c,)) for grad in grads], -1)
    return add_up([kept, grid_send(sent, (0, 0, 1, 0))]).astype(kind)


def plane_parts(parts):
    _, y, _, x = grid_place()
    found = [pick(parts, (1, 2), (y, x))]
    for fy, fx in FLIPS:
        piece = pick(parts, (1, 2), (y ^ fy, x ^ fx))
        found.append(grid_send(piece, (0, fy, 0, fx)))
    return found


def line_parts(parts):
    high = lax.axis_size("dp") // 4
    z, _, _, _ = grid_place()
    found = [pick(parts, (0,), (z,))]
    for hop in range(1, high):
        piece = pick(parts, (0,), (lax.rem(z + hop, high),))
        found.append(grid_send(piece, (hop, 0, 0, 0)))
    return found


def gather_line(own):
    high = lax.axis_size("dp") // 4
    return jnp.stack([own] + [grid_send(own, (hop, 0, 0, 0)) for hop in range(1, high)])


def gather_plane(tall):
    return [tall] + [grid_send(tall, (0, fy, 0, fx)) for fy, fx in FLIPS]


def join_kernel(cuts, place_ref, *refs):
    pieces, outs = refs[:8], refs[8:]
    high = pieces[0].shape[0]
    for slot, piece in enumerate(pieces):
        fy, fx = (((0, 0),) + FLIPS)[slot // 2]
        y, c, x = place_ref[1] ^ fy, place_ref[2] ^ (slot % 2), place_ref[3] ^ fx
        for hop in range(high):
            z = lax.rem(place_ref[0] + high - hop, high)
            for out, cut in zip(outs, cuts):
                for j, (start, size) in enumerate(cut):
                    out[z, y, c, x, j] = piece[hop, :, start : start + size]


def core_pieces(pieces):
    both = []
    for piece in pieces:
        both += [piece, grid_send(piece, (0, 0, 1, 0))]
    return both


def place_now():
    return jnp.stack([jnp.asarray(p, jnp.int32) for p in grid_place()])


def join_options():
    return pltpu.CompilerParams(vmem_limit_bytes=24 * 1024 * 1024)


def gather_core(pieces, cuts):
    high, rows, _ = pieces[0].shape
    shapes = [(high, 2, 2, 2, len(cut), rows, cut[0][1]) for cut in cuts]
    outs = pl.pallas_call(
        functools.partial(join_kernel, cuts),
        in_specs=[pl.BlockSpec(memory_space=pltpu.SMEM)] + [pl.BlockSpec(memory_space=pltpu.VMEM)] * 8,
        out_specs=[pl.BlockSpec(memory_space=pltpu.VMEM)] * len(cuts),
        out_shape=[jax.ShapeDtypeStruct(shape, pieces[0].dtype) for shape in shapes],
        compiler_params=join_options(),
        name="join_rows",
    )(place_now(), *core_pieces(pieces))
    return [full.reshape((-1, full.shape[-1])) for full in outs]


def join_first_kernel(cuts, place_ref, *refs):
    spots, masks, skip_ref = refs[8:11], refs[11:14], refs[14]
    full_ref, taps_ref, lanes_ref, gain_ref, held_ref = refs[15:]
    join_kernel(cuts, place_ref, *refs[:8], full_ref)
    high = refs[0].shape[0]
    for slot, piece in enumerate(refs[:8]):
        fy, fx = (((0, 0),) + FLIPS)[slot // 2]
        y, c, x = place_ref[1] ^ fy, place_ref[2] ^ (slot % 2), place_ref[3] ^ fx
        for hop in range(high):
            z = lax.rem(place_ref[0] + high - hop, high)
            owner = ((z * 2 + y) * 2 + c) * 2 + x
            block = piece[hop, 0:16, XTAIL - PAIR : XTAIL].astype(jnp.float32)
            held_ref[owner] = block[0:8]

    def line(row, which):
        spread = jnp.dot(
            held_ref[:, row, :].astype(jnp.bfloat16), spots[which][...], preferred_element_type=jnp.float32
        )
        return jnp.sum(spread * masks[which][...], 0, keepdims=True)

    taps_ref[...] = jnp.zeros_like(taps_ref)
    for row in range(KCONV + 1):
        taps_ref[row : row + 1, :] = line(row, 0)
    lanes_ref[...] = jnp.zeros_like(lanes_ref)
    lanes_ref[0:1, :] = line(KCONV + 1, 1)
    lanes_ref[1:2, :] = skip_ref[0:1, :]
    gain_ref[...] = jnp.zeros_like(gain_ref)
    gain_ref[0:1, :] = line(KCONV + 2, 2)


def spread_tables(width, devices):
    size = width // devices
    lane = lax.broadcasted_iota(jnp.int32, (PAIR, width), 1)
    spot = lax.broadcasted_iota(jnp.int32, (PAIR, width), 0) - (SPARE - XTAIL + PAIR) == lane % size
    owner = lax.broadcasted_iota(jnp.int32, (devices, width), 0)
    mask = owner == lax.broadcasted_iota(jnp.int32, (devices, width), 1) // size
    return (spot.astype(jnp.bfloat16), mask.astype(jnp.float32))


def gather_first(pieces, skip_lanes):
    high, rows, width = pieces[0].shape
    devices = 8 * high
    tables = [spread_tables(w, devices) for w in (CONVW, INNER, WIDE)]
    f32 = jnp.float32
    full, taps, lanes, gain = pl.pallas_call(
        functools.partial(join_first_kernel, (((0, width),),)),
        in_specs=[pl.BlockSpec(memory_space=pltpu.SMEM)] + [pl.BlockSpec(memory_space=pltpu.VMEM)] * 15,
        out_specs=[pl.BlockSpec(memory_space=pltpu.VMEM)] * 4,
        out_shape=[
            jax.ShapeDtypeStruct((high, 2, 2, 2, 1, rows, width), pieces[0].dtype),
            shape_of(8, CONVW, f32), shape_of(8, INNER, f32), shape_of(8, WIDE, f32),
        ],
        scratch_shapes=[pltpu.VMEM((devices, 8, PAIR), f32)],
        compiler_params=join_options(),
        name="join_first",
    )(
        place_now(), *core_pieces(pieces), *[t[0] for t in tables], *[t[1] for t in tables],
        jnp.broadcast_to(skip_lanes[None], (8, INNER)),
    )
    return (full.reshape(-1, width), taps, lanes, gain[0])


def after(value, *others):
    return lax.optimization_barrier((value,) + others)[0]


def swap_pick(parts):
    return lax.dynamic_index_in_dim(parts, 1 - lax.axis_index("seq"), 0, False)


def swap_send(parts):
    return grid_send(swap_pick(parts), (0, 0, 0, 1))


def swap_join(parts, got):
    place = lax.axis_index("seq")
    own = lax.dynamic_index_in_dim(parts, place, 0, False)
    return jnp.concatenate([jnp.where(place == 0, own, got), jnp.where(place == 0, got, own)], 0)


def swap_halves(parts, *guards):
    return swap_join(parts, after(swap_send(parts), *guards))


def pack_small(gain, taps, bias, gate, heads):
    lines = [taps, bias[None], gate[None], gain[None], heads[None]]
    lines = [jnp.pad(line, ((0, 0), (0, PAIR - line.shape[1]))) for line in lines]
    return jnp.concatenate(lines, 0)


def unpack_small(block, sizes):
    taps = block[..., :KCONV, : sizes[0]]
    return [taps] + [block[..., KCONV + k, :size] for k, size in enumerate(sizes[1:])]


def fast_shards(
    x_in, grad_out, norm_gain, in_weight, conv_weight, conv_bias, gate_gain, out_weight, dt_bias, a_log, skip
):
    rate = -jnp.exp(a_log)
    devices = lax.axis_size(("dp", "seq"))
    micro, _, length, _ = x_in.shape
    rows = in_weight.shape[0]
    sizes = (conv_weight.shape[1], conv_bias.size, gate_gain.size, norm_gain.size)
    x_sent = swap_pick(x_in[:, 0])
    small = pack_small(norm_gain, conv_weight, conv_bias, gate_gain, jnp.zeros((8,), norm_gain.dtype))
    small = jnp.pad(small[:, : XTAIL - SPARE], ((0, rows - KCONV - 4), (0, 0)))
    first = jnp.concatenate([in_weight[:, INNER:], small], 1)
    second = jnp.concatenate([in_weight[:, :INNER], out_weight[:rows], out_weight[rows:]], 1)

    line_first = gather_line(first)
    x_got = grid_send(x_sent, (0, 0, 0, 1))
    xb = swap_join(x_in[:, 0], x_got)
    plane_first = gather_plane(line_first)
    line_second = gather_line(after(second, plane_first[2]))
    heads, skip_lanes = head_tables(dt_bias, rate, skip)
    seg = head_segments()
    w_xt, taps_bias, lanes, gain_in = gather_first(plane_first, skip_lanes)
    plane_second = gather_plane(after(line_second, *plane_first))
    xf, r_in, normed = input_norm(xb, gain_in)
    xt = low_dot(normed, w_xt)
    mixed, slope, states, ssd = run_scan(xt, taps_bias, heads, lanes)
    cot = swap_halves(after(grad_out[:, 0], *plane_first), ssd)

    plane_second = [after(piece, ssd) for piece in plane_second]
    w_z, w_out = gather_core(
        plane_second, (((0, INNER),), ((INNER, WIDE), (INNER + WIDE, WIDE)))
    )
    z = low_dot(normed, w_z)
    y, gnorm, dz, dssd, delta, ggain = run_gate(z, ssd, mixed, xb, cot, w_out, lanes, seg)
    grad_wout = tdot(gnorm, cot).astype(jnp.bfloat16).reshape(devices, 2, rows, WIDE)
    grad_wz = tdot(normed, dz).astype(jnp.bfloat16)
    early = [grad_wz] + [grad_wout[:, k] for k in range(2)]
    early = reduce_core([part.reshape(devices, rows, -1) for part in early])
    dssd = after(dssd, early)
    y_got = swap_send(y.reshape(micro, length, WIDE))
    early = plane_parts(early)
    dxt, gconv, ghead, gskip = run_backward(
        xt, mixed, slope, dssd, states, delta, taps_bias, heads, lanes, seg
    )
    dxt, y_got = lax.optimization_barrier((dxt, y_got) + tuple(early))[:2]
    y_out = swap_join(y.reshape(micro, length, WIDE), y_got).reshape(x_in.shape)
    grad_wxt = tdot(normed, dxt).astype(jnp.bfloat16)
    late = reduce_core([grad_wxt.reshape(devices, rows, -1)])
    head_terms = jnp.concatenate(
        [ghead[0, :HEADS], ghead[1, :HEADS], jnp.sum(gskip[0].reshape(HEADS, HEADDIM), -1)]
    )
    tiny = jax.vmap(pack_small)(
        jnp.zeros((devices, 8), jnp.float32),
        gconv[:KCONV].reshape(KCONV, devices, -1).transpose(1, 0, 2),
        gconv[KCONV].reshape(devices, -1),
        jnp.sum(ggain, 0).reshape(devices, -1),
        jnp.broadcast_to(head_terms, (devices, 3 * HEADS)),
    )[:, :, : XTAIL - SPARE]
    tiny = reduce_core([tiny], jnp.float32)
    tiny = jnp.pad(tiny, ((0, 0),) * 3 + ((0, rows - KCONV - 4), (SPARE, 0)))
    late = (late.astype(jnp.float32) + tiny).astype(jnp.bfloat16)
    dnormed = ndot(after(dz, late), w_z) + ndot(after(dxt, late), w_xt)
    late = plane_parts(late)
    dx = input_grad(xf, r_in, gain_in, dnormed, cot)
    dx_got = swap_send(after(dx.reshape(micro, length, WIDE), *late))
    early = add_up(line_parts(after(add_up(early).astype(jnp.bfloat16), late[2])))
    late = tuple(line_parts(add_up(late).astype(jnp.bfloat16)))
    late = add_up(lax.optimization_barrier(late + (dx_got,))[:-1])
    dx_in = swap_join(dx.reshape(micro, length, WIDE), dx_got).reshape(x_in.shape)
    own_in = jnp.concatenate([early[:, :INNER], late[:, :SPARE]], 1)
    owned = early[:, INNER:]
    own_out = jnp.concatenate([owned[:, :WIDE], owned[:, WIDE:]], 0)
    own = late[:, SPARE:]
    found = unpack_small(own, sizes)
    heads_sum = own[KCONV + 3]
    weighted = jnp.sum(own_in * in_weight.astype(jnp.float32), -1)
    grad_gain = weighted / norm_gain.astype(jnp.float32)
    return (
        y_out, dx_in, grad_gain, own_in, found[0], found[1], found[2], own_out,
        heads_sum[:HEADS], heads_sum[HEADS : 2 * HEADS], heads_sum[2 * HEADS : 3 * HEADS],
    )


def shards(x_in, *rest):
    dp, seq = lax.axis_size("dp"), lax.axis_size("seq")
    if x_in.shape[0] == seq == 2 and dp % 4 == 0 and rest[1].size * dp * seq == WIDE:
        return fast_shards(x_in, *rest)
    return shards_general(x_in, *rest)


def shards_general(
    x_in,
    grad_out,
    norm_gain,
    in_weight,
    conv_weight,
    conv_bias,
    gate_gain,
    out_weight,
    dt_bias,
    a_log,
    skip,
):
    micro = x_in.shape[0]
    rate = -jnp.exp(a_log)
    devices = lax.axis_size(("dp", "seq"))
    results = []
    saves = []
    for index in range(micro):
        wts = (
            lax.all_gather(norm_gain, ("dp", "seq"), axis=0, tiled=True),
            lax.all_gather(in_weight, ("dp", "seq"), axis=0, tiled=True),
            lax.all_gather(conv_weight, ("dp", "seq"), axis=1, tiled=True),
            lax.all_gather(conv_bias, ("dp", "seq"), axis=0, tiled=True),
            lax.all_gather(gate_gain, ("dp", "seq"), axis=0, tiled=True),
            lax.all_gather(out_weight, ("dp", "seq"), axis=0, tiled=True),
        )
        result, saved = forward(x_in[index, 0], wts, dt_bias, rate, skip)
        results.append(result)
        saves.append(saved)
    dx_list = [None] * micro
    summed = None
    for index in reversed(range(micro)):
        wts = (
            lax.all_gather(norm_gain, ("dp", "seq"), axis=0, tiled=True),
            lax.all_gather(in_weight, ("dp", "seq"), axis=0, tiled=True),
            lax.all_gather(conv_weight, ("dp", "seq"), axis=1, tiled=True),
            lax.all_gather(conv_bias, ("dp", "seq"), axis=0, tiled=True),
            lax.all_gather(gate_gain, ("dp", "seq"), axis=0, tiled=True),
            lax.all_gather(out_weight, ("dp", "seq"), axis=0, tiled=True),
        )
        dx_part, terms = backward(saves[index], grad_out[index, 0], wts, dt_bias, rate, skip)
        dx_list[index] = dx_part
        summed = terms if summed is None else jax.tree.map(lambda a, b: a + b, summed, terms)
    spread = summed[:6] + (jnp.broadcast_to(summed[6], (devices, 3 * HEADS)),)
    summed = (
        lax.psum_scatter(spread[0], ("dp", "seq"), scatter_dimension=0, tiled=True),
        lax.psum_scatter(spread[1], ("dp", "seq"), scatter_dimension=0, tiled=True),
        lax.psum_scatter(spread[2], ("dp", "seq"), scatter_dimension=1, tiled=True),
        lax.psum_scatter(spread[3], ("dp", "seq"), scatter_dimension=0, tiled=True),
        lax.psum_scatter(spread[4], ("dp", "seq"), scatter_dimension=0, tiled=True),
        lax.psum_scatter(spread[5], ("dp", "seq"), scatter_dimension=0, tiled=True),
        lax.psum_scatter(spread[6], ("dp", "seq"), scatter_dimension=0, tiled=True),
    )
    heads_sum = summed[6].reshape(3, HEADS)
    y_out = jnp.stack(results)[:, None]
    dx_in = jnp.stack(dx_list)[:, None]
    return (
        y_out,
        dx_in,
        summed[0],
        summed[1],
        summed[2],
        summed[3],
        summed[4],
        summed[5],
        heads_sum[0],
        heads_sum[1],
        heads_sum[2],
    )


def solution(mesh):
    return jax.shard_map(
        shards,
        mesh=mesh,
        in_specs=(
            P(None, "dp", "seq", None),
            P(None, "dp", "seq", None),
            P(("dp", "seq")),
            P(("dp", "seq"), None),
            P(None, ("dp", "seq")),
            P(("dp", "seq")),
            P(("dp", "seq")),
            P(("dp", "seq"), None),
            P(),
            P(),
            P(),
        ),
        out_specs=(
            P(None, "dp", "seq", None),
            P(None, "dp", "seq", None),
            P(("dp", "seq")),
            P(("dp", "seq"), None),
            P(None, ("dp", "seq")),
            P(("dp", "seq")),
            P(("dp", "seq")),
            P(("dp", "seq"), None),
            P(),
            P(),
            P(),
        ),
        check_vma=False,
    )
```

```python
import functools

import jax
import jax.numpy as jnp
from jax import lax
from jax.experimental import pallas as pl
from jax.experimental.pallas import tpu as pltpu
from jax.sharding import PartitionSpec as P

HEADS = 24
HEADDIM = 64
STATE = 128
KCONV = 4
GROUP = 256
INNER = 1536
CONVW = 1792


EPS = 1e-05


def shifted(array, axis, by):
    devices = lax.axis_size(axis)
    pairs = [(i, i + by) for i in range(devices) if 0 <= i + by < devices]
    return lax.ppermute(array, axis, pairs)


def prefix(array, axis, join, neutral, backward):
    count = lax.axis_size(axis)
    place = lax.axis_index(axis)
    ahead = count - 1 - place if backward else place
    gathered = jax.tree.map(
        lambda a, kind: lax.all_gather(a.astype(kind), axis), array, (jnp.bfloat16, jnp.bfloat16)
    )
    state = jax.tree.map(lambda a, e: jnp.zeros_like(a) + jnp.asarray(e, a.dtype), array, neutral)

    def one(hop, state):
        source = count - 1 - hop if backward else hop
        return join(
            state,
            jax.tree.map(
                lambda a, own: lax.dynamic_index_in_dim(a, source, 0, False).astype(own.dtype),
                gathered,
                array,
            ),
        )

    return lax.fori_loop(0, ahead, one, state)


def tdot(left, right):
    return lax.dot_general(
        left, right, (((0,), (0,)), ((), ())), preferred_element_type=jnp.float32
    )


def ndot(left, right):
    return lax.dot_general(
        left, right, (((1,), (1,)), ((), ())), preferred_element_type=jnp.float32
    )


def dsilu(value):
    sig = jax.nn.sigmoid(value)
    return sig * (1.0 + value * (1.0 - sig))


def merge_states(earlier, later):
    return (earlier[0] * later[0], earlier[1] * later[0][:, None, None] + later[1])


def decay_table(cum_t):
    size = cum_t.shape[-1]
    rows = lax.broadcasted_iota(jnp.int32, (size, size), 0)
    cols = lax.broadcasted_iota(jnp.int32, (size, size), 1)
    lower = rows >= cols
    diff = cum_t[:, :, :, None] - cum_t[:, :, None, :]
    return jnp.exp(jnp.where(lower, diff, 0.0)) * lower.astype(jnp.float32)


def forward(xb, wts, dt_bias, rate, skip):
    gain_in, w_in, w_conv, b_conv, gain_gate, w_out = wts
    length = xb.shape[0]
    count = length // GROUP
    xf = xb.astype(jnp.float32)
    r_in = lax.rsqrt(jnp.mean(xf * xf, -1, keepdims=True) + EPS)
    normed = (xf * r_in * gain_in.astype(jnp.float32)).astype(jnp.bfloat16)
    proj = jnp.dot(normed, w_in, preferred_element_type=jnp.float32).astype(jnp.bfloat16)
    conv_in = proj[:, INNER : INNER + CONVW]
    rim = shifted(conv_in[length - KCONV + 1 :], "seq", 1)
    padded = jnp.concatenate([rim, conv_in], 0).astype(jnp.float32)
    taps = w_conv.astype(jnp.float32)
    conv_out = b_conv.astype(jnp.float32) + jnp.zeros((length, CONVW), jnp.float32)
    for tap in range(KCONV):
        conv_out = conv_out + taps[tap] * padded[tap : tap + length]
    mixed = jax.nn.silu(conv_out).astype(jnp.bfloat16)
    xh = mixed[:, :INNER].reshape(count, GROUP, HEADS, HEADDIM)
    bm = mixed[:, INNER : INNER + STATE].reshape(count, GROUP, STATE)
    cm = mixed[:, INNER + STATE :].reshape(count, GROUP, STATE)
    dt_raw = proj[:, INNER + CONVW :].astype(jnp.float32)
    step = jax.nn.softplus(dt_raw + dt_bias)
    step_t = step.reshape(count, GROUP, HEADS).transpose(0, 2, 1)
    cum_t = jnp.cumsum(step_t * rate[None, :, None], -1)
    decay = decay_table(cum_t)
    cbm = jnp.einsum("ctn,csn->cts", cm, bm, preferred_element_type=jnp.float32)
    weights = (cbm[:, None] * decay * step_t[:, :, None, :]).astype(jnp.bfloat16)
    inside = jnp.einsum("chts,cshp->cthp", weights, xh, preferred_element_type=jnp.float32)
    last = cum_t[:, :, -1]
    block_decay = jnp.exp(last)
    scale = (jnp.exp(last[:, :, None] - cum_t) * step_t).transpose(0, 2, 1)
    x_scaled = (xh.astype(jnp.float32) * scale[..., None]).astype(jnp.bfloat16)
    local = jnp.einsum("cshp,csn->chpn", x_scaled, bm, preferred_element_type=jnp.float32)
    total_decay = jnp.ones((HEADS,), jnp.float32)
    total_state = jnp.zeros((HEADS, HEADDIM, STATE), jnp.float32)
    for block in range(count):
        total_state = total_state * block_decay[block][:, None, None] + local[block]
        total_decay = total_decay * block_decay[block]
    identity = (jnp.ones((HEADS,), jnp.float32), jnp.zeros((HEADS, HEADDIM, STATE), jnp.float32))
    _, incoming = prefix((total_decay, total_state), "seq", merge_states, identity, False)
    entering = []
    running = incoming
    for block in range(count):
        entering.append(running)
        running = running * block_decay[block][:, None, None] + local[block]
    state_in = jnp.stack(entering)
    state_low = state_in.astype(jnp.bfloat16)
    exp_cum = jnp.exp(cum_t).transpose(0, 2, 1)
    carried = exp_cum[..., None] * jnp.einsum(
        "ctn,chpn->cthp", cm, state_low, preferred_element_type=jnp.float32
    )
    ssd = (inside + carried + skip[None, None, :, None] * xh.astype(jnp.float32)).reshape(
        length, INNER
    )
    zsig = jax.nn.silu(proj[:, :INNER].astype(jnp.float32))
    gated = ssd * zsig
    r_gate = lax.rsqrt(jnp.mean(gated * gated, -1, keepdims=True) + EPS)
    gnorm = (gated * r_gate * gain_gate.astype(jnp.float32)).astype(jnp.bfloat16)
    result = (xf + jnp.dot(gnorm, w_out, preferred_element_type=jnp.float32)).astype(jnp.bfloat16)
    saved = (
        xf,
        r_in,
        normed,
        proj,
        padded,
        conv_out,
        mixed,
        step_t,
        cum_t,
        state_in,
        state_low,
        carried,
        ssd,
        zsig,
        gated,
        r_gate,
        gnorm,
    )
    return (result, saved)


def backward(saved, cot, wts, dt_bias, rate, skip):
    gain_in, w_in, w_conv, b_conv, gain_gate, w_out = wts
    (
        xf,
        r_in,
        normed,
        proj,
        padded,
        conv_out,
        mixed,
        step_t,
        cum_t,
        state_in,
        state_low,
        carried,
        ssd,
        zsig,
        gated,
        r_gate,
        gnorm,
    ) = saved
    length = xf.shape[0]
    count = length // GROUP
    grad_wout = tdot(gnorm, cot)
    dgnorm = ndot(cot, w_out)
    scaled_g = gain_gate.astype(jnp.float32) * dgnorm
    grad_ggain = jnp.sum(dgnorm * gated * r_gate, 0)
    dgated = r_gate * scaled_g - gated * r_gate**3 * jnp.mean(scaled_g * gated, -1, keepdims=True)
    dssd = (dgated * zsig).astype(jnp.bfloat16)
    zpart = proj[:, :INNER].astype(jnp.float32)
    dzpart = dgated * ssd * dsilu(zpart)
    xh = mixed[:, :INNER].reshape(count, GROUP, HEADS, HEADDIM)
    bm = mixed[:, INNER : INNER + STATE].reshape(count, GROUP, STATE)
    cm = mixed[:, INNER + STATE :].reshape(count, GROUP, STATE)
    xhf = xh.astype(jnp.float32)
    dyr = dssd.reshape(count, GROUP, HEADS, HEADDIM)
    dyf = dyr.astype(jnp.float32)
    decay = decay_table(cum_t)
    cbm = jnp.einsum("ctn,csn->cts", cm, bm, preferred_element_type=jnp.float32)
    full = cbm[:, None] * decay * step_t[:, :, None, :]
    weights = full.astype(jnp.bfloat16)
    grad_skip = jnp.sum(dyf * xhf, (0, 1, 3))
    dxh = skip[None, None, :, None] * dyf
    dweights = jnp.einsum("cthp,cshp->chts", dyr, xh, preferred_element_type=jnp.float32)
    dxh = dxh + jnp.einsum("chts,cthp->cshp", weights, dyr, preferred_element_type=jnp.float32)
    dcbm = jnp.sum(dweights * decay * step_t[:, :, None, :], 1).astype(jnp.bfloat16)
    dstep = jnp.sum(dweights * cbm[:, None] * decay, 2)
    product = dweights * full
    dcum = jnp.sum(product, 3) - jnp.sum(product, 2)
    dcum = dcum + jnp.sum(dyf * carried, -1).transpose(0, 2, 1)
    exp_cum = jnp.exp(cum_t).transpose(0, 2, 1)
    dcarry = (dyf * exp_cum[..., None]).astype(jnp.bfloat16)
    dcm = jnp.einsum("cthp,chpn->ctn", dcarry, state_low, preferred_element_type=jnp.float32)
    dstate_low = jnp.einsum("cthp,ctn->chpn", dcarry, cm, preferred_element_type=jnp.float32)
    last = cum_t[:, :, -1]
    block_decay = jnp.exp(last)
    total_decay = jnp.ones((HEADS,), jnp.float32)
    running = jnp.zeros((HEADS, HEADDIM, STATE), jnp.float32)
    for block in reversed(range(count)):
        running = running * block_decay[block][:, None, None] + dstate_low[block]
        total_decay = total_decay * block_decay[block]
    identity = (jnp.ones((HEADS,), jnp.float32), jnp.zeros((HEADS, HEADDIM, STATE), jnp.float32))
    _, later = prefix((total_decay, running), "seq", merge_states, identity, True)
    leaving = [later] * count
    running = later
    for block in reversed(range(count)):
        leaving[block] = running
        running = running * block_decay[block][:, None, None] + dstate_low[block]
    grad_state = jnp.stack(leaving)
    dlast = block_decay * jnp.sum(grad_state * state_in, (2, 3))
    scale_t = jnp.exp(last[:, :, None] - cum_t) * step_t
    scale = scale_t.transpose(0, 2, 1)
    x_scaled = (xhf * scale[..., None]).astype(jnp.bfloat16)
    grad_low = grad_state.astype(jnp.bfloat16)
    dxs = jnp.einsum("csn,chpn->cshp", bm, grad_low, preferred_element_type=jnp.float32)
    dbm = jnp.einsum("cshp,chpn->csn", x_scaled, grad_low, preferred_element_type=jnp.float32)
    dxh = dxh + dxs * scale[..., None]
    dscale = jnp.sum(dxs * xhf, -1).transpose(0, 2, 1)
    dstep = dstep + dscale * jnp.exp(last[:, :, None] - cum_t)
    dlast = dlast + jnp.sum(dscale * scale_t, -1)
    dcum = dcum - dscale * scale_t
    final = (lax.broadcasted_iota(jnp.int32, (GROUP,), 0) == GROUP - 1).astype(jnp.float32)
    dcum = dcum + dlast[:, :, None] * final
    dlog = jnp.flip(jnp.cumsum(jnp.flip(dcum, -1), -1), -1)
    dstep = dstep + dlog * rate[None, :, None]
    grad_alog = jnp.sum(dlog * step_t, (0, 2)) * rate
    dcm = dcm + jnp.einsum("cts,csn->ctn", dcbm, bm, preferred_element_type=jnp.float32)
    dbm = dbm + jnp.einsum("cts,ctn->csn", dcbm, cm, preferred_element_type=jnp.float32)
    dmixed = jnp.concatenate(
        [dxh.reshape(length, INNER), dbm.reshape(length, STATE), dcm.reshape(length, STATE)], -1
    )
    dmixed = dmixed.astype(jnp.bfloat16).astype(jnp.float32)
    dconv = dmixed * dsilu(conv_out)
    grad_cbias = jnp.sum(dconv, 0)
    grad_cweight = jnp.stack(
        [jnp.sum(dconv * padded[tap : tap + length], 0) for tap in range(KCONV)]
    )
    rim_back = shifted(dconv[: KCONV - 1], "seq", -1)
    extended = jnp.concatenate([dconv, rim_back], 0)
    taps = w_conv.astype(jnp.float32)
    dconv_in = jnp.zeros((length, CONVW), jnp.float32)
    for tap in range(KCONV):
        dconv_in = dconv_in + taps[tap] * extended[KCONV - 1 - tap : KCONV - 1 - tap + length]
    dt_raw = proj[:, INNER + CONVW :].astype(jnp.float32)
    ddt_raw = dstep.transpose(0, 2, 1).reshape(length, HEADS) * jax.nn.sigmoid(dt_raw + dt_bias)
    grad_dtb = jnp.sum(ddt_raw, 0)
    dproj = jnp.concatenate([dzpart, dconv_in, ddt_raw], -1).astype(jnp.bfloat16)
    grad_win = tdot(normed, dproj)
    dnormed = ndot(dproj, w_in)
    scaled_in = gain_in.astype(jnp.float32) * dnormed
    grad_gin = jnp.sum(dnormed * xf * r_in, 0)
    dx_in = (
        r_in * scaled_in
        - xf * r_in**3 * jnp.mean(scaled_in * xf, -1, keepdims=True)
        + cot.astype(jnp.float32)
    )
    head_terms = jnp.stack([grad_dtb, grad_alog, grad_skip]).reshape(1, 3 * HEADS)
    return (
        dx_in.astype(jnp.bfloat16),
        (grad_gin, grad_win, grad_cweight, grad_cbias, grad_ggain, grad_wout, head_terms),
    )


PAIR = 2 * HEADDIM
WIDE = 768
XTAIL = 1920
STRIP = 64
LOW = -1e30


def silu_parts(value):
    sig = 0.5 * jnp.tanh(0.5 * value) + 0.5
    return (sig, value * sig)


def split_dot(value, right):
    top = value.astype(jnp.bfloat16)
    rest = (value - top.astype(jnp.float32)).astype(jnp.bfloat16)
    return jnp.dot(top, right, preferred_element_type=jnp.float32) + jnp.dot(
        rest, right, preferred_element_type=jnp.float32
    )


def exact_dot(left, value):
    total = None
    for _ in range(3):
        part = value.astype(jnp.bfloat16)
        value = value - part.astype(jnp.float32)
        term = jnp.dot(left, part, preferred_element_type=jnp.float32)
        total = term if total is None else total + term
    return total


def lower_ones(size, flipped):
    rows = lax.broadcasted_iota(jnp.int32, (size, size), 0)
    cols = lax.broadcasted_iota(jnp.int32, (size, size), 1)
    return rows <= cols if flipped else rows >= cols


def step_sizes(raw, heads_ref):
    shifted_raw = raw.astype(jnp.float32) + heads_ref[0:1, :]
    dt = jnp.maximum(shifted_raw, 0.0) + jnp.log1p(jnp.exp(-jnp.abs(shifted_raw)))
    ones = lower_ones(GROUP, False).astype(jnp.float32).astype(jnp.bfloat16)
    cum = exact_dot(ones, dt * heads_ref[1:2, :])
    return (shifted_raw, dt, cum, cum - jnp.log(dt))


def spread_pair(table, pair, first):
    rows = table.shape[0]
    return jnp.where(first, spread_lanes(table, 2 * pair, rows), spread_lanes(table, 2 * pair + 1, rows))


def spread_lanes(table, head, rows):
    return jnp.broadcast_to(table[:, head : head + 1], (rows, PAIR))


def scan_kernel(
    xt_ref, taps_ref, heads_ref, lanes_ref,
    mixed_ref, slope_ref, state_ref, ssd_ref,
    run_ref, cin_ref, cb_ref,
):
    half = GROUP // 2

    @pl.when(pl.program_id(0) == 0)
    def _():
        run_ref[...] = jnp.zeros_like(run_ref)
        cin_ref[:, 0:8, :] = jnp.zeros((CONVW // PAIR, 8, PAIR), jnp.float32)

    def conv_chunk(chunk, carry):
        at = pl.ds(pl.multiple_of(chunk * PAIR, PAIR), PAIR)
        cin_ref[chunk, 8 : 8 + GROUP, :] = xt_ref[:, at].astype(jnp.float32)
        for row in range(0, GROUP, STRIP):
            total = taps_ref[KCONV : KCONV + 1, at]
            for tap in range(KCONV):
                total = total + taps_ref[tap : tap + 1, at] * cin_ref[chunk, 5 + tap + row : 5 + tap + row + STRIP, :]
            sig, value = silu_parts(total)
            mixed_ref[row : row + STRIP, at] = value.astype(jnp.bfloat16)
            slope_ref[row : row + STRIP, at] = sig + value * (1.0 - sig)
        cin_ref[chunk, 0:8, :] = cin_ref[chunk, GROUP : GROUP + 8, :]
        return carry

    lax.fori_loop(0, CONVW // PAIR, conv_chunk, 0)

    bm = mixed_ref[:, INNER : INNER + STATE]
    cm = mixed_ref[:, INNER + STATE : CONVW]
    bm_t = bm.astype(jnp.float32).T.astype(jnp.bfloat16)
    cb_ref[...] = ndot(cm, bm)
    _, _, cum, late = step_sizes(xt_ref[:, CONVW:], heads_ref)
    late_t = late.T
    scale = jnp.exp(cum[GROUP - 1 : GROUP, :] - late)
    lower = lower_ones(half, False)
    first = lax.broadcasted_iota(jnp.int32, (1, PAIR), 1) < HEADDIM
    for pair in range(HEADS // 2):
        at = slice(pair * PAIR, (pair + 1) * PAIR)
        xp = mixed_ref[:, at]
        spread = []
        inside = []
        for head in (2 * pair, 2 * pair + 1):
            here = spread_lanes(cum, head, GROUP)
            row = late_t[head : head + 1, :]
            near = jnp.exp(jnp.where(lower, here[:half] - row[:, :half], LOW))
            far = jnp.exp(here[half:] - row[:, :half])
            last = jnp.exp(jnp.where(lower, here[half:] - row[:, half:], LOW))
            near = (cb_ref[:half, :half] * near).astype(jnp.bfloat16)
            far = (cb_ref[half:, :half] * far).astype(jnp.bfloat16)
            last = (cb_ref[half:, half:] * last).astype(jnp.bfloat16)
            above = jnp.dot(near, xp[:half], preferred_element_type=jnp.float32)
            below = jnp.dot(
                jnp.concatenate([far, last], 1), xp, preferred_element_type=jnp.float32
            )
            inside.append(jnp.concatenate([above, below], 0))
            spread.append(here)
        both = jnp.exp(jnp.where(first, spread[0], spread[1]))
        decay = both[GROUP - 1 : GROUP, :]
        state = run_ref[:, at]
        carried = both * jnp.dot(
            cm, state.astype(jnp.bfloat16), preferred_element_type=jnp.float32
        )
        xf = xp.astype(jnp.float32)
        ssd_ref[:, at] = (
            jnp.where(first, inside[0], inside[1]) + carried + lanes_ref[1:2, at] * xf
        )
        xw = (xf * spread_pair(scale, pair, first)).astype(jnp.bfloat16)
        state_ref[:, at] = state
        run_ref[:, at] = decay * state + jnp.dot(
            bm_t, xw, preferred_element_type=jnp.float32
        )


def gate_kernel(
    z_ref, ssd_ref, xh_ref, x_ref, go_ref, wout_ref, lanes_ref, seg_ref,
    y_ref, gn_ref, dz_ref, dssd_ref, delta_ref, ggain_ref,
    dgn_ref, high_ref, rest_ref,
):
    @pl.when(pl.program_id(0) == 0)
    def _():
        ggain_ref[...] = jnp.zeros_like(ggain_ref)

    dgn_ref[...] = ndot(go_ref[...], wout_ref[...])

    def gate_rows(index, carry):
        rows = pl.ds(pl.multiple_of(index * 16, 16), 16)
        kept = []
        square = jnp.zeros((16, PAIR), jnp.float32)
        cross = jnp.zeros((16, PAIR), jnp.float32)
        for chunk in range(INNER // PAIR):
            at = slice(chunk * PAIR, (chunk + 1) * PAIR)
            sig, value = silu_parts(z_ref[rows, at].astype(jnp.float32))
            gated = ssd_ref[rows, at] * value
            square = square + gated * gated
            cross = cross + lanes_ref[0:1, at] * dgn_ref[rows, at] * gated
            kept.append((sig, value, gated))
        scale = lax.rsqrt(jnp.sum(square, -1, keepdims=True) * (1.0 / INNER) + EPS)
        pull = scale * scale * scale * (jnp.sum(cross, -1, keepdims=True) * (1.0 / INNER))
        for chunk in range(INNER // PAIR):
            at = slice(chunk * PAIR, (chunk + 1) * PAIR)
            sig, value, gated = kept[chunk]
            gain = lanes_ref[0:1, at]
            ssd = ssd_ref[rows, at]
            unit = gated * scale
            gn_ref[rows, at] = (unit * gain).astype(jnp.bfloat16)
            dgn = dgn_ref[rows, at]
            term = dgn * unit
            ggain_ref[:, at] += term[0:8] + term[8:16]
            dgated = scale * (gain * dgn) - gated * pull
            dssd = (dgated * value).astype(jnp.bfloat16)
            dssd_ref[rows, at] = dssd
            dz_ref[rows, at] = (dgated * ssd * (sig + value * (1.0 - sig))).astype(jnp.bfloat16)
            xh = xh_ref[rows, at].astype(jnp.float32)
            product = dssd.astype(jnp.float32) * (ssd - lanes_ref[1:2, at] * xh)
            top = product.astype(jnp.bfloat16)
            high_ref[rows, at] = top
            rest_ref[rows, at] = (product - top.astype(jnp.float32)).astype(jnp.bfloat16)
        return carry

    lax.fori_loop(0, GROUP // 16, gate_rows, 0, unroll=4)
    seg = seg_ref[...]
    delta_ref[...] = jnp.dot(
        high_ref[...], seg, preferred_element_type=jnp.float32
    ) + jnp.dot(rest_ref[...], seg, preferred_element_type=jnp.float32)
    y_ref[...] = (
        x_ref[...].astype(jnp.float32)
        + jnp.dot(gn_ref[...], wout_ref[...], preferred_element_type=jnp.float32)
    ).astype(jnp.bfloat16)


def backward_kernel(
    xt_ref, mixed_ref, slope_ref, dssd_ref, state_ref, delta_ref,
    taps_ref, heads_ref, lanes_ref, seg_ref,
    dxt_ref, gconv_ref, ghead_ref, gskip_ref,
    run_ref, dext_ref, cb_ref, dcb_ref, xw_ref, dcarry_ref, high_ref, rest_ref, lane_ref, low_ref,
):
    half = GROUP // 2

    @pl.when(pl.program_id(0) == 0)
    def _():
        run_ref[...] = jnp.zeros_like(run_ref)
        dext_ref[:, GROUP:, :] = jnp.zeros((CONVW // PAIR, 8, PAIR), jnp.float32)
        gconv_ref[...] = jnp.zeros_like(gconv_ref)
        ghead_ref[...] = jnp.zeros_like(ghead_ref)
        gskip_ref[...] = jnp.zeros_like(gskip_ref)
        lane_ref[...] = jnp.zeros_like(lane_ref)

    bm = mixed_ref[:, INNER : INNER + STATE]
    cm = mixed_ref[:, INNER + STATE : CONVW]
    cm_t = cm.astype(jnp.float32).T.astype(jnp.bfloat16)
    cb_ref[...] = ndot(bm, cm)
    dcb_ref[...] = jnp.zeros_like(dcb_ref)
    raw, dt, cum, late = step_sizes(xt_ref[:, CONVW:], heads_ref)
    cum_t = cum.T
    exp_cum = jnp.exp(cum)
    late_scale = jnp.exp(cum[GROUP - 1 : GROUP, :] - late)
    upper = lower_ones(half, True)
    first = lax.broadcasted_iota(jnp.int32, (1, PAIR), 1) < HEADDIM
    masks = (first.astype(jnp.float32), 1.0 - first.astype(jnp.float32))
    for pair in range(HEADS // 2):
        at = slice(pair * PAIR, (pair + 1) * PAIR)
        xp = mixed_ref[:, at]
        dp = dssd_ref[:, at]
        xf = xp.astype(jnp.float32)
        df = dp.astype(jnp.float32)
        inside = []
        for place, head in enumerate((2 * pair, 2 * pair + 1)):
            here = spread_lanes(late, head, GROUP)
            row = cum_t[head : head + 1, :]
            own = (xf * masks[place]).astype(jnp.bfloat16)
            dw_top = ndot(own[:half], dp)
            dw_low = ndot(own[half:], dp[half:])
            near = jnp.exp(jnp.where(upper, row[:, :half] - here[:half], LOW))
            dcb_ref[:half, :half] += dw_top[:, :half] * near
            near = (cb_ref[:half, :half] * near).astype(jnp.bfloat16)
            far = jnp.exp(row[:, half:] - here[:half])
            dcb_ref[:half, half:] += dw_top[:, half:] * far
            far = (cb_ref[:half, half:] * far).astype(jnp.bfloat16)
            last = jnp.exp(jnp.where(upper, row[:, half:] - here[half:], LOW))
            dcb_ref[half:, half:] += dw_low * last
            last = (cb_ref[half:, half:] * last).astype(jnp.bfloat16)
            above = jnp.dot(
                jnp.concatenate([near, far], 1), dp, preferred_element_type=jnp.float32
            )
            below = jnp.dot(last, dp[half:], preferred_element_type=jnp.float32)
            inside.append(jnp.concatenate([above, below], 0))
        both = spread_pair(exp_cum, pair, first)
        decay = both[GROUP - 1 : GROUP, :]
        scale = spread_pair(late_scale, pair, first)
        xw_ref[:, at] = (xf * scale).astype(jnp.bfloat16)
        dcarry = (df * both).astype(jnp.bfloat16)
        dcarry_ref[:, at] = dcarry
        grad = run_ref[:, at]
        grad_low = grad.astype(jnp.bfloat16)
        low_ref[:, at] = grad_low
        dxs = jnp.dot(bm, grad_low, preferred_element_type=jnp.float32) * scale
        inner = jnp.where(first, inside[0], inside[1]) + dxs
        gskip_ref[0:1, at] += jnp.sum(df * xf, 0, keepdims=True)
        product = xf * inner
        top = product.astype(jnp.bfloat16)
        high_ref[:, at] = top
        rest_ref[:, at] = (product - top.astype(jnp.float32)).astype(jnp.bfloat16)
        dmixed = (inner + lanes_ref[1:2, at] * df).astype(jnp.bfloat16).astype(jnp.float32)
        dext_ref[pair, 0:GROUP, :] = dmixed * slope_ref[:, at]
        lane_ref[0:1, at] = jnp.sum(xf * dxs, 0, keepdims=True) + decay * jnp.sum(
            grad * state_ref[:, at], 0, keepdims=True
        )
        run_ref[:, at] = decay * grad + jnp.dot(cm_t, dcarry, preferred_element_type=jnp.float32)

    dcb_t = dcb_ref[...]
    dcb = dcb_t.T.astype(jnp.bfloat16)
    dbm = ndot(xw_ref[...], low_ref[...]) + jnp.dot(
        dcb_t.astype(jnp.bfloat16), cm, preferred_element_type=jnp.float32
    )
    dcm = ndot(dcarry_ref[...], state_ref[...].astype(jnp.bfloat16)) + jnp.dot(
        dcb, bm, preferred_element_type=jnp.float32
    )
    for place, part in enumerate((dbm, dcm)):
        at = slice(INNER + place * STATE, INNER + (place + 1) * STATE)
        dext_ref[INNER // PAIR + place, 0:GROUP, :] = part.astype(jnp.bfloat16).astype(jnp.float32) * slope_ref[:, at]
    seg = seg_ref[...]
    sums = jnp.dot(high_ref[...], seg, preferred_element_type=jnp.float32) + jnp.dot(
        rest_ref[...], seg, preferred_element_type=jnp.float32
    )
    dlast = split_dot(lane_ref[...], seg)[0:1, :]
    final = lax.broadcasted_iota(jnp.int32, (GROUP, 1), 0) == GROUP - 1
    dcum = delta_ref[...] - sums + jnp.where(final, dlast, 0.0)
    ones = lower_ones(GROUP, True).astype(jnp.float32).astype(jnp.bfloat16)
    dlog = exact_dot(ones, dcum)
    rate = heads_ref[1:2, :]
    ddt = jnp.where(dt > 0.0, sums / dt, 0.0) + dlog * rate
    ddt = ddt / (1.0 + jnp.exp(-raw))
    dxt_ref[:, CONVW:] = ddt.astype(jnp.bfloat16)
    ghead_ref[0:1, :] += jnp.sum(ddt, 0, keepdims=True)
    ghead_ref[1:2, :] += jnp.sum(dlog * dt, 0, keepdims=True) * rate

    def conv_chunk(chunk, carry):
        at = pl.ds(pl.multiple_of(chunk * PAIR, PAIR), PAIR)
        sums = [jnp.zeros((8, PAIR), jnp.float32)] * (KCONV + 1)
        for row in range(0, GROUP, STRIP):
            given = xt_ref[row : row + STRIP, at].astype(jnp.float32)
            total = None
            for tap in range(KCONV):
                start = KCONV - 1 - tap + row
                moved = dext_ref[chunk, start : start + STRIP, :]
                term = taps_ref[tap : tap + 1, at] * moved
                total = term if total is None else total + term
                sums[tap] = sums[tap] + jnp.sum((given * moved).reshape(-1, 8, PAIR), 0)
                if tap == KCONV - 1:
                    sums[KCONV] = sums[KCONV] + jnp.sum(moved.reshape(-1, 8, PAIR), 0)
            dxt_ref[row : row + STRIP, at] = total.astype(jnp.bfloat16)
        for k in range(KCONV + 1):
            gconv_ref[k : k + 1, at] += jnp.sum(sums[k], 0, keepdims=True)
        return carry

    lax.fori_loop(0, CONVW // PAIR, conv_chunk, 0)
    dext_ref[:, GROUP:, :] = dext_ref[:, 0:8, :]


def tall_block(width, count=None):
    if count is None:
        return pl.BlockSpec((GROUP, width), lambda i: (i, 0))
    return pl.BlockSpec((GROUP, width), lambda i: (count - 1 - i, 0))


def fixed_block(shape):
    return pl.BlockSpec(shape, lambda i: (0, 0))


def kernel_options():
    return pltpu.CompilerParams(
        dimension_semantics=("arbitrary",), vmem_limit_bytes=48 * 1024 * 1024
    )


def shape_of(rows, width, kind):
    return jax.ShapeDtypeStruct((rows, width), kind)


def run_scan(xt, taps, heads, lanes):
    length = xt.shape[0]
    count = length // GROUP
    f32, b16 = jnp.float32, jnp.bfloat16
    return pl.pallas_call(
        scan_kernel,
        grid=(count,),
        in_specs=[
            tall_block(XTAIL), fixed_block(taps.shape), fixed_block(heads.shape), fixed_block(lanes.shape),
        ],
        out_specs=[
            tall_block(CONVW), tall_block(CONVW), pl.BlockSpec((STATE, INNER), lambda i: (i, 0)),
            tall_block(INNER),
        ],
        out_shape=[
            shape_of(length, CONVW, b16), shape_of(length, CONVW, f32),
            shape_of(count * STATE, INNER, f32), shape_of(length, INNER, f32),
        ],
        scratch_shapes=[
            pltpu.VMEM((STATE, INNER), f32), pltpu.VMEM((CONVW // PAIR, GROUP + 8, PAIR), f32),
            pltpu.VMEM((GROUP, GROUP), f32),
        ],
        compiler_params=kernel_options(),
        cost_estimate=pl.CostEstimate(flops=25 * 10**9, bytes_accessed=30 * 10**6, transcendentals=10**7),
        name="scan_forward",
    )(xt, taps, heads, lanes)


def run_gate(z, ssd, mixed, x, go, wout, lanes, seg):
    length = x.shape[0]
    f32, b16 = jnp.float32, jnp.bfloat16
    return pl.pallas_call(
        gate_kernel,
        grid=(length // GROUP,),
        in_specs=[
            tall_block(INNER), tall_block(INNER), tall_block(INNER), tall_block(WIDE), tall_block(WIDE),
            fixed_block(wout.shape), fixed_block(lanes.shape), fixed_block(seg.shape),
        ],
        out_specs=[
            tall_block(WIDE), tall_block(INNER), tall_block(INNER), tall_block(INNER), tall_block(PAIR),
            fixed_block((8, INNER)),
        ],
        out_shape=[
            shape_of(length, WIDE, b16), shape_of(length, INNER, b16), shape_of(length, INNER, b16),
            shape_of(length, INNER, b16), shape_of(length, PAIR, f32), shape_of(8, INNER, f32),
        ],
        scratch_shapes=[
            pltpu.VMEM((GROUP, INNER), f32), pltpu.VMEM((GROUP, INNER), b16),
            pltpu.VMEM((GROUP, INNER), b16),
        ],
        compiler_params=kernel_options(),
        cost_estimate=pl.CostEstimate(flops=20 * 10**9, bytes_accessed=30 * 10**6, transcendentals=10**7),
        name="gate_both_ways",
    )(z, ssd, mixed, x, go, wout, lanes, seg)


def run_backward(xt, mixed, slope, dssd, states, delta, taps, heads, lanes, seg):
    length = xt.shape[0]
    count = length // GROUP
    f32, b16 = jnp.float32, jnp.bfloat16
    return pl.pallas_call(
        backward_kernel,
        grid=(count,),
        in_specs=[
            tall_block(XTAIL, count), tall_block(CONVW, count), tall_block(CONVW, count),
            tall_block(INNER, count), pl.BlockSpec((STATE, INNER), lambda i: (count - 1 - i, 0)),
            tall_block(PAIR, count), fixed_block(taps.shape), fixed_block(heads.shape),
            fixed_block(lanes.shape), fixed_block(seg.shape),
        ],
        out_specs=[
            tall_block(XTAIL, count), fixed_block((8, CONVW)), fixed_block((8, PAIR)),
            fixed_block((8, INNER)),
        ],
        out_shape=[
            shape_of(length, XTAIL, b16), shape_of(8, CONVW, f32), shape_of(8, PAIR, f32),
            shape_of(8, INNER, f32),
        ],
        scratch_shapes=[
            pltpu.VMEM((STATE, INNER), f32), pltpu.VMEM((CONVW // PAIR, GROUP + 8, PAIR), f32),
            pltpu.VMEM((GROUP, GROUP), f32), pltpu.VMEM((GROUP, GROUP), f32),
            pltpu.VMEM((GROUP, INNER), b16), pltpu.VMEM((GROUP, INNER), b16),
            pltpu.VMEM((GROUP, INNER), b16), pltpu.VMEM((GROUP, INNER), b16),
            pltpu.VMEM((8, INNER), f32), pltpu.VMEM((STATE, INNER), b16),
        ],
        compiler_params=kernel_options(),
        cost_estimate=pl.CostEstimate(flops=30 * 10**9, bytes_accessed=30 * 10**6, transcendentals=10**7),
        name="scan_backward",
    )(xt, mixed, slope, dssd, states, delta, taps, heads, lanes, seg)


def head_segments():
    rows = lax.broadcasted_iota(jnp.int32, (INNER, PAIR), 0) // HEADDIM
    cols = lax.broadcasted_iota(jnp.int32, (INNER, PAIR), 1)
    return (rows == cols).astype(jnp.bfloat16)


def head_tables(dt_bias, rate, skip):
    pad = lambda v: jnp.pad(v.astype(jnp.float32), (0, PAIR - HEADS))
    zero = jnp.zeros((PAIR,), jnp.float32)
    heads = jnp.stack([pad(dt_bias), pad(rate)] + [zero] * 6)
    return (heads, jnp.repeat(skip, HEADDIM))


def input_norm(xb, gain_in):
    xf = xb.astype(jnp.float32)
    r_in = lax.rsqrt(jnp.mean(xf * xf, -1, keepdims=True) + EPS)
    return (xf, r_in, (xf * r_in * gain_in.astype(jnp.float32)).astype(jnp.bfloat16))


def input_grad(xf, r_in, gain_in, dnormed, cot):
    scaled = gain_in.astype(jnp.float32) * dnormed
    return (
        r_in * scaled
        - xf * r_in**3 * jnp.mean(scaled * xf, -1, keepdims=True)
        + cot.astype(jnp.float32)
    ).astype(jnp.bfloat16)


def low_dot(left, right):
    return jnp.dot(left, right, preferred_element_type=jnp.float32).astype(jnp.bfloat16)


SPARE = 1816


def grid_place():
    dp = lax.axis_index("dp")
    return (dp // 4, lax.rem(dp // 2, 2), lax.rem(dp, 2), lax.axis_index("seq"))


def grid_moves(step):
    high = lax.axis_size("dp") // 4
    pairs = []
    for z in range(high):
        for y in range(2):
            for c in range(2):
                for x in range(2):
                    to = ((z + step[0]) % high, y ^ step[1], c ^ step[2], x ^ step[3])
                    pairs.append((((z * 2 + y) * 2 + c) * 2 + x, ((to[0] * 2 + to[1]) * 2 + to[2]) * 2 + to[3]))
    return pairs


def grid_send(array, step):
    return lax.ppermute(array, ("dp", "seq"), grid_moves(step))


def pick(array, axes, places):
    start = [0] * array.ndim
    size = list(array.shape)
    for axis, place in zip(axes, places):
        start[axis] = place
        size[axis] = 1
    out = lax.dynamic_slice(array, start, size)
    return out.reshape([n for axis, n in enumerate(array.shape) if axis not in axes])


def add_up(parts):
    total = parts[0].astype(jnp.float32)
    for part in parts[1:]:
        total = total + part.astype(jnp.float32)
    return total


FLIPS = ((0, 1), (1, 0), (1, 1))


def reduce_core(grads, kind=jnp.bfloat16):
    high = lax.axis_size("dp") // 4
    _, _, c, _ = grid_place()
    grads = [grad.reshape((high, 2, 2, 2) + grad.shape[1:]) for grad in grads]
    sent = jnp.concatenate([pick(grad, (2,), (1 - c,)) for grad in grads], -1)
    kept = jnp.concatenate([pick(grad, (2,), (c,)) for grad in grads], -1)
    return add_up([kept, grid_send(sent, (0, 0, 1, 0))]).astype(kind)


def plane_parts(parts):
    _, y, _, x = grid_place()
    found = [pick(parts, (1, 2), (y, x))]
    for fy, fx in FLIPS:
        piece = pick(parts, (1, 2), (y ^ fy, x ^ fx))
        found.append(grid_send(piece, (0, fy, 0, fx)))
    return found


def line_parts(parts):
    high = lax.axis_size("dp") // 4
    z, _, _, _ = grid_place()
    found = [pick(parts, (0,), (z,))]
    for hop in range(1, high):
        piece = pick(parts, (0,), (lax.rem(z + hop, high),))
        found.append(grid_send(piece, (hop, 0, 0, 0)))
    return found


def gather_line(own):
    high = lax.axis_size("dp") // 4
    return jnp.stack([own] + [grid_send(own, (hop, 0, 0, 0)) for hop in range(1, high)])


def gather_plane(tall):
    return [tall] + [grid_send(tall, (0, fy, 0, fx)) for fy, fx in FLIPS]


def join_kernel(cuts, place_ref, *refs):
    pieces, outs = refs[:8], refs[8:]
    high = pieces[0].shape[0]
    for slot, piece in enumerate(pieces):
        fy, fx = (((0, 0),) + FLIPS)[slot // 2]
        y, c, x = place_ref[1] ^ fy, place_ref[2] ^ (slot % 2), place_ref[3] ^ fx
        for hop in range(high):
            z = lax.rem(place_ref[0] + high - hop, high)
            for out, cut in zip(outs, cuts):
                for j, (start, size) in enumerate(cut):
                    out[z, y, c, x, j] = piece[hop, :, start : start + size]


def core_pieces(pieces):
    both = []
    for piece in pieces:
        both += [piece, grid_send(piece, (0, 0, 1, 0))]
    return both


def place_now():
    return jnp.stack([jnp.asarray(p, jnp.int32) for p in grid_place()])


def join_options():
    return pltpu.CompilerParams(vmem_limit_bytes=24 * 1024 * 1024)


def gather_core(pieces, cuts):
    high, rows, _ = pieces[0].shape
    shapes = [(high, 2, 2, 2, len(cut), rows, cut[0][1]) for cut in cuts]
    outs = pl.pallas_call(
        functools.partial(join_kernel, cuts),
        in_specs=[pl.BlockSpec(memory_space=pltpu.SMEM)] + [pl.BlockSpec(memory_space=pltpu.VMEM)] * 8,
        out_specs=[pl.BlockSpec(memory_space=pltpu.VMEM)] * len(cuts),
        out_shape=[jax.ShapeDtypeStruct(shape, pieces[0].dtype) for shape in shapes],
        compiler_params=join_options(),
        name="join_rows",
    )(place_now(), *core_pieces(pieces))
    return [full.reshape((-1, full.shape[-1])) for full in outs]


def join_first_kernel(cuts, place_ref, *refs):
    spots, masks, skip_ref = refs[8:11], refs[11:14], refs[14]
    full_ref, taps_ref, lanes_ref, gain_ref, held_ref = refs[15:]
    join_kernel(cuts, place_ref, *refs[:8], full_ref)
    high = refs[0].shape[0]
    for slot, piece in enumerate(refs[:8]):
        fy, fx = (((0, 0),) + FLIPS)[slot // 2]
        y, c, x = place_ref[1] ^ fy, place_ref[2] ^ (slot % 2), place_ref[3] ^ fx
        for hop in range(high):
            z = lax.rem(place_ref[0] + high - hop, high)
            owner = ((z * 2 + y) * 2 + c) * 2 + x
            block = piece[hop, 0:16, XTAIL - PAIR : XTAIL].astype(jnp.float32)
            held_ref[owner] = block[0:8]

    def line(row, which):
        spread = jnp.dot(
            held_ref[:, row, :].astype(jnp.bfloat16), spots[which][...], preferred_element_type=jnp.float32
        )
        return jnp.sum(spread * masks[which][...], 0, keepdims=True)

    taps_ref[...] = jnp.zeros_like(taps_ref)
    for row in range(KCONV + 1):
        taps_ref[row : row + 1, :] = line(row, 0)
    lanes_ref[...] = jnp.zeros_like(lanes_ref)
    lanes_ref[0:1, :] = line(KCONV + 1, 1)
    lanes_ref[1:2, :] = skip_ref[0:1, :]
    gain_ref[...] = jnp.zeros_like(gain_ref)
    gain_ref[0:1, :] = line(KCONV + 2, 2)


def spread_tables(width, devices):
    size = width // devices
    lane = lax.broadcasted_iota(jnp.int32, (PAIR, width), 1)
    spot = lax.broadcasted_iota(jnp.int32, (PAIR, width), 0) - (SPARE - XTAIL + PAIR) == lane % size
    owner = lax.broadcasted_iota(jnp.int32, (devices, width), 0)
    mask = owner == lax.broadcasted_iota(jnp.int32, (devices, width), 1) // size
    return (spot.astype(jnp.bfloat16), mask.astype(jnp.float32))


def gather_first(pieces, skip_lanes):
    high, rows, width = pieces[0].shape
    devices = 8 * high
    tables = [spread_tables(w, devices) for w in (CONVW, INNER, WIDE)]
    f32 = jnp.float32
    full, taps, lanes, gain = pl.pallas_call(
        functools.partial(join_first_kernel, (((0, width),),)),
        in_specs=[pl.BlockSpec(memory_space=pltpu.SMEM)] + [pl.BlockSpec(memory_space=pltpu.VMEM)] * 15,
        out_specs=[pl.BlockSpec(memory_space=pltpu.VMEM)] * 4,
        out_shape=[
            jax.ShapeDtypeStruct((high, 2, 2, 2, 1, rows, width), pieces[0].dtype),
            shape_of(8, CONVW, f32), shape_of(8, INNER, f32), shape_of(8, WIDE, f32),
        ],
        scratch_shapes=[pltpu.VMEM((devices, 8, PAIR), f32)],
        compiler_params=join_options(),
        name="join_first",
    )(
        place_now(), *core_pieces(pieces), *[t[0] for t in tables], *[t[1] for t in tables],
        jnp.broadcast_to(skip_lanes[None], (8, INNER)),
    )
    return (full.reshape(-1, width), taps, lanes, gain[0])


def after(value, *others):
    return lax.optimization_barrier((value,) + others)[0]


def swap_pick(parts):
    return lax.dynamic_index_in_dim(parts, 1 - lax.axis_index("seq"), 0, False)


def swap_send(parts):
    return grid_send(swap_pick(parts), (0, 0, 0, 1))


def swap_join(parts, got):
    place = lax.axis_index("seq")
    own = lax.dynamic_index_in_dim(parts, place, 0, False)
    return jnp.concatenate([jnp.where(place == 0, own, got), jnp.where(place == 0, got, own)], 0)


def swap_halves(parts, *guards):
    return swap_join(parts, after(swap_send(parts), *guards))


def pack_small(gain, taps, bias, gate, heads):
    lines = [taps, bias[None], gate[None], gain[None], heads[None]]
    lines = [jnp.pad(line, ((0, 0), (0, PAIR - line.shape[1]))) for line in lines]
    return jnp.concatenate(lines, 0)


def unpack_small(block, sizes):
    taps = block[..., :KCONV, : sizes[0]]
    return [taps] + [block[..., KCONV + k, :size] for k, size in enumerate(sizes[1:])]


def fast_shards(
    x_in, grad_out, norm_gain, in_weight, conv_weight, conv_bias, gate_gain, out_weight, dt_bias, a_log, skip
):
    rate = -jnp.exp(a_log)
    devices = lax.axis_size(("dp", "seq"))
    micro, _, length, _ = x_in.shape
    rows = in_weight.shape[0]
    sizes = (conv_weight.shape[1], conv_bias.size, gate_gain.size, norm_gain.size)
    place = lambda a, row, column: jnp.pad(
        a, ((row, rows - row - a.shape[0]), (column, XTAIL - column - a.shape[1]))
    )
    first = (
        place(in_weight[:, INNER:], 0, 0)
        + place(conv_weight, 0, SPARE)
        + place(conv_bias[None], KCONV, SPARE)
        + place(gate_gain[None], KCONV + 1, SPARE)
        + place(norm_gain[None], KCONV + 2, SPARE)
    )
    second = jnp.concatenate([in_weight[:, :INNER], out_weight[:rows], out_weight[rows:]], 1)

    line_first = gather_line(first)
    x_got = swap_send(x_in[:, 0])
    xb = swap_join(x_in[:, 0], x_got)
    plane_first = gather_plane(line_first)
    line_second = gather_line(after(second, plane_first[2]))
    heads, skip_lanes = head_tables(dt_bias, rate, skip)
    seg = head_segments()
    w_xt, taps_bias, lanes, gain_in = gather_first(plane_first, skip_lanes)
    line_second = after(line_second, *plane_first)
    second_y = grid_send(line_second, (0, 1, 0, 0))
    second_x = grid_send(line_second, (0, 0, 0, 1))
    plane_second = [line_second, second_x, second_y, grid_send(second_x, (0, 1, 0, 0))]
    xf, r_in, normed = input_norm(xb, gain_in)
    normed = after(normed)
    xt = after(low_dot(normed, w_xt), second_x)
    mixed, slope, states, ssd = run_scan(xt, taps_bias, heads, lanes)
    cot = swap_halves(after(grad_out[:, 0], second_x), ssd)

    plane_second = [after(piece, ssd) for piece in plane_second]
    w_z, w_out = gather_core(
        plane_second, (((0, INNER),), ((INNER, WIDE), (INNER + WIDE, WIDE)))
    )
    z = low_dot(normed, w_z)
    y, gnorm, dz, dssd, delta, ggain = run_gate(z, ssd, mixed, xb, cot, w_out, lanes, seg)
    grad_wout = tdot(gnorm, cot).astype(jnp.bfloat16).reshape(devices, 2, rows, WIDE)
    grad_wz = tdot(normed, dz).astype(jnp.bfloat16)
    early = [grad_wz] + [grad_wout[:, k] for k in range(2)]
    early = reduce_core([part.reshape(devices, rows, -1) for part in early])
    dssd = after(dssd, early)
    y_got = swap_send(y.reshape(micro, length, WIDE))
    early = plane_parts(early)
    dxt, gconv, ghead, gskip = run_backward(
        xt, mixed, slope, dssd, states, delta, taps_bias, heads, lanes, seg
    )
    dxt, y_got = lax.optimization_barrier((dxt, y_got) + tuple(early))[:2]
    grad_wxt = tdot(normed, dxt).astype(jnp.bfloat16)
    late = reduce_core([grad_wxt.reshape(devices, rows, -1)])
    head_terms = jnp.concatenate(
        [ghead[0, :HEADS], ghead[1, :HEADS], jnp.sum(gskip[0].reshape(HEADS, HEADDIM), -1)]
    )
    tiny = jax.vmap(pack_small)(
        jnp.zeros((devices, 8), jnp.float32),
        gconv[:KCONV].reshape(KCONV, devices, -1).transpose(1, 0, 2),
        gconv[KCONV].reshape(devices, -1),
        jnp.sum(ggain, 0).reshape(devices, -1),
        jnp.broadcast_to(head_terms, (devices, 3 * HEADS)),
    )[:, :, : XTAIL - SPARE]
    tiny = reduce_core([tiny], jnp.float32)
    tiny = jnp.pad(tiny, ((0, 0),) * 3 + ((0, rows - KCONV - 4), (SPARE, 0)))
    late = (late.astype(jnp.float32) + tiny).astype(jnp.bfloat16)
    dn_z = ndot(after(dz, late), w_z)
    late = plane_parts(late)
    early = lax.optimization_barrier(tuple(early) + (late[2],))[:-1]
    dnormed = dn_z + ndot(after(dxt, late[2]), w_xt)
    dx = input_grad(xf, r_in, gain_in, dnormed, cot)
    dx_got = swap_send(after(dx.reshape(micro, length, WIDE), *late))
    early = add_up(line_parts(add_up(early).astype(jnp.bfloat16)))
    late = tuple(line_parts(add_up(late).astype(jnp.bfloat16)))
    y_got = after(y_got, late[1])
    y_out = swap_join(y.reshape(micro, length, WIDE), y_got).reshape(x_in.shape)
    late = add_up(lax.optimization_barrier(late + (dx_got,))[:-1])
    dx_in = swap_join(dx.reshape(micro, length, WIDE), dx_got).reshape(x_in.shape)
    own_in = jnp.concatenate([early[:, :INNER], late[:, :SPARE]], 1)
    owned = early[:, INNER:]
    own_out = jnp.concatenate([owned[:, :WIDE], owned[:, WIDE:]], 0)
    own = late[:, SPARE:]
    found = unpack_small(own, sizes)
    heads_sum = own[KCONV + 3]
    weighted = jnp.sum(own_in * in_weight.astype(jnp.float32), -1)
    grad_gain = weighted / norm_gain.astype(jnp.float32)
    return (
        y_out, dx_in, grad_gain, own_in, found[0], found[1], found[2], own_out,
        heads_sum[:HEADS], heads_sum[HEADS : 2 * HEADS], heads_sum[2 * HEADS : 3 * HEADS],
    )


def shards(x_in, *rest):
    dp, seq = lax.axis_size("dp"), lax.axis_size("seq")
    if x_in.shape[0] == seq == 2 and dp % 4 == 0 and rest[1].size * dp * seq == WIDE:
        return fast_shards(x_in, *rest)
    return shards_general(x_in, *rest)


def shards_general(
    x_in,
    grad_out,
    norm_gain,
    in_weight,
    conv_weight,
    conv_bias,
    gate_gain,
    out_weight,
    dt_bias,
    a_log,
    skip,
):
    micro = x_in.shape[0]
    rate = -jnp.exp(a_log)
    devices = lax.axis_size(("dp", "seq"))
    results = []
    saves = []
    for index in range(micro):
        wts = (
            lax.all_gather(norm_gain, ("dp", "seq"), axis=0, tiled=True),
            lax.all_gather(in_weight, ("dp", "seq"), axis=0, tiled=True),
            lax.all_gather(conv_weight, ("dp", "seq"), axis=1, tiled=True),
            lax.all_gather(conv_bias, ("dp", "seq"), axis=0, tiled=True),
            lax.all_gather(gate_gain, ("dp", "seq"), axis=0, tiled=True),
            lax.all_gather(out_weight, ("dp", "seq"), axis=0, tiled=True),
        )
        result, saved = forward(x_in[index, 0], wts, dt_bias, rate, skip)
        results.append(result)
        saves.append(saved)
    dx_list = [None] * micro
    summed = None
    for index in reversed(range(micro)):
        wts = (
            lax.all_gather(norm_gain, ("dp", "seq"), axis=0, tiled=True),
            lax.all_gather(in_weight, ("dp", "seq"), axis=0, tiled=True),
            lax.all_gather(conv_weight, ("dp", "seq"), axis=1, tiled=True),
            lax.all_gather(conv_bias, ("dp", "seq"), axis=0, tiled=True),
            lax.all_gather(gate_gain, ("dp", "seq"), axis=0, tiled=True),
            lax.all_gather(out_weight, ("dp", "seq"), axis=0, tiled=True),
        )
        dx_part, terms = backward(saves[index], grad_out[index, 0], wts, dt_bias, rate, skip)
        dx_list[index] = dx_part
        summed = terms if summed is None else jax.tree.map(lambda a, b: a + b, summed, terms)
    spread = summed[:6] + (jnp.broadcast_to(summed[6], (devices, 3 * HEADS)),)
    summed = (
        lax.psum_scatter(spread[0], ("dp", "seq"), scatter_dimension=0, tiled=True),
        lax.psum_scatter(spread[1], ("dp", "seq"), scatter_dimension=0, tiled=True),
        lax.psum_scatter(spread[2], ("dp", "seq"), scatter_dimension=1, tiled=True),
        lax.psum_scatter(spread[3], ("dp", "seq"), scatter_dimension=0, tiled=True),
        lax.psum_scatter(spread[4], ("dp", "seq"), scatter_dimension=0, tiled=True),
        lax.psum_scatter(spread[5], ("dp", "seq"), scatter_dimension=0, tiled=True),
        lax.psum_scatter(spread[6], ("dp", "seq"), scatter_dimension=0, tiled=True),
    )
    heads_sum = summed[6].reshape(3, HEADS)
    y_out = jnp.stack(results)[:, None]
    dx_in = jnp.stack(dx_list)[:, None]
    return (
        y_out,
        dx_in,
        summed[0],
        summed[1],
        summed[2],
        summed[3],
        summed[4],
        summed[5],
        heads_sum[0],
        heads_sum[1],
        heads_sum[2],
    )


def solution(mesh):
    return jax.shard_map(
        shards,
        mesh=mesh,
        in_specs=(
            P(None, "dp", "seq", None),
            P(None, "dp", "seq", None),
            P(("dp", "seq")),
            P(("dp", "seq"), None),
            P(None, ("dp", "seq")),
            P(("dp", "seq")),
            P(("dp", "seq")),
            P(("dp", "seq"), None),
            P(),
            P(),
            P(),
        ),
        out_specs=(
            P(None, "dp", "seq", None),
            P(None, "dp", "seq", None),
            P(("dp", "seq")),
            P(("dp", "seq"), None),
            P(None, ("dp", "seq")),
            P(("dp", "seq")),
            P(("dp", "seq")),
            P(("dp", "seq"), None),
            P(),
            P(),
            P(),
        ),
        check_vma=False,
    )
```

```python
import functools

import jax
import jax.numpy as jnp
from jax import lax
from jax.experimental import pallas as pl
from jax.experimental.pallas import tpu as pltpu
from jax.sharding import PartitionSpec as P

HEADS = 24
HEADDIM = 64
STATE = 128
KCONV = 4
GROUP = 256
INNER = 1536
CONVW = 1792


EPS = 1e-05


def shifted(array, axis, by):
    devices = lax.axis_size(axis)
    pairs = [(i, i + by) for i in range(devices) if 0 <= i + by < devices]
    return lax.ppermute(array, axis, pairs)


def prefix(array, axis, join, neutral, backward):
    count = lax.axis_size(axis)
    place = lax.axis_index(axis)
    ahead = count - 1 - place if backward else place
    gathered = jax.tree.map(
        lambda a, kind: lax.all_gather(a.astype(kind), axis), array, (jnp.bfloat16, jnp.bfloat16)
    )
    state = jax.tree.map(lambda a, e: jnp.zeros_like(a) + jnp.asarray(e, a.dtype), array, neutral)

    def one(hop, state):
        source = count - 1 - hop if backward else hop
        return join(
            state,
            jax.tree.map(
                lambda a, own: lax.dynamic_index_in_dim(a, source, 0, False).astype(own.dtype),
                gathered,
                array,
            ),
        )

    return lax.fori_loop(0, ahead, one, state)


def tdot(left, right):
    return lax.dot_general(
        left, right, (((0,), (0,)), ((), ())), preferred_element_type=jnp.float32
    )


def ndot(left, right):
    return lax.dot_general(
        left, right, (((1,), (1,)), ((), ())), preferred_element_type=jnp.float32
    )


def dsilu(value):
    sig = jax.nn.sigmoid(value)
    return sig * (1.0 + value * (1.0 - sig))


def merge_states(earlier, later):
    return (earlier[0] * later[0], earlier[1] * later[0][:, None, None] + later[1])


def decay_table(cum_t):
    size = cum_t.shape[-1]
    rows = lax.broadcasted_iota(jnp.int32, (size, size), 0)
    cols = lax.broadcasted_iota(jnp.int32, (size, size), 1)
    lower = rows >= cols
    diff = cum_t[:, :, :, None] - cum_t[:, :, None, :]
    return jnp.exp(jnp.where(lower, diff, 0.0)) * lower.astype(jnp.float32)


def forward(xb, wts, dt_bias, rate, skip):
    gain_in, w_in, w_conv, b_conv, gain_gate, w_out = wts
    length = xb.shape[0]
    count = length // GROUP
    xf = xb.astype(jnp.float32)
    r_in = lax.rsqrt(jnp.mean(xf * xf, -1, keepdims=True) + EPS)
    normed = (xf * r_in * gain_in.astype(jnp.float32)).astype(jnp.bfloat16)
    proj = jnp.dot(normed, w_in, preferred_element_type=jnp.float32).astype(jnp.bfloat16)
    conv_in = proj[:, INNER : INNER + CONVW]
    rim = shifted(conv_in[length - KCONV + 1 :], "seq", 1)
    padded = jnp.concatenate([rim, conv_in], 0).astype(jnp.float32)
    taps = w_conv.astype(jnp.float32)
    conv_out = b_conv.astype(jnp.float32) + jnp.zeros((length, CONVW), jnp.float32)
    for tap in range(KCONV):
        conv_out = conv_out + taps[tap] * padded[tap : tap + length]
    mixed = jax.nn.silu(conv_out).astype(jnp.bfloat16)
    xh = mixed[:, :INNER].reshape(count, GROUP, HEADS, HEADDIM)
    bm = mixed[:, INNER : INNER + STATE].reshape(count, GROUP, STATE)
    cm = mixed[:, INNER + STATE :].reshape(count, GROUP, STATE)
    dt_raw = proj[:, INNER + CONVW :].astype(jnp.float32)
    step = jax.nn.softplus(dt_raw + dt_bias)
    step_t = step.reshape(count, GROUP, HEADS).transpose(0, 2, 1)
    cum_t = jnp.cumsum(step_t * rate[None, :, None], -1)
    decay = decay_table(cum_t)
    cbm = jnp.einsum("ctn,csn->cts", cm, bm, preferred_element_type=jnp.float32)
    weights = (cbm[:, None] * decay * step_t[:, :, None, :]).astype(jnp.bfloat16)
    inside = jnp.einsum("chts,cshp->cthp", weights, xh, preferred_element_type=jnp.float32)
    last = cum_t[:, :, -1]
    block_decay = jnp.exp(last)
    scale = (jnp.exp(last[:, :, None] - cum_t) * step_t).transpose(0, 2, 1)
    x_scaled = (xh.astype(jnp.float32) * scale[..., None]).astype(jnp.bfloat16)
    local = jnp.einsum("cshp,csn->chpn", x_scaled, bm, preferred_element_type=jnp.float32)
    total_decay = jnp.ones((HEADS,), jnp.float32)
    total_state = jnp.zeros((HEADS, HEADDIM, STATE), jnp.float32)
    for block in range(count):
        total_state = total_state * block_decay[block][:, None, None] + local[block]
        total_decay = total_decay * block_decay[block]
    identity = (jnp.ones((HEADS,), jnp.float32), jnp.zeros((HEADS, HEADDIM, STATE), jnp.float32))
    _, incoming = prefix((total_decay, total_state), "seq", merge_states, identity, False)
    entering = []
    running = incoming
    for block in range(count):
        entering.append(running)
        running = running * block_decay[block][:, None, None] + local[block]
    state_in = jnp.stack(entering)
    state_low = state_in.astype(jnp.bfloat16)
    exp_cum = jnp.exp(cum_t).transpose(0, 2, 1)
    carried = exp_cum[..., None] * jnp.einsum(
        "ctn,chpn->cthp", cm, state_low, preferred_element_type=jnp.float32
    )
    ssd = (inside + carried + skip[None, None, :, None] * xh.astype(jnp.float32)).reshape(
        length, INNER
    )
    zsig = jax.nn.silu(proj[:, :INNER].astype(jnp.float32))
    gated = ssd * zsig
    r_gate = lax.rsqrt(jnp.mean(gated * gated, -1, keepdims=True) + EPS)
    gnorm = (gated * r_gate * gain_gate.astype(jnp.float32)).astype(jnp.bfloat16)
    result = (xf + jnp.dot(gnorm, w_out, preferred_element_type=jnp.float32)).astype(jnp.bfloat16)
    saved = (
        xf,
        r_in,
        normed,
        proj,
        padded,
        conv_out,
        mixed,
        step_t,
        cum_t,
        state_in,
        state_low,
        carried,
        ssd,
        zsig,
        gated,
        r_gate,
        gnorm,
    )
    return (result, saved)


def backward(saved, cot, wts, dt_bias, rate, skip):
    gain_in, w_in, w_conv, b_conv, gain_gate, w_out = wts
    (
        xf,
        r_in,
        normed,
        proj,
        padded,
        conv_out,
        mixed,
        step_t,
        cum_t,
        state_in,
        state_low,
        carried,
        ssd,
        zsig,
        gated,
        r_gate,
        gnorm,
    ) = saved
    length = xf.shape[0]
    count = length // GROUP
    grad_wout = tdot(gnorm, cot)
    dgnorm = ndot(cot, w_out)
    scaled_g = gain_gate.astype(jnp.float32) * dgnorm
    grad_ggain = jnp.sum(dgnorm * gated * r_gate, 0)
    dgated = r_gate * scaled_g - gated * r_gate**3 * jnp.mean(scaled_g * gated, -1, keepdims=True)
    dssd = (dgated * zsig).astype(jnp.bfloat16)
    zpart = proj[:, :INNER].astype(jnp.float32)
    dzpart = dgated * ssd * dsilu(zpart)
    xh = mixed[:, :INNER].reshape(count, GROUP, HEADS, HEADDIM)
    bm = mixed[:, INNER : INNER + STATE].reshape(count, GROUP, STATE)
    cm = mixed[:, INNER + STATE :].reshape(count, GROUP, STATE)
    xhf = xh.astype(jnp.float32)
    dyr = dssd.reshape(count, GROUP, HEADS, HEADDIM)
    dyf = dyr.astype(jnp.float32)
    decay = decay_table(cum_t)
    cbm = jnp.einsum("ctn,csn->cts", cm, bm, preferred_element_type=jnp.float32)
    full = cbm[:, None] * decay * step_t[:, :, None, :]
    weights = full.astype(jnp.bfloat16)
    grad_skip = jnp.sum(dyf * xhf, (0, 1, 3))
    dxh = skip[None, None, :, None] * dyf
    dweights = jnp.einsum("cthp,cshp->chts", dyr, xh, preferred_element_type=jnp.float32)
    dxh = dxh + jnp.einsum("chts,cthp->cshp", weights, dyr, preferred_element_type=jnp.float32)
    dcbm = jnp.sum(dweights * decay * step_t[:, :, None, :], 1).astype(jnp.bfloat16)
    dstep = jnp.sum(dweights * cbm[:, None] * decay, 2)
    product = dweights * full
    dcum = jnp.sum(product, 3) - jnp.sum(product, 2)
    dcum = dcum + jnp.sum(dyf * carried, -1).transpose(0, 2, 1)
    exp_cum = jnp.exp(cum_t).transpose(0, 2, 1)
    dcarry = (dyf * exp_cum[..., None]).astype(jnp.bfloat16)
    dcm = jnp.einsum("cthp,chpn->ctn", dcarry, state_low, preferred_element_type=jnp.float32)
    dstate_low = jnp.einsum("cthp,ctn->chpn", dcarry, cm, preferred_element_type=jnp.float32)
    last = cum_t[:, :, -1]
    block_decay = jnp.exp(last)
    total_decay = jnp.ones((HEADS,), jnp.float32)
    running = jnp.zeros((HEADS, HEADDIM, STATE), jnp.float32)
    for block in reversed(range(count)):
        running = running * block_decay[block][:, None, None] + dstate_low[block]
        total_decay = total_decay * block_decay[block]
    identity = (jnp.ones((HEADS,), jnp.float32), jnp.zeros((HEADS, HEADDIM, STATE), jnp.float32))
    _, later = prefix((total_decay, running), "seq", merge_states, identity, True)
    leaving = [later] * count
    running = later
    for block in reversed(range(count)):
        leaving[block] = running
        running = running * block_decay[block][:, None, None] + dstate_low[block]
    grad_state = jnp.stack(leaving)
    dlast = block_decay * jnp.sum(grad_state * state_in, (2, 3))
    scale_t = jnp.exp(last[:, :, None] - cum_t) * step_t
    scale = scale_t.transpose(0, 2, 1)
    x_scaled = (xhf * scale[..., None]).astype(jnp.bfloat16)
    grad_low = grad_state.astype(jnp.bfloat16)
    dxs = jnp.einsum("csn,chpn->cshp", bm, grad_low, preferred_element_type=jnp.float32)
    dbm = jnp.einsum("cshp,chpn->csn", x_scaled, grad_low, preferred_element_type=jnp.float32)
    dxh = dxh + dxs * scale[..., None]
    dscale = jnp.sum(dxs * xhf, -1).transpose(0, 2, 1)
    dstep = dstep + dscale * jnp.exp(last[:, :, None] - cum_t)
    dlast = dlast + jnp.sum(dscale * scale_t, -1)
    dcum = dcum - dscale * scale_t
    final = (lax.broadcasted_iota(jnp.int32, (GROUP,), 0) == GROUP - 1).astype(jnp.float32)
    dcum = dcum + dlast[:, :, None] * final
    dlog = jnp.flip(jnp.cumsum(jnp.flip(dcum, -1), -1), -1)
    dstep = dstep + dlog * rate[None, :, None]
    grad_alog = jnp.sum(dlog * step_t, (0, 2)) * rate
    dcm = dcm + jnp.einsum("cts,csn->ctn", dcbm, bm, preferred_element_type=jnp.float32)
    dbm = dbm + jnp.einsum("cts,ctn->csn", dcbm, cm, preferred_element_type=jnp.float32)
    dmixed = jnp.concatenate(
        [dxh.reshape(length, INNER), dbm.reshape(length, STATE), dcm.reshape(length, STATE)], -1
    )
    dmixed = dmixed.astype(jnp.bfloat16).astype(jnp.float32)
    dconv = dmixed * dsilu(conv_out)
    grad_cbias = jnp.sum(dconv, 0)
    grad_cweight = jnp.stack(
        [jnp.sum(dconv * padded[tap : tap + length], 0) for tap in range(KCONV)]
    )
    rim_back = shifted(dconv[: KCONV - 1], "seq", -1)
    extended = jnp.concatenate([dconv, rim_back], 0)
    taps = w_conv.astype(jnp.float32)
    dconv_in = jnp.zeros((length, CONVW), jnp.float32)
    for tap in range(KCONV):
        dconv_in = dconv_in + taps[tap] * extended[KCONV - 1 - tap : KCONV - 1 - tap + length]
    dt_raw = proj[:, INNER + CONVW :].astype(jnp.float32)
    ddt_raw = dstep.transpose(0, 2, 1).reshape(length, HEADS) * jax.nn.sigmoid(dt_raw + dt_bias)
    grad_dtb = jnp.sum(ddt_raw, 0)
    dproj = jnp.concatenate([dzpart, dconv_in, ddt_raw], -1).astype(jnp.bfloat16)
    grad_win = tdot(normed, dproj)
    dnormed = ndot(dproj, w_in)
    scaled_in = gain_in.astype(jnp.float32) * dnormed
    grad_gin = jnp.sum(dnormed * xf * r_in, 0)
    dx_in = (
        r_in * scaled_in
        - xf * r_in**3 * jnp.mean(scaled_in * xf, -1, keepdims=True)
        + cot.astype(jnp.float32)
    )
    head_terms = jnp.stack([grad_dtb, grad_alog, grad_skip]).reshape(1, 3 * HEADS)
    return (
        dx_in.astype(jnp.bfloat16),
        (grad_gin, grad_win, grad_cweight, grad_cbias, grad_ggain, grad_wout, head_terms),
    )


PAIR = 2 * HEADDIM
WIDE = 768
XTAIL = 1920
STRIP = 64
LOW = -1e30


def silu_parts(value):
    sig = 0.5 * jnp.tanh(0.5 * value) + 0.5
    return (sig, value * sig)


def split_dot(value, right):
    top = value.astype(jnp.bfloat16)
    rest = (value - top.astype(jnp.float32)).astype(jnp.bfloat16)
    return jnp.dot(top, right, preferred_element_type=jnp.float32) + jnp.dot(
        rest, right, preferred_element_type=jnp.float32
    )


def exact_dot(left, value):
    total = None
    for _ in range(3):
        part = value.astype(jnp.bfloat16)
        value = value - part.astype(jnp.float32)
        term = jnp.dot(left, part, preferred_element_type=jnp.float32)
        total = term if total is None else total + term
    return total


def lower_ones(size, flipped):
    rows = lax.broadcasted_iota(jnp.int32, (size, size), 0)
    cols = lax.broadcasted_iota(jnp.int32, (size, size), 1)
    return rows <= cols if flipped else rows >= cols


def step_sizes(raw, heads_ref):
    shifted_raw = raw.astype(jnp.float32) + heads_ref[0:1, :]
    dt = jnp.maximum(shifted_raw, 0.0) + jnp.log1p(jnp.exp(-jnp.abs(shifted_raw)))
    ones = lower_ones(GROUP, False).astype(jnp.float32).astype(jnp.bfloat16)
    cum = exact_dot(ones, dt * heads_ref[1:2, :])
    return (shifted_raw, dt, cum, cum - jnp.log(dt))


def spread_pair(table, pair, first):
    rows = table.shape[0]
    return jnp.where(first, spread_lanes(table, 2 * pair, rows), spread_lanes(table, 2 * pair + 1, rows))


def spread_lanes(table, head, rows):
    return jnp.broadcast_to(table[:, head : head + 1], (rows, PAIR))


def scan_kernel(
    xt_ref, taps_ref, heads_ref, lanes_ref,
    mixed_ref, slope_ref, state_ref, ssd_ref,
    run_ref, cin_ref, cb_ref,
):
    half = GROUP // 2

    @pl.when(pl.program_id(0) == 0)
    def _():
        run_ref[...] = jnp.zeros_like(run_ref)
        cin_ref[:, 0:8, :] = jnp.zeros((CONVW // PAIR, 8, PAIR), jnp.float32)

    def conv_chunk(chunk, carry):
        at = pl.ds(pl.multiple_of(chunk * PAIR, PAIR), PAIR)
        cin_ref[chunk, 8 : 8 + GROUP, :] = xt_ref[:, at].astype(jnp.float32)
        for row in range(0, GROUP, STRIP):
            total = taps_ref[KCONV : KCONV + 1, at]
            for tap in range(KCONV):
                total = total + taps_ref[tap : tap + 1, at] * cin_ref[chunk, 5 + tap + row : 5 + tap + row + STRIP, :]
            sig, value = silu_parts(total)
            mixed_ref[row : row + STRIP, at] = value.astype(jnp.bfloat16)
            slope_ref[row : row + STRIP, at] = sig + value * (1.0 - sig)
        cin_ref[chunk, 0:8, :] = cin_ref[chunk, GROUP : GROUP + 8, :]
        return carry

    lax.fori_loop(0, CONVW // PAIR, conv_chunk, 0)

    bm = mixed_ref[:, INNER : INNER + STATE]
    cm = mixed_ref[:, INNER + STATE : CONVW]
    bm_t = bm.astype(jnp.float32).T.astype(jnp.bfloat16)
    cb_ref[...] = ndot(cm, bm)
    _, _, cum, late = step_sizes(xt_ref[:, CONVW:], heads_ref)
    late_t = late.T
    scale = jnp.exp(cum[GROUP - 1 : GROUP, :] - late)
    lower = lower_ones(half, False)
    first = lax.broadcasted_iota(jnp.int32, (1, PAIR), 1) < HEADDIM
    for pair in range(HEADS // 2):
        at = slice(pair * PAIR, (pair + 1) * PAIR)
        xp = mixed_ref[:, at]
        spread = []
        inside = []
        for head in (2 * pair, 2 * pair + 1):
            here = spread_lanes(cum, head, GROUP)
            row = late_t[head : head + 1, :]
            near = jnp.exp(jnp.where(lower, here[:half] - row[:, :half], LOW))
            far = jnp.exp(here[half:] - row[:, :half])
            last = jnp.exp(jnp.where(lower, here[half:] - row[:, half:], LOW))
            near = (cb_ref[:half, :half] * near).astype(jnp.bfloat16)
            far = (cb_ref[half:, :half] * far).astype(jnp.bfloat16)
            last = (cb_ref[half:, half:] * last).astype(jnp.bfloat16)
            above = jnp.dot(near, xp[:half], preferred_element_type=jnp.float32)
            below = jnp.dot(
                jnp.concatenate([far, last], 1), xp, preferred_element_type=jnp.float32
            )
            inside.append(jnp.concatenate([above, below], 0))
            spread.append(here)
        both = jnp.exp(jnp.where(first, spread[0], spread[1]))
        decay = both[GROUP - 1 : GROUP, :]
        state = run_ref[:, at]
        carried = both * jnp.dot(
            cm, state.astype(jnp.bfloat16), preferred_element_type=jnp.float32
        )
        xf = xp.astype(jnp.float32)
        ssd_ref[:, at] = (
            jnp.where(first, inside[0], inside[1]) + carried + lanes_ref[1:2, at] * xf
        )
        xw = (xf * spread_pair(scale, pair, first)).astype(jnp.bfloat16)
        state_ref[:, at] = state
        run_ref[:, at] = decay * state + jnp.dot(
            bm_t, xw, preferred_element_type=jnp.float32
        )


def gate_kernel(
    z_ref, ssd_ref, xh_ref, x_ref, go_ref, wout_ref, lanes_ref, seg_ref,
    y_ref, gn_ref, dz_ref, dssd_ref, delta_ref, ggain_ref,
    dgn_ref, high_ref, rest_ref,
):
    @pl.when(pl.program_id(0) == 0)
    def _():
        ggain_ref[...] = jnp.zeros_like(ggain_ref)

    dgn_ref[...] = ndot(go_ref[...], wout_ref[...])

    def gate_rows(index, carry):
        rows = pl.ds(pl.multiple_of(index * 16, 16), 16)
        kept = []
        square = jnp.zeros((16, PAIR), jnp.float32)
        cross = jnp.zeros((16, PAIR), jnp.float32)
        for chunk in range(INNER // PAIR):
            at = slice(chunk * PAIR, (chunk + 1) * PAIR)
            sig, value = silu_parts(z_ref[rows, at].astype(jnp.float32))
            gated = ssd_ref[rows, at] * value
            square = square + gated * gated
            cross = cross + lanes_ref[0:1, at] * dgn_ref[rows, at] * gated
            kept.append((sig, value, gated))
        scale = lax.rsqrt(jnp.sum(square, -1, keepdims=True) * (1.0 / INNER) + EPS)
        pull = scale * scale * scale * (jnp.sum(cross, -1, keepdims=True) * (1.0 / INNER))
        for chunk in range(INNER // PAIR):
            at = slice(chunk * PAIR, (chunk + 1) * PAIR)
            sig, value, gated = kept[chunk]
            gain = lanes_ref[0:1, at]
            ssd = ssd_ref[rows, at]
            unit = gated * scale
            gn_ref[rows, at] = (unit * gain).astype(jnp.bfloat16)
            dgn = dgn_ref[rows, at]
            term = dgn * unit
            ggain_ref[:, at] += term[0:8] + term[8:16]
            dgated = scale * (gain * dgn) - gated * pull
            dssd = (dgated * value).astype(jnp.bfloat16)
            dssd_ref[rows, at] = dssd
            dz_ref[rows, at] = (dgated * ssd * (sig + value * (1.0 - sig))).astype(jnp.bfloat16)
            xh = xh_ref[rows, at].astype(jnp.float32)
            product = dssd.astype(jnp.float32) * (ssd - lanes_ref[1:2, at] * xh)
            top = product.astype(jnp.bfloat16)
            high_ref[rows, at] = top
            rest_ref[rows, at] = (product - top.astype(jnp.float32)).astype(jnp.bfloat16)
        return carry

    lax.fori_loop(0, GROUP // 16, gate_rows, 0, unroll=8)
    seg = seg_ref[...]
    delta_ref[...] = jnp.dot(
        high_ref[...], seg, preferred_element_type=jnp.float32
    ) + jnp.dot(rest_ref[...], seg, preferred_element_type=jnp.float32)
    y_ref[...] = (
        x_ref[...].astype(jnp.float32)
        + jnp.dot(gn_ref[...], wout_ref[...], preferred_element_type=jnp.float32)
    ).astype(jnp.bfloat16)


def backward_kernel(
    xt_ref, mixed_ref, slope_ref, dssd_ref, state_ref, delta_ref,
    taps_ref, heads_ref, lanes_ref, seg_ref,
    dxt_ref, gconv_ref, ghead_ref, gskip_ref,
    run_ref, dext_ref, cb_ref, dcb_ref, xw_ref, dcarry_ref, high_ref, rest_ref, lane_ref, low_ref,
):
    half = GROUP // 2

    @pl.when(pl.program_id(0) == 0)
    def _():
        run_ref[...] = jnp.zeros_like(run_ref)
        dext_ref[:, GROUP:, :] = jnp.zeros((CONVW // PAIR, 8, PAIR), jnp.float32)
        gconv_ref[...] = jnp.zeros_like(gconv_ref)
        ghead_ref[...] = jnp.zeros_like(ghead_ref)
        gskip_ref[...] = jnp.zeros_like(gskip_ref)
        lane_ref[...] = jnp.zeros_like(lane_ref)

    bm = mixed_ref[:, INNER : INNER + STATE]
    cm = mixed_ref[:, INNER + STATE : CONVW]
    cm_t = cm.astype(jnp.float32).T.astype(jnp.bfloat16)
    cb_ref[...] = ndot(bm, cm)
    dcb_ref[...] = jnp.zeros_like(dcb_ref)
    raw, dt, cum, late = step_sizes(xt_ref[:, CONVW:], heads_ref)
    cum_t = cum.T
    exp_cum = jnp.exp(cum)
    late_scale = jnp.exp(cum[GROUP - 1 : GROUP, :] - late)
    upper = lower_ones(half, True)
    first = lax.broadcasted_iota(jnp.int32, (1, PAIR), 1) < HEADDIM
    masks = (first.astype(jnp.float32), 1.0 - first.astype(jnp.float32))
    for pair in range(HEADS // 2):
        at = slice(pair * PAIR, (pair + 1) * PAIR)
        xp = mixed_ref[:, at]
        dp = dssd_ref[:, at]
        xf = xp.astype(jnp.float32)
        df = dp.astype(jnp.float32)
        inside = []
        for place, head in enumerate((2 * pair, 2 * pair + 1)):
            here = spread_lanes(late, head, GROUP)
            row = cum_t[head : head + 1, :]
            own = (xf * masks[place]).astype(jnp.bfloat16)
            dw_top = ndot(own[:half], dp)
            dw_low = ndot(own[half:], dp[half:])
            near = jnp.exp(jnp.where(upper, row[:, :half] - here[:half], LOW))
            dcb_ref[:half, :half] += dw_top[:, :half] * near
            near = (cb_ref[:half, :half] * near).astype(jnp.bfloat16)
            far = jnp.exp(row[:, half:] - here[:half])
            dcb_ref[:half, half:] += dw_top[:, half:] * far
            far = (cb_ref[:half, half:] * far).astype(jnp.bfloat16)
            last = jnp.exp(jnp.where(upper, row[:, half:] - here[half:], LOW))
            dcb_ref[half:, half:] += dw_low * last
            last = (cb_ref[half:, half:] * last).astype(jnp.bfloat16)
            above = jnp.dot(
                jnp.concatenate([near, far], 1), dp, preferred_element_type=jnp.float32
            )
            below = jnp.dot(last, dp[half:], preferred_element_type=jnp.float32)
            inside.append(jnp.concatenate([above, below], 0))
        both = spread_pair(exp_cum, pair, first)
        decay = both[GROUP - 1 : GROUP, :]
        scale = spread_pair(late_scale, pair, first)
        xw_ref[:, at] = (xf * scale).astype(jnp.bfloat16)
        dcarry = (df * both).astype(jnp.bfloat16)
        dcarry_ref[:, at] = dcarry
        grad = run_ref[:, at]
        grad_low = grad.astype(jnp.bfloat16)
        low_ref[:, at] = grad_low
        dxs = jnp.dot(bm, grad_low, preferred_element_type=jnp.float32) * scale
        inner = jnp.where(first, inside[0], inside[1]) + dxs
        gskip_ref[0:1, at] += jnp.sum(df * xf, 0, keepdims=True)
        product = xf * inner
        top = product.astype(jnp.bfloat16)
        high_ref[:, at] = top
        rest_ref[:, at] = (product - top.astype(jnp.float32)).astype(jnp.bfloat16)
        dmixed = (inner + lanes_ref[1:2, at] * df).astype(jnp.bfloat16).astype(jnp.float32)
        dext_ref[pair, 0:GROUP, :] = dmixed * slope_ref[:, at]
        lane_ref[0:1, at] = jnp.sum(xf * dxs, 0, keepdims=True) + decay * jnp.sum(
            grad * state_ref[:, at], 0, keepdims=True
        )
        run_ref[:, at] = decay * grad + jnp.dot(cm_t, dcarry, preferred_element_type=jnp.float32)

    dcb_t = dcb_ref[...]
    dcb = dcb_t.T.astype(jnp.bfloat16)
    dbm = ndot(xw_ref[...], low_ref[...]) + jnp.dot(
        dcb_t.astype(jnp.bfloat16), cm, preferred_element_type=jnp.float32
    )
    dcm = ndot(dcarry_ref[...], state_ref[...].astype(jnp.bfloat16)) + jnp.dot(
        dcb, bm, preferred_element_type=jnp.float32
    )
    for place, part in enumerate((dbm, dcm)):
        at = slice(INNER + place * STATE, INNER + (place + 1) * STATE)
        dext_ref[INNER // PAIR + place, 0:GROUP, :] = part.astype(jnp.bfloat16).astype(jnp.float32) * slope_ref[:, at]
    seg = seg_ref[...]
    sums = jnp.dot(high_ref[...], seg, preferred_element_type=jnp.float32) + jnp.dot(
        rest_ref[...], seg, preferred_element_type=jnp.float32
    )
    dlast = split_dot(lane_ref[...], seg)[0:1, :]
    final = lax.broadcasted_iota(jnp.int32, (GROUP, 1), 0) == GROUP - 1
    dcum = delta_ref[...] - sums + jnp.where(final, dlast, 0.0)
    ones = lower_ones(GROUP, True).astype(jnp.float32).astype(jnp.bfloat16)
    dlog = exact_dot(ones, dcum)
    rate = heads_ref[1:2, :]
    ddt = jnp.where(dt > 0.0, sums / dt, 0.0) + dlog * rate
    ddt = ddt / (1.0 + jnp.exp(-raw))
    dxt_ref[:, CONVW:] = ddt.astype(jnp.bfloat16)
    ghead_ref[0:1, :] += jnp.sum(ddt, 0, keepdims=True)
    ghead_ref[1:2, :] += jnp.sum(dlog * dt, 0, keepdims=True) * rate

    def conv_chunk(chunk, carry):
        at = pl.ds(pl.multiple_of(chunk * PAIR, PAIR), PAIR)
        sums = [jnp.zeros((8, PAIR), jnp.float32)] * (KCONV + 1)
        for row in range(0, GROUP, STRIP):
            given = xt_ref[row : row + STRIP, at].astype(jnp.float32)
            total = None
            for tap in range(KCONV):
                start = KCONV - 1 - tap + row
                moved = dext_ref[chunk, start : start + STRIP, :]
                term = taps_ref[tap : tap + 1, at] * moved
                total = term if total is None else total + term
                sums[tap] = sums[tap] + jnp.sum((given * moved).reshape(-1, 8, PAIR), 0)
                if tap == KCONV - 1:
                    sums[KCONV] = sums[KCONV] + jnp.sum(moved.reshape(-1, 8, PAIR), 0)
            dxt_ref[row : row + STRIP, at] = total.astype(jnp.bfloat16)
        for k in range(KCONV + 1):
            gconv_ref[k : k + 1, at] += jnp.sum(sums[k], 0, keepdims=True)
        return carry

    lax.fori_loop(0, CONVW // PAIR, conv_chunk, 0)
    dext_ref[:, GROUP:, :] = dext_ref[:, 0:8, :]


def tall_block(width, count=None):
    if count is None:
        return pl.BlockSpec((GROUP, width), lambda i: (i, 0))
    return pl.BlockSpec((GROUP, width), lambda i: (count - 1 - i, 0))


def fixed_block(shape):
    return pl.BlockSpec(shape, lambda i: (0, 0))


def kernel_options():
    return pltpu.CompilerParams(
        dimension_semantics=("arbitrary",), vmem_limit_bytes=48 * 1024 * 1024
    )


def shape_of(rows, width, kind):
    return jax.ShapeDtypeStruct((rows, width), kind)


def run_scan(xt, taps, heads, lanes):
    length = xt.shape[0]
    count = length // GROUP
    f32, b16 = jnp.float32, jnp.bfloat16
    return pl.pallas_call(
        scan_kernel,
        grid=(count,),
        in_specs=[
            tall_block(XTAIL), fixed_block(taps.shape), fixed_block(heads.shape), fixed_block(lanes.shape),
        ],
        out_specs=[
            tall_block(CONVW), tall_block(CONVW), pl.BlockSpec((STATE, INNER), lambda i: (i, 0)),
            tall_block(INNER),
        ],
        out_shape=[
            shape_of(length, CONVW, b16), shape_of(length, CONVW, f32),
            shape_of(count * STATE, INNER, f32), shape_of(length, INNER, f32),
        ],
        scratch_shapes=[
            pltpu.VMEM((STATE, INNER), f32), pltpu.VMEM((CONVW // PAIR, GROUP + 8, PAIR), f32),
            pltpu.VMEM((GROUP, GROUP), f32),
        ],
        compiler_params=kernel_options(),
        cost_estimate=pl.CostEstimate(flops=25 * 10**9, bytes_accessed=30 * 10**6, transcendentals=10**7),
        name="scan_forward",
    )(xt, taps, heads, lanes)


def run_gate(z, ssd, mixed, x, go, wout, lanes, seg):
    length = x.shape[0]
    f32, b16 = jnp.float32, jnp.bfloat16
    return pl.pallas_call(
        gate_kernel,
        grid=(length // GROUP,),
        in_specs=[
            tall_block(INNER), tall_block(INNER), tall_block(INNER), tall_block(WIDE), tall_block(WIDE),
            fixed_block(wout.shape), fixed_block(lanes.shape), fixed_block(seg.shape),
        ],
        out_specs=[
            tall_block(WIDE), tall_block(INNER), tall_block(INNER), tall_block(INNER), tall_block(PAIR),
            fixed_block((8, INNER)),
        ],
        out_shape=[
            shape_of(length, WIDE, b16), shape_of(length, INNER, b16), shape_of(length, INNER, b16),
            shape_of(length, INNER, b16), shape_of(length, PAIR, f32), shape_of(8, INNER, f32),
        ],
        scratch_shapes=[
            pltpu.VMEM((GROUP, INNER), f32), pltpu.VMEM((GROUP, INNER), b16),
            pltpu.VMEM((GROUP, INNER), b16),
        ],
        compiler_params=kernel_options(),
        cost_estimate=pl.CostEstimate(flops=20 * 10**9, bytes_accessed=30 * 10**6, transcendentals=10**7),
        name="gate_both_ways",
    )(z, ssd, mixed, x, go, wout, lanes, seg)


def run_backward(xt, mixed, slope, dssd, states, delta, taps, heads, lanes, seg):
    length = xt.shape[0]
    count = length // GROUP
    f32, b16 = jnp.float32, jnp.bfloat16
    return pl.pallas_call(
        backward_kernel,
        grid=(count,),
        in_specs=[
            tall_block(XTAIL, count), tall_block(CONVW, count), tall_block(CONVW, count),
            tall_block(INNER, count), pl.BlockSpec((STATE, INNER), lambda i: (count - 1 - i, 0)),
            tall_block(PAIR, count), fixed_block(taps.shape), fixed_block(heads.shape),
            fixed_block(lanes.shape), fixed_block(seg.shape),
        ],
        out_specs=[
            tall_block(XTAIL, count), fixed_block((8, CONVW)), fixed_block((8, PAIR)),
            fixed_block((8, INNER)),
        ],
        out_shape=[
            shape_of(length, XTAIL, b16), shape_of(8, CONVW, f32), shape_of(8, PAIR, f32),
            shape_of(8, INNER, f32),
        ],
        scratch_shapes=[
            pltpu.VMEM((STATE, INNER), f32), pltpu.VMEM((CONVW // PAIR, GROUP + 8, PAIR), f32),
            pltpu.VMEM((GROUP, GROUP), f32), pltpu.VMEM((GROUP, GROUP), f32),
            pltpu.VMEM((GROUP, INNER), b16), pltpu.VMEM((GROUP, INNER), b16),
            pltpu.VMEM((GROUP, INNER), b16), pltpu.VMEM((GROUP, INNER), b16),
            pltpu.VMEM((8, INNER), f32), pltpu.VMEM((STATE, INNER), b16),
        ],
        compiler_params=kernel_options(),
        cost_estimate=pl.CostEstimate(flops=30 * 10**9, bytes_accessed=30 * 10**6, transcendentals=10**7),
        name="scan_backward",
    )(xt, mixed, slope, dssd, states, delta, taps, heads, lanes, seg)


def head_segments():
    rows = lax.broadcasted_iota(jnp.int32, (INNER, PAIR), 0) // HEADDIM
    cols = lax.broadcasted_iota(jnp.int32, (INNER, PAIR), 1)
    return (rows == cols).astype(jnp.bfloat16)


def head_tables(dt_bias, rate, skip):
    pad = lambda v: jnp.pad(v.astype(jnp.float32), (0, PAIR - HEADS))
    zero = jnp.zeros((PAIR,), jnp.float32)
    heads = jnp.stack([pad(dt_bias), pad(rate)] + [zero] * 6)
    return (heads, jnp.repeat(skip, HEADDIM))


def input_norm(xb, gain_in):
    xf = xb.astype(jnp.float32)
    r_in = lax.rsqrt(jnp.mean(xf * xf, -1, keepdims=True) + EPS)
    return (xf, r_in, (xf * r_in * gain_in.astype(jnp.float32)).astype(jnp.bfloat16))


def input_grad(xf, r_in, gain_in, dnormed, cot):
    scaled = gain_in.astype(jnp.float32) * dnormed
    return (
        r_in * scaled
        - xf * r_in**3 * jnp.mean(scaled * xf, -1, keepdims=True)
        + cot.astype(jnp.float32)
    ).astype(jnp.bfloat16)


def low_dot(left, right):
    return jnp.dot(left, right, preferred_element_type=jnp.float32).astype(jnp.bfloat16)


SPARE = 1816


def grid_place():
    dp = lax.axis_index("dp")
    return (dp // 4, lax.rem(dp // 2, 2), lax.rem(dp, 2), lax.axis_index("seq"))


def grid_moves(step):
    high = lax.axis_size("dp") // 4
    pairs = []
    for z in range(high):
        for y in range(2):
            for c in range(2):
                for x in range(2):
                    to = ((z + step[0]) % high, y ^ step[1], c ^ step[2], x ^ step[3])
                    pairs.append((((z * 2 + y) * 2 + c) * 2 + x, ((to[0] * 2 + to[1]) * 2 + to[2]) * 2 + to[3]))
    return pairs


def grid_send(array, step):
    return lax.ppermute(array, ("dp", "seq"), grid_moves(step))


def pick(array, axes, places):
    start = [0] * array.ndim
    size = list(array.shape)
    for axis, place in zip(axes, places):
        start[axis] = place
        size[axis] = 1
    out = lax.dynamic_slice(array, start, size)
    return out.reshape([n for axis, n in enumerate(array.shape) if axis not in axes])


def add_up(parts):
    total = parts[0].astype(jnp.float32)
    for part in parts[1:]:
        total = total + part.astype(jnp.float32)
    return total


FLIPS = ((0, 1), (1, 0), (1, 1))


def reduce_core(grads, kind=jnp.bfloat16):
    high = lax.axis_size("dp") // 4
    _, _, c, _ = grid_place()
    grads = [grad.reshape((high, 2, 2, 2) + grad.shape[1:]) for grad in grads]
    sent = jnp.concatenate([pick(grad, (2,), (1 - c,)) for grad in grads], -1)
    kept = jnp.concatenate([pick(grad, (2,), (c,)) for grad in grads], -1)
    return add_up([kept, grid_send(sent, (0, 0, 1, 0))]).astype(kind)


def plane_parts(parts):
    _, y, _, x = grid_place()
    found = [pick(parts, (1, 2), (y, x))]
    for fy, fx in FLIPS:
        piece = pick(parts, (1, 2), (y ^ fy, x ^ fx))
        found.append(grid_send(piece, (0, fy, 0, fx)))
    return found


def line_parts(parts):
    high = lax.axis_size("dp") // 4
    z, _, _, _ = grid_place()
    found = [pick(parts, (0,), (z,))]
    for hop in range(1, high):
        piece = pick(parts, (0,), (lax.rem(z + hop, high),))
        found.append(grid_send(piece, (hop, 0, 0, 0)))
    return found


def gather_line(own):
    high = lax.axis_size("dp") // 4
    return jnp.stack([own] + [grid_send(own, (hop, 0, 0, 0)) for hop in range(1, high)])


def gather_plane(tall):
    return [tall] + [grid_send(tall, (0, fy, 0, fx)) for fy, fx in FLIPS]


def join_kernel(cuts, place_ref, *refs):
    pieces, outs = refs[:8], refs[8:]
    high = pieces[0].shape[0]
    for slot, piece in enumerate(pieces):
        fy, fx = (((0, 0),) + FLIPS)[slot // 2]
        y, c, x = place_ref[1] ^ fy, place_ref[2] ^ (slot % 2), place_ref[3] ^ fx
        for hop in range(high):
            z = lax.rem(place_ref[0] + high - hop, high)
            for out, cut in zip(outs, cuts):
                for j, (start, size) in enumerate(cut):
                    out[z, y, c, x, j] = piece[hop, :, start : start + size]


def core_pieces(pieces):
    both = []
    for piece in pieces:
        both += [piece, grid_send(piece, (0, 0, 1, 0))]
    return both


def place_now():
    return jnp.stack([jnp.asarray(p, jnp.int32) for p in grid_place()])


def join_options():
    return pltpu.CompilerParams(vmem_limit_bytes=24 * 1024 * 1024)


def gather_core(pieces, cuts):
    high, rows, _ = pieces[0].shape
    shapes = [(high, 2, 2, 2, len(cut), rows, cut[0][1]) for cut in cuts]
    outs = pl.pallas_call(
        functools.partial(join_kernel, cuts),
        in_specs=[pl.BlockSpec(memory_space=pltpu.SMEM)] + [pl.BlockSpec(memory_space=pltpu.VMEM)] * 8,
        out_specs=[pl.BlockSpec(memory_space=pltpu.VMEM)] * len(cuts),
        out_shape=[jax.ShapeDtypeStruct(shape, pieces[0].dtype) for shape in shapes],
        compiler_params=join_options(),
        name="join_rows",
    )(place_now(), *core_pieces(pieces))
    return [full.reshape((-1, full.shape[-1])) for full in outs]


def join_first_kernel(cuts, place_ref, *refs):
    spots, masks, skip_ref = refs[8:11], refs[11:14], refs[14]
    full_ref, taps_ref, lanes_ref, gain_ref, held_ref = refs[15:]
    join_kernel(cuts, place_ref, *refs[:8], full_ref)
    high = refs[0].shape[0]
    for slot, piece in enumerate(refs[:8]):
        fy, fx = (((0, 0),) + FLIPS)[slot // 2]
        y, c, x = place_ref[1] ^ fy, place_ref[2] ^ (slot % 2), place_ref[3] ^ fx
        for hop in range(high):
            z = lax.rem(place_ref[0] + high - hop, high)
            owner = ((z * 2 + y) * 2 + c) * 2 + x
            block = piece[hop, 0:16, XTAIL - PAIR : XTAIL].astype(jnp.float32)
            held_ref[owner] = block[0:8]

    def line(row, which):
        spread = jnp.dot(
            held_ref[:, row, :].astype(jnp.bfloat16), spots[which][...], preferred_element_type=jnp.float32
        )
        return jnp.sum(spread * masks[which][...], 0, keepdims=True)

    taps_ref[...] = jnp.zeros_like(taps_ref)
    for row in range(KCONV + 1):
        taps_ref[row : row + 1, :] = line(row, 0)
    lanes_ref[...] = jnp.zeros_like(lanes_ref)
    lanes_ref[0:1, :] = line(KCONV + 1, 1)
    lanes_ref[1:2, :] = skip_ref[0:1, :]
    gain_ref[...] = jnp.zeros_like(gain_ref)
    gain_ref[0:1, :] = line(KCONV + 2, 2)


def spread_tables(width, devices):
    size = width // devices
    lane = lax.broadcasted_iota(jnp.int32, (PAIR, width), 1)
    spot = lax.broadcasted_iota(jnp.int32, (PAIR, width), 0) - (SPARE - XTAIL + PAIR) == lane % size
    owner = lax.broadcasted_iota(jnp.int32, (devices, width), 0)
    mask = owner == lax.broadcasted_iota(jnp.int32, (devices, width), 1) // size
    return (spot.astype(jnp.bfloat16), mask.astype(jnp.float32))


def gather_first(pieces, skip_lanes):
    high, rows, width = pieces[0].shape
    devices = 8 * high
    tables = [spread_tables(w, devices) for w in (CONVW, INNER, WIDE)]
    f32 = jnp.float32
    full, taps, lanes, gain = pl.pallas_call(
        functools.partial(join_first_kernel, (((0, width),),)),
        in_specs=[pl.BlockSpec(memory_space=pltpu.SMEM)] + [pl.BlockSpec(memory_space=pltpu.VMEM)] * 15,
        out_specs=[pl.BlockSpec(memory_space=pltpu.VMEM)] * 4,
        out_shape=[
            jax.ShapeDtypeStruct((high, 2, 2, 2, 1, rows, width), pieces[0].dtype),
            shape_of(8, CONVW, f32), shape_of(8, INNER, f32), shape_of(8, WIDE, f32),
        ],
        scratch_shapes=[pltpu.VMEM((devices, 8, PAIR), f32)],
        compiler_params=join_options(),
        name="join_first",
    )(
        place_now(), *core_pieces(pieces), *[t[0] for t in tables], *[t[1] for t in tables],
        jnp.broadcast_to(skip_lanes[None], (8, INNER)),
    )
    return (full.reshape(-1, width), taps, lanes, gain[0])


def after(value, *others):
    return lax.optimization_barrier((value,) + others)[0]


def swap_pick(parts):
    return lax.dynamic_index_in_dim(parts, 1 - lax.axis_index("seq"), 0, False)


def swap_send(parts):
    return grid_send(swap_pick(parts), (0, 0, 0, 1))


def swap_join(parts, got):
    place = lax.axis_index("seq")
    own = lax.dynamic_index_in_dim(parts, place, 0, False)
    return jnp.concatenate([jnp.where(place == 0, own, got), jnp.where(place == 0, got, own)], 0)


def swap_halves(parts, *guards):
    return swap_join(parts, after(swap_send(parts), *guards))


def pack_small(gain, taps, bias, gate, heads):
    lines = [taps, bias[None], gate[None], gain[None], heads[None]]
    lines = [jnp.pad(line, ((0, 0), (0, PAIR - line.shape[1]))) for line in lines]
    return jnp.concatenate(lines, 0)


def unpack_small(block, sizes):
    taps = block[..., :KCONV, : sizes[0]]
    return [taps] + [block[..., KCONV + k, :size] for k, size in enumerate(sizes[1:])]


def fast_shards(
    x_in, grad_out, norm_gain, in_weight, conv_weight, conv_bias, gate_gain, out_weight, dt_bias, a_log, skip
):
    rate = -jnp.exp(a_log)
    devices = lax.axis_size(("dp", "seq"))
    micro, _, length, _ = x_in.shape
    rows = in_weight.shape[0]
    sizes = (conv_weight.shape[1], conv_bias.size, gate_gain.size, norm_gain.size)
    place = lambda a, row, column: jnp.pad(
        a, ((row, rows - row - a.shape[0]), (column, XTAIL - column - a.shape[1]))
    )
    first = (
        place(in_weight[:, INNER:], 0, 0)
        + place(conv_weight, 0, SPARE)
        + place(conv_bias[None], KCONV, SPARE)
        + place(gate_gain[None], KCONV + 1, SPARE)
        + place(norm_gain[None], KCONV + 2, SPARE)
    )
    second = jnp.concatenate([in_weight[:, :INNER], out_weight[:rows], out_weight[rows:]], 1)

    line_first = gather_line(first)
    x_got = swap_send(x_in[:, 0])
    xb = swap_join(x_in[:, 0], x_got)
    plane_first = gather_plane(line_first)
    line_second = gather_line(after(second, plane_first[2]))
    heads, skip_lanes = head_tables(dt_bias, rate, skip)
    seg = head_segments()
    seg, skip_lanes = lax.optimization_barrier((seg, skip_lanes))
    w_xt, taps_bias, lanes, gain_in = gather_first(plane_first, skip_lanes)
    line_second = after(line_second, *plane_first)
    second_y = grid_send(line_second, (0, 1, 0, 0))
    second_x = grid_send(line_second, (0, 0, 0, 1))
    plane_second = [line_second, second_x, second_y, grid_send(second_x, (0, 1, 0, 0))]
    xf, r_in, normed = input_norm(xb, gain_in)
    normed = after(normed)
    xt = after(low_dot(normed, w_xt), second_x)
    mixed, slope, states, ssd = run_scan(xt, taps_bias, heads, lanes)
    cot = swap_halves(after(grad_out[:, 0], second_x), ssd)

    plane_second = [after(piece, ssd) for piece in plane_second]
    w_z, w_out = gather_core(
        plane_second, (((0, INNER),), ((INNER, WIDE), (INNER + WIDE, WIDE)))
    )
    z = low_dot(normed, w_z)
    y, gnorm, dz, dssd, delta, ggain = run_gate(z, ssd, mixed, xb, cot, w_out, lanes, seg)
    grad_wout = tdot(gnorm, cot).astype(jnp.bfloat16).reshape(devices, 2, rows, WIDE)
    grad_wz = tdot(normed, dz).astype(jnp.bfloat16)
    early = [grad_wz] + [grad_wout[:, k] for k in range(2)]
    early = reduce_core([part.reshape(devices, rows, -1) for part in early])
    dssd = after(dssd, early)
    y_got = swap_send(y.reshape(micro, length, WIDE))
    early = plane_parts(early)
    dxt, gconv, ghead, gskip = run_backward(
        xt, mixed, slope, dssd, states, delta, taps_bias, heads, lanes, seg
    )
    dxt, y_got = lax.optimization_barrier((dxt, y_got) + tuple(early))[:2]
    grad_wxt = tdot(normed, dxt).astype(jnp.bfloat16)
    late = reduce_core([grad_wxt.reshape(devices, rows, -1)])
    head_terms = jnp.concatenate(
        [ghead[0, :HEADS], ghead[1, :HEADS], jnp.sum(gskip[0].reshape(HEADS, HEADDIM), -1)]
    )
    tiny = jax.vmap(pack_small)(
        jnp.zeros((devices, 8), jnp.float32),
        gconv[:KCONV].reshape(KCONV, devices, -1).transpose(1, 0, 2),
        gconv[KCONV].reshape(devices, -1),
        jnp.sum(ggain, 0).reshape(devices, -1),
        jnp.broadcast_to(head_terms, (devices, 3 * HEADS)),
    )[:, :, : XTAIL - SPARE]
    tiny = reduce_core([tiny], jnp.float32)
    tiny = jnp.pad(tiny, ((0, 0),) * 3 + ((0, rows - KCONV - 4), (SPARE, 0)))
    late = (late.astype(jnp.float32) + tiny).astype(jnp.bfloat16)
    dn_z = ndot(after(dz, late), w_z)
    late = plane_parts(late)
    early = lax.optimization_barrier(tuple(early) + (late[2],))[:-1]
    dnormed = dn_z + ndot(after(dxt, late[2]), w_xt)
    dx = input_grad(xf, r_in, gain_in, dnormed, cot)
    dx_got = swap_send(after(dx.reshape(micro, length, WIDE), *late))
    early = add_up(line_parts(add_up(early).astype(jnp.bfloat16)))
    late = tuple(line_parts(add_up(late).astype(jnp.bfloat16)))
    y_got = after(y_got, late[1])
    y_out = swap_join(y.reshape(micro, length, WIDE), y_got).reshape(x_in.shape)
    late = add_up(lax.optimization_barrier(late + (dx_got,))[:-1])
    dx_in = swap_join(dx.reshape(micro, length, WIDE), dx_got).reshape(x_in.shape)
    own_in = jnp.concatenate([early[:, :INNER], late[:, :SPARE]], 1)
    owned = early[:, INNER:]
    own_out = jnp.concatenate([owned[:, :WIDE], owned[:, WIDE:]], 0)
    own = late[:, SPARE:]
    found = unpack_small(own, sizes)
    heads_sum = own[KCONV + 3]
    weighted = jnp.sum(own_in * in_weight.astype(jnp.float32), -1)
    grad_gain = weighted / norm_gain.astype(jnp.float32)
    return (
        y_out, dx_in, grad_gain, own_in, found[0], found[1], found[2], own_out,
        heads_sum[:HEADS], heads_sum[HEADS : 2 * HEADS], heads_sum[2 * HEADS : 3 * HEADS],
    )


def shards(x_in, *rest):
    dp, seq = lax.axis_size("dp"), lax.axis_size("seq")
    if x_in.shape[0] == seq == 2 and dp % 4 == 0 and rest[1].size * dp * seq == WIDE:
        return fast_shards(x_in, *rest)
    return shards_general(x_in, *rest)


def shards_general(
    x_in,
    grad_out,
    norm_gain,
    in_weight,
    conv_weight,
    conv_bias,
    gate_gain,
    out_weight,
    dt_bias,
    a_log,
    skip,
):
    micro = x_in.shape[0]
    rate = -jnp.exp(a_log)
    devices = lax.axis_size(("dp", "seq"))
    results = []
    saves = []
    for index in range(micro):
        wts = (
            lax.all_gather(norm_gain, ("dp", "seq"), axis=0, tiled=True),
            lax.all_gather(in_weight, ("dp", "seq"), axis=0, tiled=True),
            lax.all_gather(conv_weight, ("dp", "seq"), axis=1, tiled=True),
            lax.all_gather(conv_bias, ("dp", "seq"), axis=0, tiled=True),
            lax.all_gather(gate_gain, ("dp", "seq"), axis=0, tiled=True),
            lax.all_gather(out_weight, ("dp", "seq"), axis=0, tiled=True),
        )
        result, saved = forward(x_in[index, 0], wts, dt_bias, rate, skip)
        results.append(result)
        saves.append(saved)
    dx_list = [None] * micro
    summed = None
    for index in reversed(range(micro)):
        wts = (
            lax.all_gather(norm_gain, ("dp", "seq"), axis=0, tiled=True),
            lax.all_gather(in_weight, ("dp", "seq"), axis=0, tiled=True),
            lax.all_gather(conv_weight, ("dp", "seq"), axis=1, tiled=True),
            lax.all_gather(conv_bias, ("dp", "seq"), axis=0, tiled=True),
            lax.all_gather(gate_gain, ("dp", "seq"), axis=0, tiled=True),
            lax.all_gather(out_weight, ("dp", "seq"), axis=0, tiled=True),
        )
        dx_part, terms = backward(saves[index], grad_out[index, 0], wts, dt_bias, rate, skip)
        dx_list[index] = dx_part
        summed = terms if summed is None else jax.tree.map(lambda a, b: a + b, summed, terms)
    spread = summed[:6] + (jnp.broadcast_to(summed[6], (devices, 3 * HEADS)),)
    summed = (
        lax.psum_scatter(spread[0], ("dp", "seq"), scatter_dimension=0, tiled=True),
        lax.psum_scatter(spread[1], ("dp", "seq"), scatter_dimension=0, tiled=True),
        lax.psum_scatter(spread[2], ("dp", "seq"), scatter_dimension=1, tiled=True),
        lax.psum_scatter(spread[3], ("dp", "seq"), scatter_dimension=0, tiled=True),
        lax.psum_scatter(spread[4], ("dp", "seq"), scatter_dimension=0, tiled=True),
        lax.psum_scatter(spread[5], ("dp", "seq"), scatter_dimension=0, tiled=True),
        lax.psum_scatter(spread[6], ("dp", "seq"), scatter_dimension=0, tiled=True),
    )
    heads_sum = summed[6].reshape(3, HEADS)
    y_out = jnp.stack(results)[:, None]
    dx_in = jnp.stack(dx_list)[:, None]
    return (
        y_out,
        dx_in,
        summed[0],
        summed[1],
        summed[2],
        summed[3],
        summed[4],
        summed[5],
        heads_sum[0],
        heads_sum[1],
        heads_sum[2],
    )


def solution(mesh):
    return jax.shard_map(
        shards,
        mesh=mesh,
        in_specs=(
            P(None, "dp", "seq", None),
            P(None, "dp", "seq", None),
            P(("dp", "seq")),
            P(("dp", "seq"), None),
            P(None, ("dp", "seq")),
            P(("dp", "seq")),
            P(("dp", "seq")),
            P(("dp", "seq"), None),
            P(),
            P(),
            P(),
        ),
        out_specs=(
            P(None, "dp", "seq", None),
            P(None, "dp", "seq", None),
            P(("dp", "seq")),
            P(("dp", "seq"), None),
            P(None, ("dp", "seq")),
            P(("dp", "seq")),
            P(("dp", "seq")),
            P(("dp", "seq"), None),
            P(),
            P(),
            P(),
        ),
        check_vma=False,
    )
```
